32 devices in a mesh: dp: 16 (over z, y, x), mp: 2 (over core).
Axes of the slice: x: 2, y: 2, z: 4, core: 2. Of those that a mesh axis runs over, the one named last changes fastest.
Arguments:
- tokens: bfloat16 [32, 1024, 512], P('dp'), may hold values from -6 to 6
- segment_ids: int32 [32, 1024], P('dp'), may hold values from 0 to 7, never falling along the last dimension, each value on 1 to 256 neighbouring positions
- row_fill: int32 [32], P('dp'), may hold values from 256 to 1024
- query_weight: bfloat16 [512, 512], P(None, 'mp'), may hold values from -0.25 to 0.25
- query_bias: float32 [512], P('mp'), may hold values from -3 to 3
- key_weight: bfloat16 [512, 512], P(None, 'mp'), may hold values from -0.25 to 0.25
- value_weight: bfloat16 [512, 512], P(None, 'mp'), may hold values from -0.25 to 0.25
- value_bias: float32 [512], P('mp'), may hold values from -3 to 3
- out_weight: bfloat16 [512, 512], P('mp'), may hold values from -1 to 1
- out_bias: float32 [512], replicated, may hold values from 0.1 to 0.6
- attention_gate: float32 [], replicated, may hold values from 0.5 to 1.5
- inner_weight: bfloat16 [512, 2048], P(None, 'mp'), may hold values from -0.25 to 0.25
- inner_bias: float32 [2048], P('mp'), may hold values from -3 to 3
- outer_weight: bfloat16 [2048, 512], P('mp'), may hold values from -0.1875 to 0.1875
- outer_bias: float32 [512], replicated, may hold values from 0.1 to 0.6
- feed_gate: float32 [], replicated, may hold values from 0.5 to 1.5
- cotangent: bfloat16 [32, 1024, 512], P('dp'), may hold values from -3.5 to 4.5
Outputs:
- output: bfloat16 [32, 1024, 512], P('dp')
- grad_tokens: float32 [32, 1024, 512], P('dp')
- grad_query_weight: float32 [512, 512], P(None, 'mp')
- grad_query_bias: float32 [512], P('mp')
- grad_key_weight: float32 [512, 512], P(None, 'mp')
- grad_value_weight: float32 [512, 512], P(None, 'mp')
- grad_value_bias: float32 [512], P('mp')
- grad_out_weight: float32 [512, 512], P('mp')
- grad_out_bias: float32 [512], replicated
- grad_attention_gate: float32 [], replicated
- grad_inner_weight: float32 [512, 2048], P(None, 'mp')
- grad_inner_bias: float32 [2048], P('mp')
- grad_outer_weight: float32 [2048, 512], P('mp')
- grad_outer_bias: float32 [512], replicated
- grad_feed_gate: float32 [], replicated
The draws below stay inside these ranges and needn't reach their ends.
All inputs are finite; a program needn't handle non-finite values.
Results may differ from the reference program's by a relative error of at most 0.013.
Values sent between devices are 32-bit elements; how exact they have to be, the bound alone decides.
No kernel may reach another device: no remote copies, remote signals or barrier semaphores. Data moves between devices by JAX's collectives and lax.ppermute only.
A program may use at most 128 MiB of HBM per device.

```python
import math
import jax
import jax.numpy as jnp
import numpy as np
from jax import lax

D = 512
FF = 2048
HEAD_DIM = 64
LEN = 1024
SEQS = 32


def draw_cotangent(key, part):
    key = jax.random.fold_in(key, 11)
    noise = jax.random.normal(key, (SEQS, LEN, D), jnp.float32)
    return (0.5 + jnp.clip(noise, -4.0, 4.0)).astype(jnp.bfloat16)


def with_ends(values, own_key, least, top_value):
    extent = values.shape
    index_at = [jax.random.randint(jax.random.fold_in(own_key, axis), (), 0, extent[axis]) for axis in range(len(extent))]
    values = values.at[tuple(index_at)].set(least)
    longest = extent.index(max(extent))
    index_at[longest] = (index_at[longest] + 1) % extent[longest]
    return values.at[tuple(index_at)].set(top_value)


def shard_levels(rng, extent, split, low, largest):
    def one(axis_at, shards_of):
        steps = jax.random.uniform(jax.random.fold_in(jax.random.fold_in(rng, 6), axis_at), (shards_of,), jnp.float32, low / len(split), largest / len(split))
        return jnp.repeat(jnp.exp(steps), extent[axis_at] // shards_of).reshape((-1,) + (1,) * (len(extent) - axis_at - 1))

    loudness = one(*split[0])
    for cut in split[1:]:
        loudness = loudness * one(*cut)
    return loudness


def split_up(amount, total, limit, skew):
    loads = [(1 << 20) // math.isqrt(grade ** skew) + 1 for grade in range(2, amount + 1)]
    rest, counts = total - limit - (amount - 1), [1] * (amount - 1)
    while rest > 0:
        movable = [i for i in range(amount - 1) if counts[i] < limit]
        whole, left = sum([loads[i] for i in movable]), rest
        for i in movable:
            addition = min(limit - counts[i], max(1, left * loads[i] // whole), rest)
            counts[i] = counts[i] + addition
            rest = rest - addition
    return np.array([limit] + counts)


def uneven(rng, number_of, total, reach, lean):
    if number_of == 2:
        one = jax.random.randint(rng, (), max(1, total - reach), min(reach, total - 1) + 1)
        return jnp.stack([one, total - one])
    lengths = jnp.asarray(split_up(number_of, total, reach, lean), jnp.int32)
    pairs = (number_of - 1) // 2
    donor, taker = lengths[1:1 + 2 * pairs:2], lengths[2:2 + 2 * pairs:2]
    room = jnp.minimum(donor - 1, reach - taker)
    shifted = jax.random.randint(jax.random.fold_in(rng, 1), (pairs,), 0, 1 << 20) % (room + 1)
    lengths = lengths.at[1:1 + 2 * pairs:2].set(donor - shifted).at[2:2 + 2 * pairs:2].set(taker + shifted)
    return lengths[jax.random.permutation(jax.random.fold_in(rng, 2), number_of)]


def centred(rng, dims, scale, limit, shards=(), kind=jnp.bfloat16):
    values = scale * jax.random.normal(rng, dims, jnp.float32)
    if shards:
        values = values * shard_levels(rng, dims, shards, -0.22, 0.18)
    return jnp.clip(values, -limit, limit).astype(kind)


def setup_inputs(seed: int = 0) -> dict:
    key_of = jax.random.split(jax.random.key(seed), 18)
    tokens = centred(key_of[0], (SEQS, LEN, D), 1.0, 6.0, ((0, 16),))
    segment_ids = jax.vmap(lambda own: jnp.searchsorted(jnp.cumsum(uneven(own, 8, LEN, LEN // 4, 1)), jnp.arange(LEN), side="right"))(jax.random.split(key_of[1], SEQS)).reshape((SEQS, LEN)).astype(jnp.int32)
    row_fill = with_ends(jax.random.randint(key_of[2], (SEQS,), LEN // 4, LEN + 1), jax.random.fold_in(key_of[2], 1), LEN // 4, LEN).astype(jnp.int32)
    query_weight = centred(key_of[3], (D, D), D ** -0.5, 0.25, ((1, 2),))
    query_bias = centred(key_of[4], (D,), 0.5, 3.0, ((0, 2),), jnp.float32)
    key_weight = centred(key_of[5], (D, D), D ** -0.5, 0.25, ((1, 2),))
    value_weight = centred(key_of[6], (D, D), D ** -0.5, 0.25, ((1, 2),))
    value_bias = centred(key_of[7], (D,), 0.5, 3.0, ((0, 2),), jnp.float32)
    out_weight = centred(key_of[8], (D, D), (D // 16) ** -0.5, 1.0, ((0, 2),))
    out_bias = jnp.clip(jax.random.uniform(key_of[9], (D,), jnp.float32, 0.1, 0.6), 0.1, 0.6)
    attention_gate = jnp.clip(jax.random.uniform(key_of[10], (), jnp.float32, 0.5, 1.5), 0.5, 1.5)
    inner_weight = centred(key_of[11], (D, FF), D ** -0.5, 0.25, ((1, 2),))
    inner_bias = centred(key_of[12], (FF,), 0.5, 3.0, ((0, 2),), jnp.float32)
    outer_weight = centred(key_of[13], (FF, D), (FF // 2) ** -0.5, 0.1875, ((0, 2),))
    outer_bias = jnp.clip(jax.random.uniform(key_of[14], (D,), jnp.float32, 0.1, 0.6), 0.1, 0.6)
    feed_gate = jnp.clip(jax.random.uniform(key_of[15], (), jnp.float32, 0.5, 1.5), 0.5, 1.5)
    cotangent = draw_cotangent(jax.random.fold_in(key_of[17], 71), 0)
    return dict(tokens=tokens, segment_ids=segment_ids, row_fill=row_fill, query_weight=query_weight, query_bias=query_bias, key_weight=key_weight, value_weight=value_weight, value_bias=value_bias, out_weight=out_weight, out_bias=out_bias, attention_gate=attention_gate, inner_weight=inner_weight, inner_bias=inner_bias, outer_weight=outer_weight, outer_bias=outer_bias, feed_gate=feed_gate, cotangent=cotangent)


highest = lax.Precision.HIGHEST

@jax.custom_vjp
def low(v):
    return lax.optimization_barrier(v.astype(jnp.bfloat16)).astype(jnp.float32)

@jax.custom_vjp
def low_back(v):
    return v

def low_keep(v):
    return (low(v), None)

def low_pass(kept, grad):
    return (grad,)

def back_keep(v):
    return (v, None)

def back_low(kept, grad):
    return (low(grad),)
low.defvjp(low_keep, low_pass)
low_back.defvjp(back_keep, back_low)

def rounded(value):
    return low_back(low(value))

def dense(left, right):
    return jnp.dot(left, right, precision=highest)

def encoder(params, tokens, segment, fill_count):
    query_weight, query_bias, key_weight, value_weight, value_bias, out_weight, out_bias, attention_gate, inner_weight, inner_bias, outer_weight, outer_bias, feed_gate = params
    length = tokens.shape[0]
    head_count = query_weight.shape[1] // HEAD_DIM
    places = jnp.arange(length, dtype=jnp.int32)
    same_pair = (segment[:, None] == segment[None, :]) & (places[None, :] < fill_count)
    allowed = same_pair | (places[:, None] == places[None, :])
    valid_rows = (places < fill_count).astype(jnp.float32)[:, None]
    queries = rounded(dense(tokens, query_weight) + query_bias).reshape(length, head_count, HEAD_DIM)
    key_rows = rounded(dense(tokens, key_weight)).reshape(length, head_count, HEAD_DIM)
    values = rounded(dense(tokens, value_weight) + value_bias).reshape(length, head_count, HEAD_DIM)
    scores = low_back(jnp.einsum('qhd,khd->hqk', queries, key_rows, precision=highest) * 0.125)
    scores = jnp.where(allowed[None], scores, -1e+30)
    weights = low(jax.nn.softmax(scores, axis=-1))
    attended = jnp.einsum('hqk,khd->qhd', weights, values, precision=highest)
    attended = rounded(attended.reshape(length, head_count * HEAD_DIM) * valid_rows)
    branch = low_back(dense(attended, out_weight) + out_bias)
    middle = tokens + attention_gate * branch
    pre_act = low_back(dense(low(middle), inner_weight) + inner_bias)
    hidden = low(jax.nn.gelu(pre_act, approximate=True))
    ffn_out = low_back(dense(hidden, outer_weight) + outer_bias)
    return middle + feed_gate * ffn_out

def reference(tokens, segment_ids, row_fill, query_weight, query_bias, key_weight, value_weight, value_bias, out_weight, out_bias, attention_gate, inner_weight, inner_bias, outer_weight, outer_bias, feed_gate, cotangent):
    params = tuple((array.astype(jnp.float32) for array in (query_weight, query_bias, key_weight, value_weight, value_bias, out_weight, out_bias, attention_gate, inner_weight, inner_bias, outer_weight, outer_bias, feed_gate)))

    def one_row(totals, row_item):
        row_tokens, segment, fill_count, row_grad = row_item

        def forward(weights_all, inputs):
            return encoder(weights_all, inputs, segment, fill_count)
        result, pullback = jax.vjp(forward, params, row_tokens.astype(jnp.float32))
        grad_params, grad_input = pullback(row_grad.astype(jnp.float32))
        totals = jax.tree.map(jnp.add, totals, grad_params)
        return (totals, (result.astype(jnp.bfloat16), grad_input))
    zeros = jax.tree.map(jnp.zeros_like, params)
    totals, (output, grad_tokens) = lax.scan(one_row, zeros, (tokens, segment_ids, row_fill, cotangent))
    return (output, grad_tokens, totals[0], totals[1], totals[2], totals[3], totals[4], totals[5], totals[6], totals[7], totals[8], totals[9], totals[10], totals[11], totals[12])
```

```python
from functools import partial
import math

import jax
import jax.numpy as jnp
from jax import lax
from jax.experimental import pallas as pl
from jax.experimental.pallas import tpu as pltpu
from jax.sharding import PartitionSpec as P

HEAD_DIM = 64
PAIR = 2 * HEAD_DIM
LONGEST = 256
BLOCK = 256
MASKED = -1e30
F32 = jnp.float32
BF16 = jnp.bfloat16
GELU_C = math.sqrt(2.0 / math.pi)
GELU_A = 0.044715
VMEM_LIMIT = 56 * 1024 * 1024


def dot_nn(a, b):
    return lax.dot_general(a, b, (((1,), (0,)), ((), ())), preferred_element_type=F32)


def dot_nt(a, b):
    return lax.dot_general(a, b, (((1,), (1,)), ((), ())), preferred_element_type=F32)


def dot_tn(a, b):
    return lax.dot_general(a, b, (((0,), (0,)), ((), ())), preferred_element_type=F32)


def window(first, length):
    return max(0, first - LONGEST), min(length, first + BLOCK + LONGEST)


def own_weights(refs):
    wq, wk, wv, bq, bv, wo = refs

    def triple(p):
        cut = pl.ds(pl.multiple_of(p * PAIR, PAIR), PAIR)
        weights = jnp.concatenate([wq[:, cut], wk[:, cut], wv[:, cut]], axis=1)
        bias = jnp.concatenate([bq[:, cut], jnp.zeros((1, PAIR), F32), bv[:, cut]], axis=1)
        return weights, bias

    return triple, lambda: wo[...]


def sent_weights(refs):
    (pack,) = refs
    d = pack.shape[1]
    half = d // 2

    def triple(p):
        left = pl.ds(pl.multiple_of(p * PAIR, PAIR), PAIR)
        right = pl.ds(pl.multiple_of(half + p * PAIR, PAIR), PAIR)
        weights = jnp.concatenate(
            [pack[0:d, left], pack[0:d, right], pack[d : 2 * d, left]], axis=1
        ).astype(BF16)
        bias = jnp.concatenate(
            [
                pack[2 * d : 2 * d + 1, left],
                jnp.zeros((1, PAIR), F32),
                pack[2 * d : 2 * d + 1, right],
            ],
            axis=1,
        )
        return weights, bias

    def out():
        return jnp.concatenate(
            [pack[d : d + half, half:], pack[d + half : 2 * d, half:]], axis=1
        ).astype(BF16)

    return triple, out


def fill_segments(core_ref, fill_ref, seg_ref, cols_ref):
    length = seg_ref.shape[1]
    fill = fill_ref[core_ref[0]]
    row = seg_ref[pl.ds(core_ref[0], 1), :].astype(F32)
    places = lax.broadcasted_iota(jnp.int32, (1, length), 1)
    valid = places < fill
    keyed = jnp.where(valid, row, -1.0)
    cols_ref[...] = jnp.broadcast_to(keyed, (PAIR, length)).T
    return row, jnp.where(valid, 1.0, 0.0)


def mask_for(cols_ref, row, low, high, first):
    cols = cols_ref[low:high, :]
    wide = jnp.concatenate([cols] * (BLOCK // PAIR), axis=1)
    return wide == row[:, first : first + BLOCK]


def forward_kernel(sent, core_ref, fill_ref, tokens_ref, seg_ref, *refs):
    n_weights = 1 if sent else 6
    weights, refs = refs[:n_weights], refs[n_weights:]
    if sent:
        branch_in, out_bias, gate, q_out, k_out, v_out, mixed_out, lse_out, mid_out, low_out, lowt_out, cols = refs
    else:
        q_out, k_out, v_out, mixed_out, lse_out, branch_out, xt_out, cols = refs
    triple, out_weight = (sent_weights if sent else own_weights)(weights)
    length = tokens_ref.shape[1]
    row, valid = fill_segments(core_ref, fill_ref, seg_ref, cols)
    x = tokens_ref[0]
    lanes = lax.broadcasted_iota(jnp.int32, (length, PAIR), 1)

    @pl.loop(0, q_out.shape[0])
    def _(p):
        w3, b3 = triple(p)
        y = dot_nn(x, w3) + b3
        q = (y[:, :PAIR].astype(BF16) * 0.125).astype(BF16)
        k = y[:, PAIR : 2 * PAIR].astype(BF16)
        v = y[:, 2 * PAIR :].astype(BF16)
        vt = v.T
        q_out[p] = q
        k_out[p] = k
        v_out[p] = v
        heads = [jnp.where(lanes < HEAD_DIM, q, 0), jnp.where(lanes < HEAD_DIM, 0, q)]
        for first in range(0, length, BLOCK):
            low, high = window(first, length)
            mask = mask_for(cols, row, low, high, first)
            for h in range(2):
                s = dot_nt(k[low:high], heads[h][first : first + BLOCK])
                s = jnp.where(mask, s, MASKED)
                peak = jnp.max(s, axis=0, keepdims=True)
                e = jnp.exp(s - peak)
                total = jnp.sum(e, axis=0, keepdims=True)
                o = dot_nn(vt[h * HEAD_DIM : (h + 1) * HEAD_DIM, low:high], e.astype(BF16))
                o = o * (valid[:, first : first + BLOCK] / total)
                at = pl.multiple_of(p * PAIR + h * HEAD_DIM, HEAD_DIM)
                mixed_out[pl.ds(at, HEAD_DIM), first : first + BLOCK] = o.astype(BF16)
                lse_out[pl.ds(2 * p + h, 1), first : first + BLOCK] = peak + jnp.log(total)

    branch = dot_tn(mixed_out[...], out_weight())
    if sent:
        middle = x.astype(F32) + gate[0] * (branch_in[...] + branch + out_bias[...])
        mid_out[...] = middle
        low = middle.astype(BF16)
        low_out[...] = low
        lowt_out[...] = low.T
    else:
        branch_out[...] = branch
        xt_out[...] = x.T


def row_spec(shape):
    return pl.BlockSpec((1,) + tuple(shape[1:]), lambda *a: (a[-2][0], 0, 0))


def whole(shape):
    zeros = (0,) * len(shape)
    return pl.BlockSpec(tuple(shape), lambda *a: zeros)


SMEM = pl.BlockSpec(memory_space=pltpu.SMEM)


def call(kernel, core, fill, args, specs, outs, scratch, flops, name):
    moved = sum(math.prod(a.shape) * a.dtype.itemsize for a in args)
    moved += sum(math.prod(o.shape) * o.dtype.itemsize for o in outs)
    return pl.pallas_call(
        kernel,
        grid_spec=pltpu.PrefetchScalarGridSpec(
            num_scalar_prefetch=2,
            grid=(1,),
            in_specs=specs,
            out_specs=[whole(o.shape) for o in outs],
            scratch_shapes=scratch,
        ),
        out_shape=outs,
        compiler_params=pltpu.CompilerParams(vmem_limit_bytes=VMEM_LIMIT),
        cost_estimate=pl.CostEstimate(flops=flops, bytes_accessed=moved, transcendentals=0),
        name=name,
    )(core, fill, *args)


def shape(dims, dtype=F32):
    return jax.ShapeDtypeStruct(tuple(dims), dtype)


def attend_forward(core, fill, tokens, segments, weights, sent, more):
    _, length, d = tokens.shape
    half = d // 2
    pairs = half // PAIR
    outs = [shape((pairs, length, PAIR), BF16)] * 3
    outs += [shape((half, length), BF16), shape((8, length))]
    if sent:
        outs += [shape((length, d)), shape((length, d), BF16), shape((d, length), BF16)]
    else:
        outs += [shape((length, d)), shape((d, length), BF16)]
    args = [tokens, segments, *weights, *more]
    specs = [row_spec(tokens.shape)] + [whole(a.shape) for a in args[1:]]
    if sent:
        specs[-1] = SMEM
    return call(
        partial(forward_kernel, sent), core, fill, args, specs, outs,
        [pltpu.VMEM((length, PAIR), F32)], 12 * length * d * half, "forward_sent" if sent else "forward_own",
    )


def feed_kernel(core_ref, fill_ref, cot_ref, gate, low_ref, lowt_ref, wi_ref, bi_ref, wo_ref, grad_out, hidden_out, pre_out, bias_out):
    units = wi_ref.shape[1]
    d_ffn = (gate[0] * cot_ref[0].astype(F32)).astype(BF16)
    step = 256
    d = low_ref.shape[1]
    for at in range(0, units, step):
        cut = slice(at, at + step)
        wi = wi_ref[:, cut].astype(BF16)
        wo = wo_ref[cut, :].astype(BF16)
        pre = dot_nn(low_ref[...], wi) + bi_ref[:, cut]
        square = pre * pre
        t = jnp.tanh(pre * (GELU_C + (GELU_C * GELU_A) * square))
        cdf = 0.5 + 0.5 * t
        hidden = (pre * cdf).astype(BF16)
        slope = cdf + (0.5 * pre) * (1.0 - t * t) * (GELU_C + (3.0 * GELU_C * GELU_A) * square)
        d_pre = dot_nt(d_ffn, wo) * slope
        low_d = d_pre.astype(BF16)
        hidden_out[:, cut] = hidden
        pre_out[:, cut] = low_d
        bias_out[0:1, cut] = jnp.sum(low_d.astype(F32), axis=0, keepdims=True)
        grad_out[cut, :] = dot_tn(hidden, d_ffn)
        grad_out[units : units + d, cut] = dot_nn(lowt_ref[...], low_d)


def feed(core, fill, cotangent, gate, low, lowt, wi, bi, wo, part):
    _, length, d = cotangent.shape
    units = wi.shape[1] // 2
    outs = [shape((units + d, d)), shape((length, units), BF16), shape((length, units), BF16), shape((8, units))]
    specs = [
        row_spec(cotangent.shape), SMEM, whole(low.shape), whole(lowt.shape),
        pl.BlockSpec((d, units), lambda *a: (0, part)),
        pl.BlockSpec((1, units), lambda *a: (0, part)),
        pl.BlockSpec((units, d), lambda *a: (part, 0)),
    ]
    return call(
        feed_kernel, core, fill, [cotangent, gate, low, lowt, wi, bi, wo], specs, outs, [],
        8 * length * d * units, "feed_%d" % part,
    )


def feed_out_kernel(core_ref, fill_ref, cot_ref, tokens_ref, mid_ref, feed_gate, attention_gate, out_bias, *refs):
    wi_own, wi_sent, wo_own, wo_sent = refs[:4]
    hiddens, pres = refs[4:8], refs[8:12]
    out_ref, dmid_ref, dbranch_ref, small_ref = refs[12:]
    units = hiddens[0].shape[1]
    cot = cot_ref[0].astype(F32)
    ffn = None
    dmid = None
    for i in range(4):
        wi_ref, wo_ref = (wi_own, wo_own) if i < 2 else (wi_sent, wo_sent)
        cut = slice((i % 2) * units, (i % 2 + 1) * units)
        a = dot_nn(hiddens[i][...], wo_ref[cut, :].astype(BF16))
        b = dot_nt(pres[i][...], wi_ref[:, cut].astype(BF16))
        ffn = a if ffn is None else ffn + a
        dmid = b if dmid is None else dmid + b
    ffn = ffn + out_bias[...]
    dmid = dmid + cot
    mid = mid_ref[...]
    out_ref[...] = mid + feed_gate[0] * ffn
    dmid_ref[...] = dmid
    dbranch = (attention_gate[0] * dmid).astype(BF16)
    dbranch_ref[...] = dbranch
    d_ffn = (feed_gate[0] * cot).astype(BF16)
    small_ref[...] = jnp.zeros_like(small_ref)
    small_ref[0:1, :] = jnp.sum(dbranch.astype(F32), axis=0, keepdims=True)
    small_ref[1:2, :] = jnp.sum(d_ffn.astype(F32), axis=0, keepdims=True)
    small_ref[2:3, :] = jnp.sum(cot * ffn, axis=0, keepdims=True)
    branch = mid - tokens_ref[0].astype(F32)
    small_ref[3:4, :] = jnp.sum(dmid * branch, axis=0, keepdims=True) / attention_gate[0]


def backward_kernel(sent, core_ref, fill_ref, dbranch_ref, seg_ref, *refs):
    n_weights = 1 if sent else 6
    weights, refs = refs[:n_weights], refs[n_weights:]
    (q_ref, k_ref, v_ref, mixed_ref, lse_ref, xt_ref, total_in, small_a, small_b, small_c,
     grad_out, total_out, cols, dk_acc, dv_acc, dqt) = refs
    triple, out_weight = (sent_weights if sent else own_weights)(weights)
    length = q_ref.shape[1]
    d = xt_ref.shape[0]
    half = d // 2
    row, valid = fill_segments(core_ref, fill_ref, seg_ref, cols)
    lanes = lax.broadcasted_iota(jnp.int32, (length, PAIR), 1)
    fill = fill_ref[core_ref[0]]
    places = lax.broadcasted_iota(jnp.int32, (length, 1), 0)
    dbranch = dbranch_ref[...]
    total_out[...] = total_in[...]
    grad_out[2 * d :, :] = jnp.zeros((8, d), F32)
    wo_whole = out_weight()
    d_mixed = jnp.where(places < fill, dot_nt(dbranch, wo_whole), 0.0).astype(BF16)
    out_grad = dot_nn(mixed_ref[...], dbranch)
    grad_out[d : d + half, half:] = out_grad[:, :half]
    grad_out[d + half : 2 * d, half:] = out_grad[:, half:]

    for p in range(q_ref.shape[0]):
        w3, _ = triple(p)
        q = q_ref[p]
        k = k_ref[p]
        v = v_ref[p]
        kt = k.T
        do = d_mixed[:, p * PAIR : (p + 1) * PAIR]
        qs = [jnp.where(lanes < HEAD_DIM, q, 0), jnp.where(lanes < HEAD_DIM, 0, q)]
        dos = [jnp.where(lanes < HEAD_DIM, do, 0), jnp.where(lanes < HEAD_DIM, 0, do)]
        dk_acc[...] = jnp.zeros_like(dk_acc)
        dv_acc[...] = jnp.zeros_like(dv_acc)
        for first in range(0, length, BLOCK):
            low, high = window(first, length)
            mask = mask_for(cols, row, low, high, first)
            rows = slice(first, first + BLOCK)
            dk = None
            dv = None
            for h in range(2):
                s = dot_nt(k[low:high], qs[h][rows])
                s = jnp.where(mask, s, MASKED)
                w = jnp.exp(s - lse_ref[2 * p + h : 2 * p + h + 1, rows])
                dw = dot_nt(v[low:high], dos[h][rows])
                both = w * dw
                mean = jnp.sum(both, axis=0, keepdims=True)
                ds = (both - w * mean).astype(BF16)
                a = dot_nn(w.astype(BF16), dos[h][rows])
                b = dot_nn(ds, qs[h][rows])
                dv = a if dv is None else dv + a
                dk = b if dk is None else dk + b
                dqt[h * HEAD_DIM : (h + 1) * HEAD_DIM, rows] = 0.125 * dot_nn(
                    kt[h * HEAD_DIM : (h + 1) * HEAD_DIM, low:high], ds
                )
            dk_acc[low:high, :] += dk
            dv_acc[low:high, :] += dv
        dq = dqt[...].T.astype(BF16)
        dk = dk_acc[...].astype(BF16)
        dv = dv_acc[...].astype(BF16)
        all3 = jnp.concatenate([dq, dk, dv], axis=1)
        grads = dot_nn(xt_ref[...], all3)
        at = p * PAIR
        grad_out[0:d, at : at + PAIR] = grads[:, :PAIR]
        grad_out[0:d, half + at : half + at + PAIR] = grads[:, PAIR : 2 * PAIR]
        grad_out[d : 2 * d, at : at + PAIR] = grads[:, 2 * PAIR :]
        grad_out[2 * d : 2 * d + 1, at : at + PAIR] = jnp.sum(dq.astype(F32), axis=0, keepdims=True)
        grad_out[2 * d : 2 * d + 1, half + at : half + at + PAIR] = jnp.sum(dv.astype(F32), axis=0, keepdims=True)
        total_out[...] += dot_nt(all3, w3)
    grad_out[2 * d + 1 : 2 * d + 2, :] = small_a[0:1, :]
    grad_out[2 * d + 2 : 2 * d + 3, :] = small_b[0:1, :]
    grad_out[2 * d + 3 : 2 * d + 7, :] = small_c[0:4, :]


def attend_backward(core, fill, dbranch, segments, weights, sent, kept, xt, total, smalls):
    length, d = dbranch.shape
    args = [dbranch, segments, *weights, *kept, xt, total, *smalls]
    specs = [whole(a.shape) for a in args]
    outs = [shape((2 * d + 8, d)), shape((length, d))]
    scratch = [pltpu.VMEM((length, PAIR), F32)] * 3 + [pltpu.VMEM((PAIR, length), F32)]
    return call(
        partial(backward_kernel, sent), core, fill, args, specs, outs, scratch,
        30 * length * d * d // 2, "backward_sent" if sent else "backward_own",
    )


def rows_kernel(core_ref, fill_ref, own_ref, came_ref, out_ref):
    out_ref[core_ref[0]] = own_ref[...].astype(out_ref.dtype)
    out_ref[1 - core_ref[0]] = came_ref[...].astype(out_ref.dtype)


def both_rows(core, fill, own, came, dtype):
    length, d = own.shape
    return call(
        rows_kernel, core, fill, [own, came], [whole(own.shape)] * 2,
        [shape((2, length, d), dtype)], [], 0, "both_rows",
    )[0]


def halving_step(step, members):
    pairs = []
    for place in range(members):
        for core in range(2):
            bit = step ^ core if step < 2 else step
            pairs.append((place * 2 + core, (place ^ (1 << bit)) * 2 + core))
    return pairs


def my_bits(members):
    place = lax.axis_index("dp")
    core = lax.axis_index("mp")
    bits = []
    for step in range(members.bit_length() - 1):
        bit = step ^ core if step < 2 else step
        bits.append((place >> bit) & 1)
    return bits


def reduce_halves(array, members, bits, small=None):
    width = array.shape[1]
    for step, bit in enumerate(bits):
        rows = array.shape[0] // 2
        halves = array.reshape(2, rows, width)
        send = lax.dynamic_index_in_dim(halves, 1 - bit, 0, False)
        keep = lax.dynamic_index_in_dim(halves, bit, 0, False)
        if small is not None:
            send = jnp.concatenate([send, small])
        came = lax.ppermute(send, ("dp", "mp"), halving_step(step, members))
        array = keep + came[:rows]
        if small is not None:
            small = small + came[rows:]
    return array, small


def gather_halves(array, members, bits):
    for step in reversed(range(len(bits))):
        came = lax.ppermute(array, ("dp", "mp"), halving_step(step, members))
        array = jnp.where(
            bits[step] == 0, jnp.concatenate([array, came]), jnp.concatenate([came, array])
        )
    return array


def shards(members, tokens, segment_ids, row_fill, query_weight, query_bias, key_weight,
           value_weight, value_bias, out_weight, out_bias, attention_gate, inner_weight,
           inner_bias, outer_weight, outer_bias, feed_gate, cotangent):
    _, length, d = tokens.shape
    half = d // 2
    own = lax.axis_index("mp")
    core = own.astype(jnp.int32).reshape(1)
    swap = [(0, 1), (1, 0)]

    def across(array):
        return lax.ppermute(array, "mp", swap)

    qb = query_bias.reshape(1, -1)
    vb = value_bias.reshape(1, -1)
    ib = inner_bias.reshape(1, -1)
    pack = jnp.concatenate(
        [
            jnp.concatenate([query_weight, key_weight], axis=1).astype(F32),
            jnp.concatenate(
                [value_weight, jnp.concatenate([out_weight[:, :half], out_weight[:, half:]])], axis=1
            ).astype(F32),
            jnp.concatenate([qb, vb], axis=1),
            jnp.zeros((7, d), F32),
        ]
    )
    pack_sent = across(pack)
    wi_sent = across(inner_weight.astype(F32))
    wo_sent = across(outer_weight.astype(F32))
    ib_sent = across(ib)
    a_gate = attention_gate.reshape(1)
    f_gate = feed_gate.reshape(1)
    own_set = (query_weight, key_weight, value_weight, qb, vb, out_weight)

    *kept_own, branch, xt = attend_forward(
        core, row_fill, tokens, segment_ids, own_set, False, ()
    )
    *kept_sent, middle, low, lowt = attend_forward(
        core, row_fill, tokens, segment_ids, (pack_sent,), True, (branch, out_bias.reshape(1, -1), a_gate)
    )

    def part(index, sent):
        if sent:
            weights = (wi_sent, ib_sent, wo_sent)
        else:
            weights = (inner_weight, ib, outer_weight)
        return feed(core, row_fill, cotangent, f_gate, low, lowt, *weights, index)

    bits = my_bits(members)
    sent_0 = part(0, True)
    own_0 = part(0, False)
    first = own_0[0] + across(sent_0[0])
    first, _ = reduce_halves(first, members, bits)
    sent_1 = part(1, True)
    own_1 = part(1, False)
    second = own_1[0] + across(sent_1[0])
    second, _ = reduce_halves(second, members, bits)

    parts = (own_0, own_1, sent_0, sent_1)
    args = [cotangent, tokens, middle, f_gate, a_gate, outer_bias.reshape(1, -1),
            inner_weight, wi_sent, outer_weight, wo_sent]
    args += [p[1] for p in parts] + [p[2] for p in parts]
    specs = [whole(a.shape) for a in args]
    specs[0] = specs[1] = row_spec(tokens.shape)
    specs[3] = specs[4] = SMEM
    out_own, dmid, dbranch, small = call(
        feed_out_kernel, core, row_fill, args, specs,
        [shape((length, d)), shape((length, d)), shape((length, d), BF16), shape((8, d))], [],
        16 * length * d * d, "feed_out",
    )
    out_sent = across(out_own)

    g_sent, total = attend_backward(
        core, row_fill, dbranch, segment_ids, (pack_sent,), True, kept_sent, xt, dmid,
        (sent_0[3], sent_1[3], small),
    )
    g_came = across(g_sent)
    g_own, total = attend_backward(
        core, row_fill, dbranch, segment_ids, own_set, False, kept_own, xt, total,
        (own_0[3], own_1[3], small),
    )
    total_came = across(total)
    third = g_own + g_came
    third, tiny = reduce_halves(third[: 2 * d], members, bits, third[2 * d :])

    first = gather_halves(first, members, bits)
    second = gather_halves(second, members, bits)
    third = gather_halves(third, members, bits)

    output = both_rows(core, row_fill, out_own, out_sent, BF16)
    grad_tokens = both_rows(core, row_fill, total, total_came, F32)
    units = first.shape[0] - d
    return (
        output,
        grad_tokens,
        third[:d, :half],
        tiny[0, :half],
        third[:d, half:],
        third[d:, :half],
        tiny[0, half:],
        jnp.concatenate([third[d : d + half, half:], third[d + half :, half:]], axis=1),
        tiny[3],
        jnp.sum(tiny[6]),
        jnp.concatenate([first[units:], second[units:]], axis=1),
        jnp.concatenate([tiny[1], tiny[2]]),
        jnp.concatenate([first[:units], second[:units]]),
        tiny[4],
        jnp.sum(tiny[5]),
    )


def solution(mesh):
    rows = P("dp", None, None)
    col = P(None, "mp")
    cut = P("mp")
    in_specs = (
        rows, P("dp", None), P("dp"), col, cut, col, col, cut, P("mp", None), P(), P(),
        col, cut, P("mp", None), P(), P(), rows,
    )
    out_specs = (
        rows, rows, col, cut, col, col, cut, P("mp", None), P(), P(), col, cut,
        P("mp", None), P(), P(),
    )
    return jax.shard_map(
        partial(shards, mesh.shape["dp"]), mesh=mesh, in_specs=in_specs, out_specs=out_specs,
        check_vma=False,
    )
```

```python
from functools import partial
import math

import jax
import jax.numpy as jnp
from jax import lax
from jax.experimental import pallas as pl
from jax.experimental.pallas import tpu as pltpu
from jax.sharding import PartitionSpec as P

HEAD_DIM = 64
PAIR = 2 * HEAD_DIM
LONGEST = 256
BLOCK = 128
TINY = 8
MASKED = -1e30
F32 = jnp.float32
BF16 = jnp.bfloat16
GELU_C = math.sqrt(2.0 / math.pi)
GELU_A = 0.044715
BIG_LIMIT = 60 * 1024 * 1024
WEIGHTS = {"feed_other_1": 0.0, "feed_own_1": 0.0, "backward_own": 40.0, "output": 80.0}
SMALL_LIMIT = 8 * 1024 * 1024
SMEM = pl.BlockSpec(memory_space=pltpu.SMEM)
VMEM = pl.BlockSpec(memory_space=pltpu.VMEM)
WHERE_IT_IS = pl.BlockSpec(memory_space=pl.ANY)
HBM = pl.BlockSpec(memory_space=pltpu.HBM)


def dot_nn(a, b):
    return lax.dot_general(a, b, (((1,), (0,)), ((), ())), preferred_element_type=F32)


def dot_nt(a, b):
    return lax.dot_general(a, b, (((1,), (1,)), ((), ())), preferred_element_type=F32)


def dot_tn(a, b):
    return lax.dot_general(a, b, (((0,), (0,)), ((), ())), preferred_element_type=F32)


def shape(dims, dtype=F32):
    return jax.ShapeDtypeStruct(tuple(dims), dtype)


class Take:
    def __init__(self, dims, dtype, copies, held=False):
        self.dims, self.dtype, self.copies, self.held = tuple(dims), dtype, copies, held


def take(array, index=None, dims=None):
    return Take(dims or array.shape, array.dtype, [(array, index, None)], True)


def fetch(array, index=None, dims=None):
    return Take(dims or array.shape, array.dtype, [(array, index, None)])


class Coming:
    def __init__(self, buffer, copies):
        self.buffer, self.copies = buffer, copies

    def __call__(self):
        for copy in self.copies:
            copy.wait()
        self.copies = []
        return self.buffer


class Going:
    def __init__(self, target, buffer, sem):
        self.target, self.buffer, self.sem, self.copy = target, buffer, sem, None

    def __setitem__(self, index, value):
        self.buffer[index] = value

    def __getitem__(self, index):
        return self.buffer[index]

    def send(self):
        if self.target is not None and self.copy is None:
            self.copy = pltpu.make_async_copy(self.buffer, self.target, self.sem)
            self.copy.start()


def send_swapped(swap, one, two):
    straight = [pltpu.make_async_copy(o.buffer, o.target, o.sem) for o in (one, two)]
    crossed = [
        pltpu.make_async_copy(one.buffer, two.target, one.sem),
        pltpu.make_async_copy(two.buffer, one.target, two.sem),
    ]

    @pl.when(swap)
    def _():
        for copy in crossed:
            copy.start()

    @pl.when(jnp.logical_not(swap))
    def _():
        for copy in straight:
            copy.start()

    one.copy, two.copy = straight


def pick(ref, index, scalars):
    if index is None:
        return ref
    return ref.at[index(*scalars) if callable(index) else index]


class Chain:
    def __init__(self):
        self.last = None

    def call(self, kernel, name, scalars, takes, outs, scratch=(), leaves=False, weight=None):
        arrays, spaces, spots = [], [], []

        def place(array, space):
            for i, (known, its) in enumerate(zip(arrays, spaces)):
                if known is array and its is space:
                    return i
            arrays.append(array)
            spaces.append(space)
            return len(arrays) - 1

        fetched = [one for one in takes if not one.held]
        views = []
        for one in takes:
            if one.held:
                views.append((place(one.copies[0][0], VMEM), one.copies[0][1]))
            else:
                spots.append([(place(a, HBM), s, t) for a, s, t in one.copies])
        after = [] if self.last is None else [self.last]
        n_scalar, n_array, n_out = len(scalars), len(arrays), len(outs)
        n_copies = sum(len(one) for one in spots)

        def body(*refs):
            numbers, refs = refs[:n_scalar], refs[n_scalar:]
            given, refs = refs[:n_array], refs[n_array + len(after) :]
            results, refs = refs[:n_out], refs[n_out:]
            sems, refs = refs[0], refs[1:]
            into, refs = refs[: len(fetched)], refs[len(fetched) :]
            outof, rest = (refs[:n_out], refs[n_out:]) if leaves else (results, refs)
            at = 0
            buffers = []
            for buffer, copies in zip(into, spots):
                started = []
                for which, source, target in copies:
                    copy = pltpu.make_async_copy(
                        pick(given[which], source, numbers), pick(buffer, target, numbers), sems.at[at]
                    )
                    copy.start()
                    started.append(copy)
                    at += 1
                buffers.append(Coming(buffer, started))
            left, seen, coming = list(buffers), list(views), []
            for one in takes:
                if one.held:
                    which, index = seen.pop(0)
                    coming.append(Coming(pick(given[which], index, numbers), []))
                else:
                    coming.append(left.pop(0))
            going = [
                Going(result if leaves else None, buffer, sems.at[at + i])
                for i, (result, buffer) in enumerate(zip(results, outof))
            ]
            kernel(*numbers, *coming, *going, *rest)
            for one in coming:
                one()
            for one in going:
                one.send()
            for one in going:
                if one.copy is not None:
                    one.copy.wait()

        body.__name__ = name
        out = pl.pallas_call(
            body,
            in_specs=[SMEM] * n_scalar + spaces + [WHERE_IT_IS] * len(after),
            out_specs=[HBM if leaves else VMEM] * n_out,
            out_shape=list(outs),
            scratch_shapes=[pltpu.SemaphoreType.DMA((n_copies + n_out,))]
            + [pltpu.VMEM(one.dims, one.dtype) for one in fetched]
            + [pltpu.VMEM(o.shape, o.dtype) for o in outs if leaves]
            + list(scratch),
            compiler_params=pltpu.CompilerParams(vmem_limit_bytes=BIG_LIMIT if leaves else SMALL_LIMIT),
            cost_estimate=pl.CostEstimate(flops=int(1e9 * (WEIGHTS.get(name, 17.0 if leaves else 0.0) if weight is None else weight)) + 1000, bytes_accessed=1000, transcendentals=0),
            name=name,
        )(*scalars, *arrays, *after)
        self.last = out[0]
        return out


def window(first, length):
    return max(0, first - LONGEST), min(length, first + BLOCK + LONGEST)


class Weights:
    def __init__(self, wq, wk, wv, bq, bv, wo):
        self.projections, self.biases, self.wo = (wq, wk, wv), (bq, bv), wo

    def cut(self, p, n=1):
        if callable(p):
            return lambda *numbers: pl.ds(pl.multiple_of(p(*numbers) * PAIR, PAIR), n * PAIR)
        return lambda *numbers: slice(p * PAIR, (p + n) * PAIR)

    def triple(self, p):
        d = self.wo.shape[1]
        cut = self.cut(p)
        return Take(
            (d, 3 * PAIR), BF16,
            [
                (a, lambda *n: (slice(None), cut(*n)), (slice(None), slice(i * PAIR, (i + 1) * PAIR)))
                for i, a in enumerate(self.projections)
            ],
        )

    def out(self, p, n=1):
        d = self.wo.shape[1]
        cut = self.cut(p, n)
        return Take((n * PAIR, d), BF16, [(self.wo, lambda *k: (cut(*k), slice(None)), None)])

    def bias(self):
        bq, bv = self.biases
        half = bq.shape[1]
        return Take(
            (1, 2 * half), F32,
            [(bq, None, (slice(None), slice(0, half))), (bv, None, (slice(None), slice(half, 2 * half)))],
        )


def row_index(other):
    return lambda core, *_: 1 - core[0] if other else core[0]


def row_of(array, other):
    return Take(array.shape[1:], array.dtype, [(array, row_index(other), None)])


def segments_of(place, fill_ref, seg, cols_ref):
    length = cols_ref.shape[0]
    fill = fill_ref[place]
    row = seg()[pl.ds(place, 1), :].astype(F32)
    places = lax.broadcasted_iota(jnp.int32, (1, length), 1)
    valid = places < fill
    keyed = jnp.where(valid, row, -1.0)
    cols_ref[...] = jnp.broadcast_to(keyed, (PAIR, length)).T
    return row, jnp.where(valid, 1.0, 0.0)


def mask_for(cols_ref, row, low, high, first):
    once = cols_ref[low:high, :] == row[:, first : first + BLOCK]
    return jnp.concatenate([once, once], axis=1)


def two_heads(array):
    lanes = lax.broadcasted_iota(jnp.int32, array.shape, 1)
    return jnp.where(lanes < HEAD_DIM, array, 0), jnp.where(lanes < HEAD_DIM, 0, array)


def stacked(pair, first):
    return jnp.concatenate([half[first : first + BLOCK] for half in pair], axis=0)


def forward_pair(p, x, w3, bias, row, valid, cols, qkv, mixed_out, lse):
    length = x.shape[0]
    half = bias.shape[1] // 2
    y = dot_nn(x, w3)
    at = p * PAIR
    q = y[:, :PAIR] + bias[0:1, at : at + PAIR]
    q = (q.astype(BF16) * 0.125).astype(BF16)
    k = y[:, PAIR : 2 * PAIR].astype(BF16)
    v = (y[:, 2 * PAIR :] + bias[0:1, half + at : half + at + PAIR]).astype(BF16)
    vt = v.T
    qkv[0] = q
    qkv[1] = k
    qkv[2] = v
    heads = two_heads(q)
    for first in range(0, length, BLOCK):
        low, high = window(first, length)
        block = slice(first, first + BLOCK)
        s = dot_nt(k[low:high], stacked(heads, first))
        s = jnp.where(mask_for(cols, row, low, high, first), s, MASKED)
        peak = jnp.max(s, axis=0, keepdims=True)
        e = jnp.exp(s - peak)
        total = jnp.sum(e, axis=0, keepdims=True)
        o = dot_nn(vt[:, low:high], e.astype(BF16))
        keep = valid[:, block]
        o0 = o[:HEAD_DIM, :BLOCK] * (keep / total[:, :BLOCK])
        o1 = o[HEAD_DIM:, BLOCK:] * (keep / total[:, BLOCK:])
        mixed_out[:HEAD_DIM, block] = o0.astype(BF16)
        mixed_out[HEAD_DIM:, block] = o1.astype(BF16)
        lse[0:1, 2 * first : 2 * first + 2 * BLOCK] = peak + jnp.log(total)


def forward_other_kernel(core_ref, fill_ref, x_in, w3_0, bias, seg, w3_1, wo, qkv, mixed, lse, branch_out, cols):
    row, valid = segments_of(1 - core_ref[0], fill_ref, seg, cols)
    x = x_in()[...]
    for p, w3 in enumerate((w3_0, w3_1)):
        forward_pair(
            p, x, w3()[...], bias(), row, valid, cols, qkv.buffer.at[p], mixed.buffer.at[p], lse.buffer.at[p]
        )
    qkv.send()
    mixed.send()
    lse.send()
    branch_out[...] = dot_tn(mixed[0], wo()[:PAIR, :]) + dot_tn(mixed[1], wo()[PAIR:, :])


def forward_own_kernel(p, core_ref, fill_ref, *refs):
    if p:
        gate, refs = refs[0], refs[1:]
    x_in, w3, bias, seg, *refs = refs
    if p:
        wo, mixed_0, came, out_bias, qkv, mixed, lse, middle, cols = refs
    else:
        qkv, mixed, lse, cols = refs
    row, valid = segments_of(core_ref[0], fill_ref, seg, cols)
    x = x_in()[...]
    forward_pair(p, x, w3()[...], bias(), row, valid, cols, qkv.buffer, mixed.buffer, lse.buffer)
    qkv.send()
    mixed.send()
    lse.send()
    if p:
        branch = dot_tn(mixed_0()[...], wo()[:PAIR, :]) + dot_tn(mixed[...], wo()[PAIR:, :])
        branch = (branch + came()[...]) + out_bias()[...]
        middle[...] = x.astype(F32) + gate[0] * branch


def feed_kernel(second, adds, core_ref, gate, *refs):
    if adds:
        bit, refs = refs[0], refs[1:]
    mid_in, wi_in, bias_in, cot_in, wo_in, *refs = refs
    if second:
        hidden_0, pre_0, wi_0, wo_0, out_bias, *refs = refs
    if adds:
        outer_in, inner_in, *refs = refs
    if second:
        grad_a, grad_b, bias_out, dmid_out, ffn_out = refs
    else:
        grad_a, grad_b, bias_out, hidden_out, pre_out = refs
    low = mid_in()[...].astype(BF16)
    d = low.shape[1]
    units = wi_in.buffer.shape[1]
    lowt = low.T
    cot = cot_in()[...].astype(F32)
    d_ffn = (gate[0] * cot).astype(BF16)
    step = 256
    dmid = ffn = None
    for at in range(0, units, step):
        cut = slice(at, at + step)
        wi = wi_in()[:, cut]
        pre = dot_nn(low, wi) + bias_in()[0:1, cut]
        wo = wo_in()[cut, :]
        square = pre * pre
        t = jnp.tanh(pre * (GELU_C + (GELU_C * GELU_A) * square))
        cdf = 0.5 + 0.5 * t
        hidden = (pre * cdf).astype(BF16)
        slope = cdf + (0.5 * pre) * (1.0 - t * t) * (GELU_C + (3.0 * GELU_C * GELU_A) * square)
        d_pre = dot_nt(d_ffn, wo) * slope
        low_d = d_pre.astype(BF16)
        bias_out[0:1, cut] = jnp.sum(low_d.astype(F32), axis=0, keepdims=True)
        outer = dot_tn(hidden, d_ffn)
        inner = dot_nn(lowt, low_d)
        if adds:
            outer = outer + outer_in()[cut, :]
            inner = inner + inner_in()[:, cut]
        grad_a[cut, :] = outer
        grad_b[:, cut] = inner
        if second:
            more = dot_nt(low_d, wi)
            dmid = more if dmid is None else dmid + more
            more = dot_nn(hidden, wo)
            ffn = more if ffn is None else ffn + more
        else:
            hidden_out[:, cut] = hidden
            pre_out[:, cut] = low_d
    if adds:
        send_swapped(bit[0] != 0, grad_a, grad_b)
    else:
        grad_a.send()
        grad_b.send()
    bias_out[1:, :] = jnp.zeros((TINY - 1, units), F32)
    if second:
        length = low.shape[0]
        dmid_out[:length, :] = dmid + dot_nt(pre_0()[...], wi_0()[...])
        ffn = ffn + dot_nn(hidden_0()[...], wo_0()[...])
        ffn_out[...] = ffn
        if adds:
            ffn = ffn + out_bias()[...]
        dmid_out[length:, :] = jnp.zeros((TINY, d), F32)
        dmid_out[length : length + 1, :] = jnp.sum(cot * ffn, axis=0, keepdims=True)
        bias_out[1:2, :] = jnp.sum(d_ffn.astype(F32), axis=0, keepdims=True)


def feed(chain, name, second, adds, core, gate, middle, other, cotangent, wi, wo, bi, bit=None, held=(), grads=()):
    length, d = middle.shape
    units = wi.shape[1] // 2
    halves = [slice(0, units), slice(units, 2 * units)]
    cut = halves[second]
    takes = [
        fetch(middle), fetch(wi, (slice(None), cut), (d, units)), fetch(bi, (slice(None), cut), (1, units)),
        row_of(cotangent, other), fetch(wo, (cut, slice(None)), (units, d)),
    ]
    if second:
        hidden, pre, out_bias = held
        takes += [
            fetch(hidden), fetch(pre), fetch(wi, (slice(None), halves[0]), (d, units)),
            fetch(wo, (halves[0], slice(None)), (units, d)), fetch(out_bias),
        ]
    takes += [fetch(g) for g in grads]
    outs = [shape((units, d)), shape((d, units)), shape((TINY, units))]
    if second:
        outs += [shape((length + TINY, d)), shape((length, d))]
    else:
        outs += [shape((length, units), BF16)] * 2
    return chain.call(
        partial(feed_kernel, bool(second), adds), name, [core, gate] + ([bit] if adds else []), takes, outs,
        leaves=True,
    )


def backward_pair(dbranch, do, qkv, lse, mixed, x, row, cols, dk_acc, dv_acc, dqt, grad_out):
    length, d = dbranch.shape
    q, k, v = qkv[0], qkv[1], qkv[2]
    kt = k.T
    qs = two_heads(q)
    dos = two_heads(do)
    dk_acc[...] = jnp.zeros_like(dk_acc)
    dv_acc[...] = jnp.zeros_like(dv_acc)
    for first in range(0, length, BLOCK):
        low, high = window(first, length)
        block = slice(first, first + BLOCK)
        qq = stacked(qs, first)
        dd = stacked(dos, first)
        s = dot_nt(k[low:high], qq)
        s = jnp.where(mask_for(cols, row, low, high, first), s, MASKED)
        w = jnp.exp(s - lse[0:1, 2 * first : 2 * first + 2 * BLOCK])
        dw = dot_nt(v[low:high], dd)
        both = w * dw
        mean = jnp.sum(both, axis=0, keepdims=True)
        ds = (both - w * mean).astype(BF16)
        dv_acc[low:high, :] += dot_nn(w.astype(BF16), dd)
        dk_acc[low:high, :] += dot_nn(ds, qq)
        dq = dot_nn(kt[:, low:high], ds)
        dqt[:HEAD_DIM, block] = dq[:HEAD_DIM, :BLOCK]
        dqt[HEAD_DIM:, block] = dq[HEAD_DIM:, BLOCK:]
    dq = (0.125 * dqt[...]).T.astype(BF16)
    all3 = jnp.concatenate([dq, dk_acc[...].astype(BF16), dv_acc[...].astype(BF16)], axis=1)
    grad_out[:, : 3 * PAIR] = dot_tn(x, all3)
    out_grad = dot_nn(mixed, dbranch)
    for c in range(d // PAIR):
        cut = slice(c * PAIR, (c + 1) * PAIR)
        grad_out[cut, 3 * PAIR :] = out_grad[:, cut]
    return all3


def bias_sums(all3):
    sums = jnp.sum(all3.astype(F32), axis=0, keepdims=True)
    return jnp.concatenate([sums[:, :PAIR], sums[:, 2 * PAIR :]], axis=1)


def masked_heads(dbranch, wo, fill):
    places = lax.broadcasted_iota(jnp.int32, (dbranch.shape[0], 1), 0)
    return jnp.where(places < fill, dot_nt(dbranch, wo), 0.0).astype(BF16)


def branch_gradient(gate, mine, came, cot):
    length = cot().shape[0]
    dmid = (mine()[:length, :] + came()[:length, :]) + cot()[...].astype(F32)
    return dmid, (gate[0] * dmid).astype(BF16)


def row_smalls(gate, mine, came, mid, x, dmid, dbranch):
    length = dmid.shape[0]
    branch = mid()[...] - x.astype(F32)
    return (
        jnp.sum(dbranch.astype(F32), axis=0, keepdims=True),
        jnp.sum(dmid * branch, axis=0, keepdims=True) / gate[0],
        mine()[length : length + 1, :] + came()[length : length + 1, :],
    )


def backward_own_kernel(core_ref, fill_ref, gate, mine, came, cot, wo, seg, qkv_0, lse_0, x_in, mixed_0, qkv_1, lse_1,
                        mixed_1, w3_0, w3_1, mid, bias_a0, bias_b0, bias_a1, bias_b1,
                        grad_out, total_out, small_out, cols, dk_acc, dv_acc, dqt):
    row, _ = segments_of(core_ref[0], fill_ref, seg, cols)
    fill = fill_ref[core_ref[0]]
    dmid, dbranch = branch_gradient(gate, mine, came, cot)
    total_out[...] = dmid
    do = masked_heads(dbranch, wo()[...], fill)
    x = x_in()[...]
    first = backward_pair(
        dbranch, do[:, :PAIR], qkv_0(), lse_0(), mixed_0()[...], x, row, cols, dk_acc, dv_acc, dqt, grad_out.buffer.at[0]
    )
    second = backward_pair(
        dbranch, do[:, PAIR:], qkv_1(), lse_1(), mixed_1()[...], x, row, cols, dk_acc, dv_acc, dqt, grad_out.buffer.at[1]
    )
    grad_out.send()
    total_out[...] += dot_nt(first, w3_0()[...]) + dot_nt(second, w3_1()[...])
    total_out.send()
    small_out[...] = jnp.zeros(small_out.buffer.shape, F32)
    small_out[0:1, :] = jnp.concatenate([bias_sums(first), bias_sums(second)], axis=1)
    small_out[1:2, :] = bias_a0()[0:1, :] + bias_b0()[0:1, :]
    small_out[2:3, :] = bias_a1()[0:1, :] + bias_b1()[0:1, :]
    small_out[4:5, :] = bias_a1()[1:2, :] + bias_b1()[1:2, :]
    three, five, six = row_smalls(gate, mine, came, mid, x, dmid, dbranch)
    small_out[3:4, :] = three
    small_out[5:6, :] = five
    small_out[6:7, :] = six


def backward_other_kernel(last, core_ref, fill_ref, gate, pair, *refs):
    if last:
        dbranch_in, *refs = refs
    else:
        mine, came, cot, *refs = refs
    wo, seg, qkv, lse, x_in, mixed, grad_in, small_in, *refs = refs
    if last:
        w3, all3_in, w3_before, *refs = refs
        grad_out, small_out, total_out, cols, dk_acc, dv_acc, dqt = refs
    else:
        mid, *refs = refs
        grad_out, small_out, dbranch_out, all3_out, cols, dk_acc, dv_acc, dqt = refs
    place = 1 - core_ref[0]
    row, _ = segments_of(place, fill_ref, seg, cols)
    if last:
        dbranch = dbranch_in()[...]
    else:
        dmid, dbranch = branch_gradient(gate, mine, came, cot)
        dbranch_out[...] = dbranch
        dbranch_out.send()
    do = masked_heads(dbranch, wo()[...], fill_ref[place])
    x = x_in()[...]
    all3 = backward_pair(
        dbranch, do, qkv(), lse(), mixed()[...], x, row, cols, dk_acc, dv_acc, dqt, grad_out.buffer
    )
    grad_out[...] += grad_in()[...]
    grad_out.send()
    small_out[...] = small_in()[...]
    spot = pl.ds(pl.multiple_of(pair[0] * 2 * PAIR, PAIR), 2 * PAIR)
    small_out[0:1, spot] += bias_sums(all3)
    if last:
        total_out[...] = dot_nt(all3_in()[...], w3_before()[...]) + dot_nt(all3, w3()[...])
    else:
        all3_out[...] = all3
        three, five, six = row_smalls(gate, mine, came, mid, x, dmid, dbranch)
        small_out[3:4, :] += three
        small_out[5:6, :] += five
        small_out[6:7, :] += six


def attention_scratch(length):
    return [pltpu.VMEM((length, PAIR), F32)] * 3 + [pltpu.VMEM((PAIR, length), F32)]


class Stream:
    def __init__(self, chain, members, send, bit_steps):
        self.chain, self.members = chain, members
        self.steps = members.bit_length() - 1
        self.bits = bit_steps
        self.came = self.travel(send, 0)
        self.step = 1
        self.back = False
        self.tail = 0
        self.small = None

    def keep(self, mine, small=None):
        self.mine, self.small = mine, small
        self.rows = mine.shape[0]

    def travel(self, array, step):
        pairs = []
        for place in range(self.members):
            for core in range(2):
                bit = step ^ core if step < 2 else step
                pairs.append((place * 2 + core, (place ^ (1 << bit)) * 2 + core))
        return lax.ppermute(array, ("dp", "mp"), pairs)

    def halve(self):
        rows, tail = self.rows // 2, self.tail
        begins = self.small is not None and not tail
        width = self.mine.shape[1]
        takes = [self.get(self.mine), self.get(self.came)]
        if begins:
            takes.append(self.get(self.small))

        def kernel(bit, mine, came, *refs):
            if begins:
                small, *refs = refs
            send, keep = refs
            other = pl.ds(pl.multiple_of((1 - bit[0]) * rows, 8), rows)
            own = pl.ds(pl.multiple_of(bit[0] * rows, 8), rows)
            send[:rows, :] = mine()[other, :] + came()[other, :]
            keep[:rows, :] = mine()[own, :] + came()[own, :]
            if begins or tail:
                both = small()[...] if begins else mine()[2 * rows :, :] + came()[2 * rows :, :]
                send[rows:, :] = both
                keep[rows:, :] = both

        if begins:
            self.tail = TINY
        out = shape((rows + self.tail, width))
        send, self.mine = self.chain.call(
            kernel, "halve", [self.bits[self.step]], takes, [out, out], leaves=self.far, weight=self.weight
        )
        self.came = self.travel(send, self.step)
        self.rows = rows
        self.step += 1

    def turn(self):
        rows = self.rows

        def kernel(mine, came, out, *tiny):
            out[...] = mine()[:rows, :] + came()[:rows, :]
            if tiny:
                tiny[0][...] = mine()[rows:, :] + came()[rows:, :]

        width = self.mine.shape[1]
        outs = [shape((rows, width))]
        if self.tail:
            outs.append(shape((TINY, width)))
        self.mine, *tiny = self.chain.call(
            kernel, "turn", [], [self.get(self.mine), self.get(self.came)], outs, leaves=self.far, weight=self.weight
        )
        self.small = tiny[0] if tiny else None
        self.back = True
        self.step -= 1
        self.came = self.travel(self.mine, self.step)

    def double(self):
        rows = self.rows
        ends = self.step == 1 and self.small is not None
        takes = [self.get(self.mine), self.get(self.came)]
        if ends:
            takes.append(self.get(self.small))

        def kernel(bit, mine, came, *refs):
            if ends:
                small, *refs = refs
                refs[0][2 * rows :, :] = small()[...]
            (out,) = refs
            out[pl.ds(pl.multiple_of(bit[0] * rows, 8), rows), :] = mine()[...]
            out[pl.ds(pl.multiple_of((1 - bit[0]) * rows, 8), rows), :] = came()[...]

        self.mine = self.chain.call(
            kernel, "double", [self.bits[self.step]], takes,
            [shape((2 * rows + (TINY if ends else 0), self.mine.shape[1]))], leaves=self.far, weight=self.weight,
        )[0]
        self.rows = 2 * rows
        self.step -= 1
        self.came = self.travel(self.mine, self.step)

    def get(self, array):
        return fetch(array) if self.far else take(array)

    def advance(self, far=False, weight=0.0):
        self.far, self.weight = far, weight
        if self.done():
            return
        if self.back:
            self.double()
        elif self.step < self.steps:
            self.halve()
        else:
            self.turn()

    def done(self):
        return self.back and self.step == 0


def in_order(bit, mine, came, low, high):
    @pl.when(bit[0] == 0)
    def _():
        low(mine())
        high(came())

    @pl.when(bit[0] != 0)
    def _():
        low(came())
        high(mine())


def final_feed(chain, first, second, d):
    units = first.mine.shape[0]

    def kernel(bit, mine_a, came_a, mine_b, came_b, inner, outer):
        for at, mine, came in ((0, mine_a, came_a), (1, mine_b, came_b)):
            cut = slice(at * units, (at + 1) * units)

            def low(ref, cut=cut):
                outer[cut, :] = ref[...]

            def high(ref, cut=cut):
                inner[:, cut] = ref[...]

            in_order(bit, mine, came, low, high)

    return chain.call(
        kernel, "final_feed", [first.bits[0]],
        [take(first.mine), take(first.came), take(second.mine), take(second.came)],
        [shape((d, 2 * units)), shape((2 * units, d))], leaves=True,
    )


def final_attention(chain, third, d):
    half = d // 2

    def kernel(bit, mine, came, gq, gk, gv, go, small):
        small[...] = mine()[d:, :] + came()[d:, :]

        def place(p, ref):
            cut = slice(p * PAIR, (p + 1) * PAIR)
            gq[:, cut] = ref[:d, :PAIR]
            gk[:, cut] = ref[:d, PAIR : 2 * PAIR]
            gv[:, cut] = ref[:d, 2 * PAIR : 3 * PAIR]
            for c in range(d // PAIR):
                across = slice(c * PAIR, (c + 1) * PAIR)
                go[cut, across] = ref[across, 3 * PAIR :]

        in_order(bit, mine, came, partial(place, 0), partial(place, 1))

    return chain.call(
        kernel, "final_attention", [third.bits[0]], [take(third.mine), take(third.came)],
        [shape((d, half))] * 3 + [shape((half, d)), shape((TINY, d))], leaves=True,
    )


def output_kernel(core_ref, gate, mid_own, ffn_own, came_own, out_bias, mid_other, ffn_other, came_other, out):
    def row(mid, ffn, came):
        return (mid()[...] + gate[0] * ((ffn()[...] + came()[...]) + out_bias()[...])).astype(BF16)

    out[core_ref[0]] = row(mid_own, ffn_own, came_own)
    out[1 - core_ref[0]] = row(mid_other, ffn_other, came_other)


def tokens_kernel(core_ref, own, came_own, other, came_other, out):
    out[core_ref[0]] = own()[...] + came_own()[...]
    out[1 - core_ref[0]] = other()[...] + came_other()[...]


def shards(members, tokens, segment_ids, row_fill, query_weight, query_bias, key_weight,
           value_weight, value_bias, out_weight, out_bias, attention_gate, inner_weight,
           inner_bias, outer_weight, outer_bias, feed_gate, cotangent):
    _, length, d = tokens.shape
    half = d // 2
    place = lax.axis_index("dp")
    core_id = lax.axis_index("mp")
    core = core_id.astype(jnp.int32).reshape(1)
    bits, others = [], []
    for step in range(members.bit_length() - 1):
        bit = (place >> (step ^ core_id if step < 2 else step)) & 1
        bits.append(bit.astype(jnp.int32).reshape(1))
    not_mine = 1 - bits[0]
    chain = Chain()

    def across(array):
        return lax.ppermute(array, "mp", [(0, 1), (1, 0)])

    def as_row(array):
        return array.reshape(1, -1)

    a_gate = attention_gate.reshape(1)
    f_gate = feed_gate.reshape(1)
    weights = Weights(
        query_weight, key_weight, value_weight, as_row(query_bias), as_row(value_bias), out_weight
    )
    seg = fetch(segment_ids)
    cols = [pltpu.VMEM((length, PAIR), F32)]
    pair_outs = [shape((3, length, PAIR), BF16), shape((PAIR, length), BF16), shape((TINY, 2 * length))]

    qkv_b, mixed_b, lse_b, branch_b = chain.call(
        forward_other_kernel, "forward_other", [core, row_fill],
        [row_of(tokens, True), weights.triple(0), weights.bias(), seg, weights.triple(1), weights.out(0, 2)],
        [shape((2,) + o.shape, o.dtype) for o in pair_outs] + [shape((length, d))], cols, leaves=True,
    )
    branch_came = across(branch_b)
    qkv_0, mixed_0, lse_0 = chain.call(
        partial(forward_own_kernel, 0), "forward_own_0", [core, row_fill],
        [row_of(tokens, False), weights.triple(0), weights.bias(), seg], pair_outs, cols, leaves=True,
    )
    qkv_1, mixed_1, lse_1, mid_a = chain.call(
        partial(forward_own_kernel, 1), "forward_own_1", [core, row_fill, a_gate],
        [row_of(tokens, False), weights.triple(1), weights.bias(), seg, weights.out(0, 2), fetch(mixed_0),
         fetch(branch_came), fetch(as_row(out_bias))],
        pair_outs + [shape((length, d))], cols, leaves=True,
    )
    mid_b = across(mid_a)

    feed_weights = (cotangent, inner_weight, outer_weight, as_row(inner_bias))
    ob = as_row(outer_bias)
    outer_a, inner_a, bias_a0, hidden_a, pre_a = feed(
        chain, "feed_own_0", 0, False, core, f_gate, mid_a, False, *feed_weights
    )
    keep, send, bias_b0, hidden_b, pre_b = feed(
        chain, "feed_other_0", 0, True, core, f_gate, mid_b, True, *feed_weights, bit=bits[0],
        grads=(outer_a, inner_a),
    )
    first = Stream(chain, members, send, bits)
    first.keep(keep)
    outer_b, inner_b, bias_b1, dmid_b, ffn_b = feed(
        chain, "feed_other_1", 1, False, core, f_gate, mid_b, True, *feed_weights, held=(hidden_b, pre_b, ob),
    )
    dmid_a_came = across(dmid_b)
    keep, send, bias_a1, dmid_a, ffn_a = feed(
        chain, "feed_own_1", 1, True, core, f_gate, mid_a, False, *feed_weights, bit=bits[0],
        held=(hidden_a, pre_a, ob), grads=(outer_b, inner_b),
    )
    dmid_b_came = across(dmid_a)
    second = Stream(chain, members, send, bits)
    second.keep(keep)
    first.advance(True, 30.0)

    g_own, total_a, small = chain.call(
        backward_own_kernel, "backward_own", [core, row_fill, a_gate],
        [fetch(dmid_a), fetch(dmid_a_came), row_of(cotangent, False), weights.out(0, 2), seg,
         fetch(qkv_0), fetch(lse_0), row_of(tokens, False), fetch(mixed_0), fetch(qkv_1), fetch(lse_1), fetch(mixed_1),
         weights.triple(0), weights.triple(1), fetch(mid_a),
         fetch(bias_a0), fetch(bias_b0), fetch(bias_a1), fetch(bias_b1)],
        [shape((2, d, d)), shape((length, d)), shape((TINY, d))], attention_scratch(length), leaves=True,
    )
    total_a_came = across(total_a)
    second.advance(True)
    first.advance(True)

    def chosen(array, dims):
        return fetch(array, lambda c, f, g, pair: pair[0], dims)

    def pair_of(core, fill, gate, pair):
        return pair[0]

    def pair_before(core, fill, gate, pair):
        return 1 - pair[0]

    def of_pair(small):
        return [
            weights.out(pair_of), seg, chosen(qkv_b, (3, length, PAIR)), chosen(lse_b, (TINY, 2 * length)),
            row_of(tokens, True), chosen(mixed_b, (PAIR, length)), chosen(g_own, (d, d)), fetch(small),
        ]

    send, small, dbranch, all3 = chain.call(
        partial(backward_other_kernel, False), "backward_other_0", [core, row_fill, a_gate, not_mine],
        [fetch(dmid_b), fetch(dmid_b_came), row_of(cotangent, True), *of_pair(small), fetch(mid_b)],
        [shape((d, d)), shape((TINY, d)), shape((length, d), BF16), shape((length, 3 * PAIR), BF16)],
        attention_scratch(length), leaves=True,
    )
    third = Stream(chain, members, send, bits)
    ffn_came_a = across(ffn_b)
    ffn_came_b = across(ffn_a)
    second.advance(True)
    first.advance(True)
    keep, small, total_b = chain.call(
        partial(backward_other_kernel, True), "backward_other_1", [core, row_fill, a_gate, bits[0]],
        [fetch(dbranch), *of_pair(small), weights.triple(pair_of), fetch(all3), weights.triple(pair_before)],
        [shape((d, d)), shape((TINY, d)), shape((length, d))], attention_scratch(length), leaves=True,
    )
    third.keep(keep, small)
    total_b_came = across(total_b)
    first.advance()
    second.advance()
    (output,) = chain.call(
        output_kernel, "output", [core, f_gate],
        [fetch(mid_a), fetch(ffn_a), fetch(ffn_came_a), fetch(ob), fetch(mid_b), fetch(ffn_b), fetch(ffn_came_b)],
        [shape((2, length, d), BF16)], leaves=True,
    )
    third.advance()
    first.advance()
    second.advance()
    (grad_tokens,) = chain.call(
        tokens_kernel, "tokens", [core],
        [fetch(total_a), fetch(total_b_came), fetch(total_b), fetch(total_a_came)],
        [shape((2, length, d))], leaves=True,
    )
    while not (first.done() and second.done() and third.done()):
        third.advance()
        first.advance()
        second.advance()
    inner_grad, outer_grad = final_feed(chain, first, second, d)
    gq, gk, gv, go, tiny = final_attention(chain, third, d)
    return (
        output,
        grad_tokens,
        gq,
        jnp.concatenate([tiny[0, :PAIR], tiny[0, 2 * PAIR : 3 * PAIR]]),
        gk,
        gv,
        jnp.concatenate([tiny[0, PAIR : 2 * PAIR], tiny[0, 3 * PAIR :]]),
        go,
        tiny[3],
        jnp.sum(tiny[5]),
        inner_grad,
        jnp.concatenate([tiny[1], tiny[2]]),
        outer_grad,
        tiny[4],
        jnp.sum(tiny[6]),
    )


def solution(mesh):
    rows = P("dp", None, None)
    col = P(None, "mp")
    cut = P("mp")
    in_specs = (
        rows, P("dp", None), P("dp"), col, cut, col, col, cut, P("mp", None), P(), P(),
        col, cut, P("mp", None), P(), P(), rows,
    )
    out_specs = (
        rows, rows, col, cut, col, col, cut, P("mp", None), P(), P(), col, cut,
        P("mp", None), P(), P(),
    )
    return jax.shard_map(
        partial(shards, mesh.shape["dp"]), mesh=mesh, in_specs=in_specs, out_specs=out_specs,
        check_vma=False,
    )
```

```python
from functools import partial
import math

import jax
import jax.numpy as jnp
from jax import lax
from jax.experimental import pallas as pl
from jax.experimental.pallas import tpu as pltpu
from jax.sharding import PartitionSpec as P

HEAD_DIM = 64
PAIR = 2 * HEAD_DIM
LONGEST = 256
BLOCK = 128
TINY = 8
PARTS = 12
ROWS = 256
MASKED = -1e30
F32 = jnp.float32
BF16 = jnp.bfloat16
GELU_C = math.sqrt(2.0 / math.pi)
GELU_A = 0.044715
BIG_LIMIT = 60 * 1024 * 1024
LIMITS = {"output": 62, "tokens": 62, "final_feed_0": 62, "final_feed_1": 62, "final_attention": 62}
WEIGHTS = {"backward_own": 80.0, "output": 80.0}
SMALL_LIMIT = 8 * 1024 * 1024
SMEM = pl.BlockSpec(memory_space=pltpu.SMEM)
VMEM = pl.BlockSpec(memory_space=pltpu.VMEM)
WHERE_IT_IS = pl.BlockSpec(memory_space=pl.ANY)
HBM = pl.BlockSpec(memory_space=pltpu.HBM)


def dot_nn(a, b):
    return lax.dot_general(a, b, (((1,), (0,)), ((), ())), preferred_element_type=F32)


def dot_nt(a, b):
    return lax.dot_general(a, b, (((1,), (1,)), ((), ())), preferred_element_type=F32)


def dot_tn(a, b):
    return lax.dot_general(a, b, (((0,), (0,)), ((), ())), preferred_element_type=F32)


def shape(dims, dtype=F32):
    return jax.ShapeDtypeStruct(tuple(dims), dtype)


class Take:
    def __init__(self, dims, dtype, copies, held=False):
        self.dims, self.dtype, self.copies, self.held = tuple(dims), dtype, copies, held
        self.late = False


def later(one):
    one.late = True
    return one


def take(array, index=None, dims=None):
    return Take(dims or array.shape, array.dtype, [(array, index, None)], True)


def fetch(array, index=None, dims=None):
    return Take(dims or array.shape, array.dtype, [(array, index, None)])


class Coming:
    def __init__(self, buffer, copies, late=False):
        self.buffer, self.copies, self.waiting = buffer, copies, late
        if not late:
            for copy in copies:
                copy.start()

    def start(self):
        if self.waiting:
            for copy in self.copies:
                copy.start()
        self.waiting = False

    def __call__(self):
        self.start()
        for copy in self.copies:
            copy.wait()
        self.copies = []
        return self.buffer


class Going:
    def __init__(self, target, buffer, sems):
        self.target, self.buffer, self.sems, self.copies = target, buffer, sems, []

    def __setitem__(self, index, value):
        self.buffer[index] = value

    def __getitem__(self, index):
        return self.buffer[index]

    def part(self, *index):
        copy = pltpu.make_async_copy(self.buffer.at[index], self.target.at[index], self.sems[len(self.copies)])
        copy.start()
        self.copies.append(copy)

    def send(self):
        if self.target is not None and not self.copies:
            copy = pltpu.make_async_copy(self.buffer, self.target, self.sems[0])
            copy.start()
            self.copies.append(copy)


def part_swapped(swap, one, two, one_index, two_index):
    straight, crossed = [], []
    for a, b, index in ((one, two, one_index), (two, one, two_index)):
        sem = a.sems[len(a.copies)]
        straight.append(pltpu.make_async_copy(a.buffer.at[index], a.target.at[index], sem))
        crossed.append(pltpu.make_async_copy(a.buffer.at[index], b.target.at[index], sem))

    @pl.when(swap)
    def _():
        for copy in crossed:
            copy.start()

    @pl.when(jnp.logical_not(swap))
    def _():
        for copy in straight:
            copy.start()

    one.copies.append(straight[0])
    two.copies.append(straight[1])


def pick(ref, index, scalars):
    if index is None:
        return ref
    return ref.at[index(*scalars) if callable(index) else index]


class Chain:
    def __init__(self):
        self.last = None

    def call(self, kernel, name, scalars, takes, outs, scratch=(), leaves=False, weight=None, passes=(), onto=()):
        arrays, spaces, spots = [], [], []

        def place(array, space):
            for i, (known, its) in enumerate(zip(arrays, spaces)):
                if known is array and its is space:
                    return i
            arrays.append(array)
            spaces.append(space)
            return len(arrays) - 1

        fetched = [one for one in takes if not one.held]
        views = []
        for one in takes:
            if one.held:
                views.append((place(one.copies[0][0], VMEM), one.copies[0][1]))
            else:
                spots.append([(place(a, HBM), s, t) for a, s, t in one.copies])
        after = [] if self.last is None else [self.last]
        n_scalar, n_array, n_out = len(scalars), len(arrays), len(outs)
        n_copies = sum(len(one) for one in spots)

        def body(*refs):
            numbers, refs = refs[:n_scalar], refs[n_scalar:]
            given, refs = refs[:n_array], refs[n_array + len(after) + len(passes) + len(onto) :]
            results, refs = refs[:n_out], refs[n_out + len(passes) :]
            sems, refs = refs[0], refs[1:]
            into, refs = refs[: len(fetched)], refs[len(fetched) :]
            outof, rest = (refs[:n_out], refs[n_out:]) if leaves else (results, refs)
            at = 0
            buffers = []
            for one, buffer, copies in zip(fetched, into, spots):
                listed = []
                for which, source, target in copies:
                    listed.append(
                        pltpu.make_async_copy(
                            pick(given[which], source, numbers), pick(buffer, target, numbers), sems.at[at]
                        )
                    )
                    at += 1
                buffers.append(Coming(buffer, listed, one.late))
            left, seen, coming = list(buffers), list(views), []
            for one in takes:
                if one.held:
                    which, index = seen.pop(0)
                    coming.append(Coming(pick(given[which], index, numbers), []))
                else:
                    coming.append(left.pop(0))
            going = [
                Going(result if leaves else None, buffer, [sems.at[at + PARTS * i + j] for j in range(PARTS)])
                for i, (result, buffer) in enumerate(zip(results, outof))
            ]
            kernel(*numbers, *coming, *going, *rest)
            for one in coming:
                one()
            for one in going:
                one.send()
            for one in going:
                for copy in one.copies:
                    copy.wait()

        body.__name__ = name
        out = pl.pallas_call(
            body,
            in_specs=[SMEM] * n_scalar + spaces + [WHERE_IT_IS] * len(after) + [HBM] * (len(passes) + len(onto)),
            out_specs=[HBM if leaves else VMEM] * n_out + [HBM] * len(passes),
            out_shape=list(outs) + [shape(one.shape, one.dtype) for one in passes],
            input_output_aliases={
                n_scalar + n_array + len(after) + i: (n_out + i if i < len(passes) else i - len(passes))
                for i in range(len(passes) + len(onto))
            },
            scratch_shapes=[pltpu.SemaphoreType.DMA((n_copies + PARTS * n_out,))]
            + [pltpu.VMEM(one.dims, one.dtype) for one in fetched]
            + [pltpu.VMEM(o.shape, o.dtype) for o in outs if leaves]
            + list(scratch),
            compiler_params=pltpu.CompilerParams(vmem_limit_bytes=LIMITS.get(name, BIG_LIMIT >> 20) << 20 if leaves else SMALL_LIMIT),
            cost_estimate=pl.CostEstimate(flops=int(1e9 * (WEIGHTS.get(name, 17.0 if leaves else 0.0) if weight is None else weight)) + 1000, bytes_accessed=1000, transcendentals=0),
            name=name,
        )(*scalars, *arrays, *after, *passes, *onto)
        self.last = out[0]
        return out


def window(first, length):
    return max(0, first - LONGEST), min(length, first + BLOCK + LONGEST)


class Weights:
    def __init__(self, wq, wk, wv, bq, bv, wo):
        self.projections, self.biases, self.wo = (wq, wk, wv), (bq, bv), wo

    def cut(self, p, n=1):
        if callable(p):
            return lambda *numbers: pl.ds(pl.multiple_of(p(*numbers) * PAIR, PAIR), n * PAIR)
        return lambda *numbers: slice(p * PAIR, (p + n) * PAIR)

    def triple(self, p):
        d = self.wo.shape[1]
        cut = self.cut(p)
        return Take(
            (d, 3 * PAIR), BF16,
            [
                (a, lambda *n: (slice(None), cut(*n)), (slice(None), slice(i * PAIR, (i + 1) * PAIR)))
                for i, a in enumerate(self.projections)
            ],
        )

    def out(self, p, n=1):
        d = self.wo.shape[1]
        cut = self.cut(p, n)
        return Take((n * PAIR, d), BF16, [(self.wo, lambda *k: (cut(*k), slice(None)), None)])

    def bias(self):
        bq, bv = self.biases
        half = bq.shape[1]
        return Take(
            (1, 2 * half), F32,
            [(bq, None, (slice(None), slice(0, half))), (bv, None, (slice(None), slice(half, 2 * half)))],
        )


def row_index(other):
    return lambda core, *_: 1 - core[0] if other else core[0]


def row_of(array, other):
    return Take(array.shape[1:], array.dtype, [(array, row_index(other), None)])


def segments_of(place, fill_ref, seg, cols_ref):
    length = cols_ref.shape[0]
    fill = fill_ref[place]
    row = seg()[pl.ds(place, 1), :].astype(F32)
    places = lax.broadcasted_iota(jnp.int32, (1, length), 1)
    valid = places < fill
    keyed = jnp.where(valid, row, -1.0)
    cols_ref[...] = jnp.broadcast_to(keyed, (PAIR, length)).T
    return row, jnp.where(valid, 1.0, 0.0)


def mask_for(cols_ref, row, low, high, first):
    once = cols_ref[low:high, :] == row[:, first : first + BLOCK]
    return jnp.concatenate([once, once], axis=1)


def two_heads(array):
    lanes = lax.broadcasted_iota(jnp.int32, array.shape, 1)
    return jnp.where(lanes < HEAD_DIM, array, 0), jnp.where(lanes < HEAD_DIM, 0, array)


def stacked(pair, first):
    return jnp.concatenate([half[first : first + BLOCK] for half in pair], axis=0)


def forward_pair(p, x, w3, bias, row, valid, cols, qkv, mixed_out, lse):
    length = x.shape[0]
    half = bias.shape[1] // 2
    y = dot_nn(x, w3)
    at = p * PAIR
    q = y[:, :PAIR] + bias[0:1, at : at + PAIR]
    q = (q.astype(BF16) * 0.125).astype(BF16)
    k = y[:, PAIR : 2 * PAIR].astype(BF16)
    v = (y[:, 2 * PAIR :] + bias[0:1, half + at : half + at + PAIR]).astype(BF16)
    vt = v.T
    qkv[0] = q
    qkv[1] = k
    qkv[2] = v
    heads = two_heads(q)
    for first in range(0, length, BLOCK):
        low, high = window(first, length)
        block = slice(first, first + BLOCK)
        s = dot_nt(k[low:high], stacked(heads, first))
        s = jnp.where(mask_for(cols, row, low, high, first), s, MASKED)
        peak = jnp.max(s, axis=0, keepdims=True)
        e = jnp.exp(s - peak)
        total = jnp.sum(e, axis=0, keepdims=True)
        o = dot_nn(vt[:, low:high], e.astype(BF16))
        keep = valid[:, block]
        o0 = o[:HEAD_DIM, :BLOCK] * (keep / total[:, :BLOCK])
        o1 = o[HEAD_DIM:, BLOCK:] * (keep / total[:, BLOCK:])
        mixed_out[:HEAD_DIM, block] = o0.astype(BF16)
        mixed_out[HEAD_DIM:, block] = o1.astype(BF16)
        lse[0:1, 2 * first : 2 * first + 2 * BLOCK] = peak + jnp.log(total)


def start_all(*ones):
    for one in ones:
        one.start()


def forward_other_kernel(core_ref, fill_ref, seg, x_in, w3_0, bias, w3_1, wo, qkv, mixed, lse, branch_out, cols):
    row, valid = segments_of(1 - core_ref[0], fill_ref, seg, cols)
    x = x_in()[...]
    w3_0()
    start_all(w3_1, wo)
    for p, w3 in enumerate((w3_0, w3_1)):
        forward_pair(
            p, x, w3()[...], bias(), row, valid, cols, qkv.buffer.at[p], mixed.buffer.at[p], lse.buffer.at[p]
        )
        qkv.part(p)
        mixed.part(p)
        lse.part(p)
    for at in range(0, x.shape[0], ROWS):
        rows = slice(at, at + ROWS)
        branch_out[rows, :] = dot_tn(mixed[0, :, rows], wo()[:PAIR, :]) + dot_tn(mixed[1, :, rows], wo()[PAIR:, :])
        branch_out.part(rows)


def forward_own_kernel(p, core_ref, fill_ref, *refs):
    if p:
        gate, refs = refs[0], refs[1:]
    seg, x_in, w3, bias, *refs = refs
    if p:
        wo, mixed_0, came, out_bias, qkv, mixed, lse, middle, low, cols = refs
    else:
        qkv, mixed, lse, cols = refs
    row, valid = segments_of(core_ref[0], fill_ref, seg, cols)
    x = x_in()[...]
    w3()
    if p:
        start_all(wo, mixed_0, came, out_bias)
    forward_pair(p, x, w3()[...], bias(), row, valid, cols, qkv.buffer, mixed.buffer, lse.buffer)
    qkv.send()
    mixed.send()
    lse.send()
    if p:
        for at in range(0, x.shape[0], ROWS):
            rows = slice(at, at + ROWS)
            branch = dot_tn(mixed_0()[:, rows], wo()[:PAIR, :]) + dot_tn(mixed[:, rows], wo()[PAIR:, :])
            branch = (branch + came()[rows, :]) + out_bias()[...]
            value = x[rows].astype(F32) + gate[0] * branch
            middle[rows, :] = value
            middle.part(rows)
            low[rows, :] = value.astype(BF16)
            low.part(rows)


def feed_kernel(second, adds, rounds, core_ref, gate, *refs):
    if adds:
        bit, refs = refs[0], refs[1:]
    mid_in, wi_in, bias_in, cot_in, wo_in, *refs = refs
    extra = []
    if adds:
        outer_in, inner_in, *refs = refs
        extra += [outer_in, inner_in]
    if second:
        hidden_0, pre_0, wi_0, wo_0, out_bias, full_in, x_in, *refs = refs
        extra += [hidden_0, pre_0, wi_0, wo_0, out_bias, full_in, x_in]
        grad_a, grad_b, bias_out, dmid_out, hidden_out, pre_out = refs
    else:
        grad_a, grad_b, bias_out, hidden_out, pre_out, *refs = refs
    low = mid_in()[...].astype(BF16)
    wi_in()
    start_all(cot_in, wo_in)
    length, d = low.shape
    units = wi_in.buffer.shape[1]
    lowt = low.T
    if rounds:
        refs[0][...] = low
        refs[0].send()
    step = 256
    d_ffn = None
    for at in range(0, units, step):
        cut = slice(at, at + step)
        wi = wi_in()[:, cut]
        pre = dot_nn(low, wi) + bias_in()[0:1, cut]
        square = pre * pre
        t = jnp.tanh(pre * (GELU_C + (GELU_C * GELU_A) * square))
        cdf = 0.5 + 0.5 * t
        hidden = (pre * cdf).astype(BF16)
        slope = cdf + (0.5 * pre) * (1.0 - t * t) * (GELU_C + (3.0 * GELU_C * GELU_A) * square)
        if d_ffn is None:
            cot = cot_in()[...].astype(F32)
            d_ffn = (gate[0] * cot).astype(BF16)
            wo_in()
            start_all(*extra)
        wo = wo_in()[cut, :]
        d_pre = dot_nt(d_ffn, wo) * slope
        low_d = d_pre.astype(BF16)
        bias_out[0:1, cut] = jnp.sum(low_d.astype(F32), axis=0, keepdims=True)
        outer = dot_tn(hidden, d_ffn)
        inner = dot_nn(lowt, low_d)
        if adds:
            outer = outer + outer_in()[cut, :]
            inner = inner + inner_in()[:, cut]
        grad_a[cut, :] = outer
        grad_b[:, cut] = inner
        all_rows = (cut, slice(None)), (slice(None), cut)
        if adds:
            part_swapped(bit[0] != 0, grad_a, grad_b, *all_rows)
        else:
            grad_a.part(*all_rows[0])
            grad_b.part(*all_rows[1])
        hidden_out[:, cut] = hidden
        pre_out[:, cut] = low_d
        if not second:
            hidden_out.part(*all_rows[1])
            pre_out.part(*all_rows[1])
    bias_out[1:, :] = jnp.zeros((TINY - 1, units), F32)
    if second:
        bias_out[1:2, :] = jnp.sum(d_ffn.astype(F32), axis=0, keepdims=True)
        bias_out.send()
        gates = [jnp.zeros((1, d), F32), jnp.zeros((1, d), F32)]
        for at in range(0, length, ROWS):
            rows = slice(at, at + ROWS)
            dmid = dot_nt(pre_0()[rows, :], wi_0()[...]) + dot_nt(pre_out[rows, :], wi_in()[...])
            ffn = dot_nn(hidden_0()[rows, :], wo_0()[...]) + dot_nn(hidden_out[rows, :], wo_in()[...])
            below = slice(length + TINY + at, length + TINY + at + ROWS)
            dmid_out[below, :] = ffn
            dmid_out.part(below)
            seen = cot_in()[rows, :].astype(F32)
            if adds:
                ffn = ffn + out_bias()[...]
                dmid = dmid + seen
            dmid_out[rows, :] = dmid
            dmid_out.part(rows)
            gates[0] += jnp.sum(seen * ffn, axis=0, keepdims=True)
            branch = full_in()[rows, :] - x_in()[rows, :].astype(F32)
            gates[1] += jnp.sum(dmid * branch, axis=0, keepdims=True)
        dmid_out[length : length + TINY, :] = jnp.zeros((TINY, d), F32)
        for i, value in enumerate(gates):
            dmid_out[length + i : length + i + 1, :] = value
        dmid_out.part(slice(length, length + TINY))


def feed(chain, name, second, adds, rounds, core, gate, middle, other, cotangent, wi, wo, bi, bit=None, held=(), grads=()):
    length, d = middle.shape
    units = wi.shape[1] // 2
    halves = [slice(0, units), slice(units, 2 * units)]
    cut = halves[second]
    takes = [
        fetch(middle), fetch(wi, (slice(None), cut), (d, units)), fetch(bi, (slice(None), cut), (1, units)),
        later(row_of(cotangent, other)), later(fetch(wo, (cut, slice(None)), (units, d))),
    ]
    takes += [later(fetch(g)) for g in grads]
    scratch = []
    outs = [shape((units, d)), shape((d, units)), shape((TINY, units))]
    if second:
        hidden, pre, out_bias, full, tokens = held
        takes += [
            later(one)
            for one in (
                fetch(hidden), fetch(pre), fetch(wi, (slice(None), halves[0]), (d, units)),
                fetch(wo, (halves[0], slice(None)), (units, d)), fetch(out_bias), fetch(full), row_of(tokens, other),
            )
        ]
        outs.append(shape((2 * length + TINY, d)))
        scratch = [pltpu.VMEM((length, units), BF16)] * 2
    else:
        outs += [shape((length, units), BF16)] * 2
        if rounds:
            outs.append(shape((length, d), BF16))
    return chain.call(
        partial(feed_kernel, bool(second), adds, rounds), name, [core, gate] + ([bit] if adds else []), takes, outs,
        scratch, leaves=True,
    )


def backward_pair(dbranch, do, qkv, lse, mixed, x, row, cols, dk_acc, dv_acc, dqt, grad_out):
    length, d = dbranch.shape
    q, k, v = qkv[0], qkv[1], qkv[2]
    kt = k.T
    qs = two_heads(q)
    dos = two_heads(do)
    dk_acc[...] = jnp.zeros_like(dk_acc)
    dv_acc[...] = jnp.zeros_like(dv_acc)
    for first in range(0, length, BLOCK):
        low, high = window(first, length)
        block = slice(first, first + BLOCK)
        qq = stacked(qs, first)
        dd = stacked(dos, first)
        s = dot_nt(k[low:high], qq)
        s = jnp.where(mask_for(cols, row, low, high, first), s, MASKED)
        w = jnp.exp(s - lse[0:1, 2 * first : 2 * first + 2 * BLOCK])
        dw = dot_nt(v[low:high], dd)
        both = w * dw
        mean = jnp.sum(both, axis=0, keepdims=True)
        ds = (both - w * mean).astype(BF16)
        dv_acc[low:high, :] += dot_nn(w.astype(BF16), dd)
        dk_acc[low:high, :] += dot_nn(ds, qq)
        dq = dot_nn(kt[:, low:high], ds)
        dqt[:HEAD_DIM, block] = dq[:HEAD_DIM, :BLOCK]
        dqt[HEAD_DIM:, block] = dq[HEAD_DIM:, BLOCK:]
    dq = (0.125 * dqt[...]).T.astype(BF16)
    all3 = jnp.concatenate([dq, dk_acc[...].astype(BF16), dv_acc[...].astype(BF16)], axis=1)
    grad_out[:, : 3 * PAIR] = dot_tn(x, all3)
    out_grad = dot_nn(mixed, dbranch)
    for c in range(d // PAIR):
        cut = slice(c * PAIR, (c + 1) * PAIR)
        grad_out[cut, 3 * PAIR :] = out_grad[:, cut]
    return all3


def bias_sums(all3):
    sums = jnp.sum(all3.astype(F32), axis=0, keepdims=True)
    return jnp.concatenate([sums[:, :PAIR], sums[:, 2 * PAIR :]], axis=1)


def masked_heads(dbranch, wo, fill):
    places = lax.broadcasted_iota(jnp.int32, (dbranch.shape[0], 1), 0)
    return jnp.where(places < fill, dot_nt(dbranch, wo), 0.0).astype(BF16)


def branch_gradient(gate, mine, came, length):
    dmid = mine()[:length, :] + came()[:length, :]
    return dmid, (gate[0] * dmid).astype(BF16)


def gate_sums(gate, mine, came, length):
    both = mine()[length:, :] + came()[length:, :]
    return both[1:2, :] / gate[0], both[0:1, :]


def backward_own_kernel(core_ref, fill_ref, gate, seg, mine, came, wo, qkv_0, lse_0, x_in, mixed_0, qkv_1, lse_1,
                        mixed_1, w3_0, w3_1, bias_a0, bias_b0, bias_a1, bias_b1,
                        grad_out, total_out, small_out, cols, dk_acc, dv_acc, dqt):
    length = cols.shape[0]
    row, _ = segments_of(core_ref[0], fill_ref, seg, cols)
    fill = fill_ref[core_ref[0]]
    dmid, dbranch = branch_gradient(gate, mine, came, length)
    start_all(qkv_0, lse_0, x_in, mixed_0)
    total_out[...] = dmid
    do = masked_heads(dbranch, wo()[...], fill)
    qkv_0()
    x = x_in()[...]
    start_all(qkv_1, lse_1, mixed_1, w3_0, w3_1, bias_a0, bias_b0, bias_a1, bias_b1)
    first = backward_pair(
        dbranch, do[:, :PAIR], qkv_0(), lse_0(), mixed_0()[...], x, row, cols, dk_acc, dv_acc, dqt, grad_out.buffer.at[0]
    )
    grad_out.part(0)
    second = backward_pair(
        dbranch, do[:, PAIR:], qkv_1(), lse_1(), mixed_1()[...], x, row, cols, dk_acc, dv_acc, dqt, grad_out.buffer.at[1]
    )
    grad_out.part(1)
    for at in range(0, length, ROWS):
        rows = slice(at, at + ROWS)
        total_out[rows, :] += dot_nt(first[rows], w3_0()[...]) + dot_nt(second[rows], w3_1()[...])
        total_out.part(rows)
    small_out[...] = jnp.zeros(small_out.buffer.shape, F32)
    small_out[0:1, :] = jnp.concatenate([bias_sums(first), bias_sums(second)], axis=1)
    small_out[1:2, :] = bias_a0()[0:1, :] + bias_b0()[0:1, :]
    small_out[2:3, :] = bias_a1()[0:1, :] + bias_b1()[0:1, :]
    small_out[4:5, :] = bias_a1()[1:2, :] + bias_b1()[1:2, :]
    small_out[3:4, :] = jnp.sum(dbranch.astype(F32), axis=0, keepdims=True)
    five, six = gate_sums(gate, mine, came, length)
    small_out[5:6, :] = five
    small_out[6:7, :] = six


def backward_other_kernel(last, core_ref, fill_ref, gate, pair, *refs):
    seg, *refs = refs
    if last:
        dbranch_in, *refs = refs
    else:
        mine, came, *refs = refs
    wo, qkv, lse, x_in, mixed, grad_in, small_in, *refs = refs
    if last:
        w3, all3_in, w3_before, *refs = refs
        grad_out, small_out, total_out, cols, dk_acc, dv_acc, dqt = refs
    else:
        grad_out, small_out, dbranch_out, all3_out, cols, dk_acc, dv_acc, dqt = refs
    length = cols.shape[0]
    place = 1 - core_ref[0]
    row, _ = segments_of(place, fill_ref, seg, cols)
    if last:
        dbranch = dbranch_in()[...]
    else:
        dmid, dbranch = branch_gradient(gate, mine, came, length)
    start_all(qkv, lse, x_in, mixed)
    if not last:
        dbranch_out[...] = dbranch
        dbranch_out.send()
    do = masked_heads(dbranch, wo()[...], fill_ref[place])
    qkv()
    x = x_in()[...]
    start_all(grad_in, small_in)
    if last:
        start_all(w3, all3_in, w3_before)
    all3 = backward_pair(
        dbranch, do, qkv(), lse(), mixed()[...], x, row, cols, dk_acc, dv_acc, dqt, grad_out.buffer
    )
    grad_out[...] += grad_in()[...]
    grad_out.send()
    small_out[...] = small_in()[...]
    spot = pl.ds(pl.multiple_of(pair[0] * 2 * PAIR, PAIR), 2 * PAIR)
    small_out[0:1, spot] += bias_sums(all3)
    if last:
        for at in range(0, length, ROWS):
            rows = slice(at, at + ROWS)
            total_out[rows, :] = dot_nt(all3_in()[rows, :], w3_before()[...]) + dot_nt(all3[rows], w3()[...])
            total_out.part(rows)
    else:
        all3_out[...] = all3
        five, six = gate_sums(gate, mine, came, length)
        small_out[3:4, :] += jnp.sum(dbranch.astype(F32), axis=0, keepdims=True)
        small_out[5:6, :] += five
        small_out[6:7, :] += six


def attention_scratch(length):
    return [pltpu.VMEM((length, PAIR), F32)] * 3 + [pltpu.VMEM((PAIR, length), F32)]


def place_in(refs, mask):
    at = 0
    for ref in refs:
        at = 2 * at + ref[0]
    return jnp.bitwise_xor(at, mask)


def sum_of(terms, cut):
    total = terms[0]()[cut, :]
    for one in terms[1:]:
        total = total + one()[cut, :]
    return total


class Stream:
    def __init__(self, chain, members, bits, send, out, back):
        self.chain, self.members, self.bits = chain, members, bits
        self.out, self.back = list(out), list(back)
        self.group = [0]
        self.came = [self.travel(send, 1)]
        self.tail, self.small, self.turned, self.lanes = 0, None, False, 1

    def keep(self, mine, small=None):
        self.mine, self.small = mine, small
        self.rows, self.width = mine.shape
        self.joined = []

    def join(self, other):
        self.joined = [other]

    def travel(self, array, mask):
        pairs = []
        for place in range(self.members):
            for core in range(2):
                partner = place
                for i, step in enumerate(reversed(self.group)):
                    if mask >> i & 1:
                        partner ^= 1 << (step ^ core if step < 2 else step)
                pairs.append((place * 2 + core, partner * 2 + core))
        return lax.ppermute(array, ("dp", "mp"), pairs)

    def call(self, kernel, name, group, outs, small=False):
        takes = [take(one) for stream in (self, *self.joined) for one in (stream.mine, *stream.came)]
        takes += [take(self.small)] if small else []
        results = self.chain.call(
            kernel, name, [self.bits[step] for step in group], takes, [shape(dims) for dims in outs],
            weight=self.weight, passes=self.passes,
        )
        self.passes = results[len(outs) :]
        return results[: len(outs)]

    def halve(self):
        group = self.out.pop(0)
        parts, n_terms = 1 << len(group), 1 + len(self.came)
        whole, tail = self.rows, self.tail
        rows = whole // parts
        begins = self.small is not None and not tail
        sources = 1 + len(self.joined)
        lanes = self.lanes = max(self.lanes, sources)

        def kernel(*refs):
            bits, refs = refs[: len(group)], refs[len(group) :]
            terms = [refs[i * n_terms : (i + 1) * n_terms] for i in range(sources)]
            refs = refs[sources * n_terms :]
            if begins:
                both = refs[0]()[...]
                refs = refs[1:]
            elif tail:
                both = sum_of(terms[0], slice(lanes * whole, lanes * whole + tail))
            for mask, out in enumerate(refs):
                at = place_in(bits, mask) * rows
                for lane in range(lanes):
                    source, base = (lane, 0) if sources > 1 else (0, lane * whole)
                    cut = pl.ds(pl.multiple_of(base + at, 8), rows)
                    out[lane * rows : (lane + 1) * rows, :] = sum_of(terms[source], cut)
                if begins or tail:
                    out[lanes * rows :, :] = both

        if begins:
            self.tail = TINY
        self.mine, *sends = self.call(
            kernel, "halve", group, [(lanes * rows + self.tail, self.width)] * parts, begins
        )
        self.joined = []
        self.group = group
        self.came = [self.travel(send, mask + 1) for mask, send in enumerate(sends)]
        self.rows = rows

    def turn(self):
        rows, tail = self.lanes * self.rows, self.tail
        n_came = len(self.came)

        def kernel(mine, *refs):
            came, refs = refs[:n_came], refs[n_came:]
            total = mine()[...]
            for one in came:
                total = total + one()[...]
            refs[0][...] = total[:rows]
            if tail:
                refs[1][...] = total[rows:]

        outs = [(rows, self.width)] + ([(TINY, self.width)] if tail else [])
        self.mine, *tiny = self.call(kernel, "turn", [], outs)
        self.small = tiny[0] if tiny else None
        self.turned = True
        self.spread()

    def double(self):
        rows, lanes = self.rows, self.lanes
        parts = len(self.came) + 1
        ends = len(self.back) == 1 and self.small is not None
        group = self.group

        def kernel(*refs):
            bits, refs = refs[: len(group)], refs[len(group) :]
            have, refs = refs[:parts], refs[parts:]
            out = refs[-1]
            if ends:
                out[lanes * parts * rows :, :] = refs[0]()[...]
            for mask, one in enumerate(have):
                at = place_in(bits, mask) * rows
                for lane in range(lanes):
                    cut = pl.ds(pl.multiple_of(lane * parts * rows + at, 8), rows)
                    out[cut, :] = one()[lane * rows : (lane + 1) * rows, :]

        self.rows = parts * rows
        (self.mine,) = self.call(
            kernel, "double", group, [(lanes * self.rows + (TINY if ends else 0), self.width)], ends
        )
        self.spread()

    def spread(self):
        self.group = self.back.pop(0)
        self.came = [self.travel(self.mine, mask) for mask in range(1, 1 << len(self.group))]

    def advance(self, weight=0.0, passes=()):
        self.weight, self.passes = weight, passes
        if self.out:
            self.halve()
        elif not self.turned:
            self.turn()
        elif self.back:
            self.double()
        return self.passes

    def done(self):
        return self.turned and not self.back


def in_order(bit, mine, came, low, high):
    @pl.when(bit[0] == 0)
    def _():
        low(mine())
        high(came())

    @pl.when(bit[0] != 0)
    def _():
        low(came())
        high(mine())


def final_feed(chain, stream, index, d, onto=()):
    units = stream.rows
    cut = slice(index * units, (index + 1) * units)

    def kernel(bit, mine, came, inner, outer):
        mine()
        came()

        def low(ref):
            outer[cut, :] = ref[...]

        def high(ref):
            inner[:, cut] = ref[...]

        in_order(bit, mine, came, low, high)
        outer.part(cut)
        inner.part(slice(None), cut)

    return chain.call(
        kernel, "final_feed_%d" % index, [stream.bits[0]], [fetch(stream.mine), fetch(stream.came[0])],
        [shape((d, 2 * units)), shape((2 * units, d))], leaves=True, onto=onto,
    )


def final_attention(chain, third, d):
    half = d // 2

    def kernel(bit, mine, came, gq, gk, gv, go, gqb, gvb, gob, gib, goutb, gates):
        small = mine()[d:, :] + came()[d:, :]
        for p in range(2):
            cut = slice(p * PAIR, (p + 1) * PAIR)
            gqb[:, cut] = small[0:1, 2 * p * PAIR : (2 * p + 1) * PAIR]
            gvb[:, cut] = small[0:1, (2 * p + 1) * PAIR : (2 * p + 2) * PAIR]
        gib[:, :d] = small[1:2, :]
        gib[:, d:] = small[2:3, :]
        gob[...] = small[3:4, :]
        goutb[...] = small[4:5, :]
        gates[...] = jnp.broadcast_to(jnp.sum(small, axis=1, keepdims=True), gates.buffer.shape)

        def place(p, ref):
            cut = slice(p * PAIR, (p + 1) * PAIR)
            gq[:, cut] = ref[:d, :PAIR]
            gk[:, cut] = ref[:d, PAIR : 2 * PAIR]
            gv[:, cut] = ref[:d, 2 * PAIR : 3 * PAIR]
            for c in range(d // PAIR):
                across = slice(c * PAIR, (c + 1) * PAIR)
                go[cut, across] = ref[across, 3 * PAIR :]

        in_order(bit, mine, came, partial(place, 0), partial(place, 1))

    return chain.call(
        kernel, "final_attention", [third.bits[0]], [take(third.mine), take(third.came[0])],
        [shape((d, half))] * 3
        + [shape((half, d)), shape((1, half)), shape((1, half)), shape((1, d)), shape((1, 2 * d)), shape((1, d)), shape((TINY, PAIR))],
        leaves=True,
    )


def output_kernel(core_ref, gate, mid_own, ffn_own, came_own, out_bias, mid_other, ffn_other, came_other, out):
    def row(mid, ffn, came):
        return (mid()[...] + gate[0] * ((ffn()[...] + came()[...]) + out_bias()[...])).astype(BF16)

    out[core_ref[0]] = row(mid_own, ffn_own, came_own)
    out[1 - core_ref[0]] = row(mid_other, ffn_other, came_other)


def tokens_kernel(core_ref, own, came_own, other, came_other, out):
    out[core_ref[0]] = own()[...] + came_own()[...]
    out[1 - core_ref[0]] = other()[...] + came_other()[...]


def shards(members, tokens, segment_ids, row_fill, query_weight, query_bias, key_weight,
           value_weight, value_bias, out_weight, out_bias, attention_gate, inner_weight,
           inner_bias, outer_weight, outer_bias, feed_gate, cotangent):
    _, length, d = tokens.shape
    half = d // 2
    place = lax.axis_index("dp")
    core_id = lax.axis_index("mp")
    core = core_id.astype(jnp.int32).reshape(1)
    bits, others = [], []
    for step in range(members.bit_length() - 1):
        bit = (place >> (step ^ core_id if step < 2 else step)) & 1
        bits.append(bit.astype(jnp.int32).reshape(1))
    not_mine = 1 - bits[0]
    chain = Chain()

    def across(array):
        return lax.ppermute(array, "mp", [(0, 1), (1, 0)])

    def as_row(array):
        return array.reshape(1, -1)

    a_gate = attention_gate.reshape(1)
    f_gate = feed_gate.reshape(1)
    weights = Weights(
        query_weight, key_weight, value_weight, as_row(query_bias), as_row(value_bias), out_weight
    )
    seg = fetch(segment_ids)
    cols = [pltpu.VMEM((length, PAIR), F32)]
    pair_outs = [shape((3, length, PAIR), BF16), shape((PAIR, length), BF16), shape((TINY, 2 * length))]

    qkv_b, mixed_b, lse_b, branch_b = chain.call(
        forward_other_kernel, "forward_other", [core, row_fill],
        [seg, row_of(tokens, True), weights.triple(0), weights.bias(), later(weights.triple(1)), later(weights.out(0, 2))],
        [shape((2,) + o.shape, o.dtype) for o in pair_outs] + [shape((length, d))], cols, leaves=True,
    )
    branch_came = across(branch_b)
    qkv_0, mixed_0, lse_0 = chain.call(
        partial(forward_own_kernel, 0), "forward_own_0", [core, row_fill],
        [seg, row_of(tokens, False), weights.triple(0), weights.bias()], pair_outs, cols, leaves=True,
    )
    qkv_1, mixed_1, lse_1, mid_a, low_a = chain.call(
        partial(forward_own_kernel, 1), "forward_own_1", [core, row_fill, a_gate],
        [seg, row_of(tokens, False), weights.triple(1), weights.bias(), later(weights.out(0, 2)), later(fetch(mixed_0)),
         later(fetch(branch_came)), later(fetch(as_row(out_bias)))],
        pair_outs + [shape((length, d)), shape((length, d), BF16)], cols, leaves=True,
    )
    mid_b = across(mid_a)

    feed_weights = (cotangent, inner_weight, outer_weight, as_row(inner_bias))
    ob = as_row(outer_bias)
    outer_a, inner_a, bias_a0, hidden_a, pre_a = feed(
        chain, "feed_own_0", 0, False, False, core, f_gate, low_a, False, *feed_weights
    )
    keep, send, bias_b0, hidden_b, pre_b, low_b = feed(
        chain, "feed_other_0", 0, True, True, core, f_gate, mid_b, True, *feed_weights, bit=bits[0],
        grads=(outer_a, inner_a),
    )
    wide = [[step for step in pair if step < len(bits)] for pair in ((i, i + 1) for i in range(2, len(bits), 2))]
    out, back = [[1], *wide], [*wide[::-1], [1], [0]]
    first = Stream(chain, members, bits, send, out, back)
    first.keep(keep)
    outer_b, inner_b, bias_b1, dmid_b = feed(
        chain, "feed_other_1", 1, False, False, core, f_gate, low_b, True, *feed_weights,
        held=(hidden_b, pre_b, ob, mid_b, tokens),
    )
    dmid_a_came = across(dmid_b)

    def upper(array):
        return fetch(array, (slice(0, length + TINY), slice(None)), (length + TINY, d))

    def lower(array):
        return fetch(array, (slice(length + TINY, 2 * length + TINY), slice(None)), (length, d))

    first.advance()
    keep, send, bias_a1, dmid_a = feed(
        chain, "feed_own_1", 1, True, False, core, f_gate, low_a, False, *feed_weights, bit=bits[0],
        held=(hidden_a, pre_a, ob, mid_a, tokens), grads=(outer_b, inner_b),
    )
    dmid_b_came = across(dmid_a)
    second = Stream(chain, members, bits, send, out, [[step] for step in reversed(range(len(bits)))])
    second.keep(keep)
    first.advance(80.0)

    g_own, total_a, small = chain.call(
        backward_own_kernel, "backward_own", [core, row_fill, a_gate],
        [seg, upper(dmid_a), upper(dmid_a_came), weights.out(0, 2)]
        + [
            later(one)
            for one in (
                fetch(qkv_0), fetch(lse_0), row_of(tokens, False), fetch(mixed_0), fetch(qkv_1), fetch(lse_1),
                fetch(mixed_1), weights.triple(0), weights.triple(1),
                fetch(bias_a0), fetch(bias_b0), fetch(bias_a1), fetch(bias_b1),
            )
        ],
        [shape((2, d, d)), shape((length, d)), shape((TINY, d))], attention_scratch(length), leaves=True,
    )
    second.advance()
    first.advance()

    def chosen(array, dims):
        return fetch(array, lambda c, f, g, pair: pair[0], dims)

    def pair_of(core, fill, gate, pair):
        return pair[0]

    def pair_before(core, fill, gate, pair):
        return 1 - pair[0]

    def of_pair(small):
        rest = (
            chosen(qkv_b, (3, length, PAIR)), chosen(lse_b, (TINY, 2 * length)), row_of(tokens, True),
            chosen(mixed_b, (PAIR, length)), chosen(g_own, (d, d)), fetch(small),
        )
        return [weights.out(pair_of)] + [later(one) for one in rest]

    send, small, dbranch, all3 = chain.call(
        partial(backward_other_kernel, False), "backward_other_0", [core, row_fill, a_gate, not_mine],
        [seg, upper(dmid_b), upper(dmid_b_came), *of_pair(small)],
        [shape((d, d)), shape((TINY, d)), shape((length, d), BF16), shape((length, 3 * PAIR), BF16)],
        attention_scratch(length), leaves=True,
    )
    third = Stream(chain, members, bits, send, out, back)
    second.advance()
    first.advance()
    keep, small, total_b = chain.call(
        partial(backward_other_kernel, True), "backward_other_1", [core, row_fill, a_gate, bits[0]],
        [seg, fetch(dbranch), *of_pair(small)]
        + [later(one) for one in (weights.triple(pair_of), fetch(all3), weights.triple(pair_before))],
        [shape((d, d)), shape((TINY, d)), shape((length, d))], attention_scratch(length), leaves=True,
    )
    third.keep(keep, small)
    third.advance()
    second.advance(20.0)
    first.advance(20.0)
    (output,) = chain.call(
        output_kernel, "output", [core, f_gate],
        [fetch(mid_a), lower(dmid_a), lower(dmid_a_came), fetch(ob), fetch(mid_b), lower(dmid_b), lower(dmid_b_came)],
        [shape((2, length, d), BF16)], leaves=True,
    )
    while third.out:
        third.advance()
    while len(second.back) > 2:
        second.advance()
    while not first.done():
        first.advance()
    grads = final_feed(chain, first, 0, d)
    total_a, total_b = third.advance(passes=(total_a, total_b))
    while not second.done():
        second.advance()
        if len(third.back) > 1:
            third.advance()
    while not third.done():
        third.advance()
    total_a_came = across(total_a)
    total_b_came = across(total_b)
    inner_grad, outer_grad = final_feed(chain, second, 1, d, grads)
    (grad_tokens,) = chain.call(
        tokens_kernel, "tokens", [core],
        [fetch(total_a), fetch(total_b_came), fetch(total_b), fetch(total_a_came)],
        [shape((2, length, d))], leaves=True,
    )
    gq, gk, gv, go, gqb, gvb, gob, gib, goutb, gates = final_attention(chain, third, d)
    return (
        output, grad_tokens, gq, gqb.reshape(-1), gk, gv, gvb.reshape(-1), go, gob.reshape(-1), gates[5, 0],
        inner_grad, gib.reshape(-1), outer_grad, goutb.reshape(-1), gates[6, 0],
    )


def solution(mesh):
    rows = P("dp", None, None)
    col = P(None, "mp")
    cut = P("mp")
    in_specs = (
        rows, P("dp", None), P("dp"), col, cut, col, col, cut, P("mp", None), P(), P(),
        col, cut, P("mp", None), P(), P(), rows,
    )
    out_specs = (
        rows, rows, col, cut, col, col, cut, P("mp", None), P(), P(), col, cut,
        P("mp", None), P(), P(),
    )
    return jax.shard_map(
        partial(shards, mesh.shape["dp"]), mesh=mesh, in_specs=in_specs, out_specs=out_specs,
        check_vma=False,
    )
```

```python
from functools import partial
import math

import jax
import jax.numpy as jnp
from jax import lax
from jax.experimental import pallas as pl
from jax.experimental.pallas import tpu as pltpu
from jax.sharding import PartitionSpec as P

HEAD_DIM = 64
PAIR = 2 * HEAD_DIM
LONGEST = 256
BLOCK = 128
TINY = 8
PARTS = 12
ROWS = 256
MASKED = -1e30
F32 = jnp.float32
BF16 = jnp.bfloat16
GELU_C = math.sqrt(2.0 / math.pi)
GELU_A = 0.044715
BIG_LIMIT = 60 * 1024 * 1024
LIMITS = {"output": 62, "tokens": 62, "final_feed_0": 62, "final_feed_1": 62, "final_attention": 62}
WEIGHTS = {"backward_own": 80.0, "output": 80.0}
SMALL_LIMIT = 8 * 1024 * 1024
SMEM = pl.BlockSpec(memory_space=pltpu.SMEM)
VMEM = pl.BlockSpec(memory_space=pltpu.VMEM)
WHERE_IT_IS = pl.BlockSpec(memory_space=pl.ANY)
HBM = pl.BlockSpec(memory_space=pltpu.HBM)


def dot_nn(a, b):
    return lax.dot_general(a, b, (((1,), (0,)), ((), ())), preferred_element_type=F32)


def dot_nt(a, b):
    return lax.dot_general(a, b, (((1,), (1,)), ((), ())), preferred_element_type=F32)


def dot_tn(a, b):
    return lax.dot_general(a, b, (((0,), (0,)), ((), ())), preferred_element_type=F32)


def shape(dims, dtype=F32):
    return jax.ShapeDtypeStruct(tuple(dims), dtype)


class Take:
    def __init__(self, dims, dtype, copies, held=False):
        self.dims, self.dtype, self.copies, self.held = tuple(dims), dtype, copies, held
        self.late = False


def later(one):
    one.late = True
    return one


def take(array, index=None, dims=None):
    return Take(dims or array.shape, array.dtype, [(array, index, None)], True)


def fetch(array, index=None, dims=None):
    return Take(dims or array.shape, array.dtype, [(array, index, None)])


class Coming:
    def __init__(self, buffer, copies, late=False):
        self.buffer, self.copies, self.waiting = buffer, copies, late
        if not late:
            for copy in copies:
                copy.start()

    def start(self):
        if self.waiting:
            for copy in self.copies:
                copy.start()
        self.waiting = False

    def __call__(self):
        self.start()
        for copy in self.copies:
            copy.wait()
        self.copies = []
        return self.buffer


class Going:
    def __init__(self, target, buffer, sems):
        self.target, self.buffer, self.sems, self.copies = target, buffer, sems, []

    def __setitem__(self, index, value):
        self.buffer[index] = value

    def __getitem__(self, index):
        return self.buffer[index]

    def part(self, *index):
        copy = pltpu.make_async_copy(self.buffer.at[index], self.target.at[index], self.sems[len(self.copies)])
        copy.start()
        self.copies.append(copy)

    def send(self):
        if self.target is not None and not self.copies:
            copy = pltpu.make_async_copy(self.buffer, self.target, self.sems[0])
            copy.start()
            self.copies.append(copy)


def part_swapped(swap, one, two, one_index, two_index):
    straight, crossed = [], []
    for a, b, index in ((one, two, one_index), (two, one, two_index)):
        sem = a.sems[len(a.copies)]
        straight.append(pltpu.make_async_copy(a.buffer.at[index], a.target.at[index], sem))
        crossed.append(pltpu.make_async_copy(a.buffer.at[index], b.target.at[index], sem))

    @pl.when(swap)
    def _():
        for copy in crossed:
            copy.start()

    @pl.when(jnp.logical_not(swap))
    def _():
        for copy in straight:
            copy.start()

    one.copies.append(straight[0])
    two.copies.append(straight[1])


def pick(ref, index, scalars):
    if index is None:
        return ref
    return ref.at[index(*scalars) if callable(index) else index]


class Chain:
    def __init__(self):
        self.last = None

    def call(self, kernel, name, scalars, takes, outs, scratch=(), leaves=False, weight=None, passes=(), onto=()):
        arrays, spaces, spots = [], [], []

        def place(array, space):
            for i, (known, its) in enumerate(zip(arrays, spaces)):
                if known is array and its is space:
                    return i
            arrays.append(array)
            spaces.append(space)
            return len(arrays) - 1

        fetched = [one for one in takes if not one.held]
        views = []
        for one in takes:
            if one.held:
                views.append((place(one.copies[0][0], VMEM), one.copies[0][1]))
            else:
                spots.append([(place(a, HBM), s, t) for a, s, t in one.copies])
        after = [] if self.last is None else [self.last]
        n_scalar, n_array, n_out = len(scalars), len(arrays), len(outs)
        n_copies = sum(len(one) for one in spots)

        def body(*refs):
            numbers, refs = refs[:n_scalar], refs[n_scalar:]
            given, refs = refs[:n_array], refs[n_array + len(after) + len(passes) + len(onto) :]
            results, refs = refs[:n_out], refs[n_out + len(passes) :]
            sems, refs = refs[0], refs[1:]
            into, refs = refs[: len(fetched)], refs[len(fetched) :]
            outof, rest = (refs[:n_out], refs[n_out:]) if leaves else (results, refs)
            at = 0
            buffers = []
            for one, buffer, copies in zip(fetched, into, spots):
                listed = []
                for which, source, target in copies:
                    listed.append(
                        pltpu.make_async_copy(
                            pick(given[which], source, numbers), pick(buffer, target, numbers), sems.at[at]
                        )
                    )
                    at += 1
                buffers.append(Coming(buffer, listed, one.late))
            left, seen, coming = list(buffers), list(views), []
            for one in takes:
                if one.held:
                    which, index = seen.pop(0)
                    coming.append(Coming(pick(given[which], index, numbers), []))
                else:
                    coming.append(left.pop(0))
            going = [
                Going(result if leaves else None, buffer, [sems.at[at + PARTS * i + j] for j in range(PARTS)])
                for i, (result, buffer) in enumerate(zip(results, outof))
            ]
            kernel(*numbers, *coming, *going, *rest)
            for one in coming:
                one()
            for one in going:
                one.send()
            for one in going:
                for copy in one.copies:
                    copy.wait()

        body.__name__ = name
        out = pl.pallas_call(
            body,
            in_specs=[SMEM] * n_scalar + spaces + [WHERE_IT_IS] * len(after) + [HBM] * (len(passes) + len(onto)),
            out_specs=[HBM if leaves else VMEM] * n_out + [HBM] * len(passes),
            out_shape=list(outs) + [shape(one.shape, one.dtype) for one in passes],
            input_output_aliases={
                n_scalar + n_array + len(after) + i: (n_out + i if i < len(passes) else i - len(passes))
                for i in range(len(passes) + len(onto))
            },
            scratch_shapes=[pltpu.SemaphoreType.DMA((n_copies + PARTS * n_out,))]
            + [pltpu.VMEM(one.dims, one.dtype) for one in fetched]
            + [pltpu.VMEM(o.shape, o.dtype) for o in outs if leaves]
            + list(scratch),
            compiler_params=pltpu.CompilerParams(vmem_limit_bytes=LIMITS.get(name, BIG_LIMIT >> 20) << 20 if leaves else SMALL_LIMIT),
            cost_estimate=pl.CostEstimate(flops=int(1e9 * (WEIGHTS.get(name, 17.0 if leaves else 0.0) if weight is None else weight)) + 1000, bytes_accessed=1000, transcendentals=0),
            name=name,
        )(*scalars, *arrays, *after, *passes, *onto)
        self.last = out[0]
        return out


def window(first, length):
    return max(0, first - LONGEST), min(length, first + BLOCK + LONGEST)


class Weights:
    def __init__(self, wq, wk, wv, bq, bv, wo):
        self.projections, self.biases, self.wo = (wq, wk, wv), (bq, bv), wo

    def cut(self, p, n=1):
        if callable(p):
            return lambda *numbers: pl.ds(pl.multiple_of(p(*numbers) * PAIR, PAIR), n * PAIR)
        return lambda *numbers: slice(p * PAIR, (p + n) * PAIR)

    def triple(self, p):
        d = self.wo.shape[1]
        cut = self.cut(p)
        return Take(
            (d, 3 * PAIR), BF16,
            [
                (a, lambda *n: (slice(None), cut(*n)), (slice(None), slice(i * PAIR, (i + 1) * PAIR)))
                for i, a in enumerate(self.projections)
            ],
        )

    def out(self, p, n=1):
        d = self.wo.shape[1]
        cut = self.cut(p, n)
        return Take((n * PAIR, d), BF16, [(self.wo, lambda *k: (cut(*k), slice(None)), None)])

    def bias(self):
        bq, bv = self.biases
        half = bq.shape[1]
        return Take(
            (1, 2 * half), F32,
            [(bq, None, (slice(None), slice(0, half))), (bv, None, (slice(None), slice(half, 2 * half)))],
        )


class SentWeights:
    def __init__(self, pack):
        self.pack, self.d = pack, pack.shape[1]

    def cut(self, p, base, n=1):
        def index(*numbers):
            if callable(p):
                return pl.ds(pl.multiple_of(base + p(*numbers) * PAIR, PAIR), n * PAIR)
            return slice(base + p * PAIR, base + (p + n) * PAIR)

        return index

    def triple(self, p):
        d, half = self.d, self.d // 2
        copies = []
        for i, (rows, base) in enumerate(((slice(0, d), 0), (slice(0, d), half), (slice(d, 2 * d), 0))):
            cut = self.cut(p, base)
            copies.append(
                (self.pack, lambda *n, rows=rows, cut=cut: (rows, cut(*n)), (slice(None), slice(i * PAIR, (i + 1) * PAIR)))
            )
        return Take((d, 3 * PAIR), F32, copies)

    def out(self, p, n=1):
        d, half = self.d, self.d // 2
        copies = []
        for i in range(2):
            cut = self.cut(p, d + i * half, n)
            copies.append(
                (self.pack, lambda *k, cut=cut: (cut(*k), slice(half, d)), (slice(None), slice(i * half, (i + 1) * half)))
            )
        return Take((n * PAIR, d), F32, copies)

    def bias(self):
        d = self.d
        return fetch(self.pack, (slice(2 * d, 2 * d + TINY), slice(None)), (TINY, d))


def pack_kernel(wq, wk, wv, wo, bq, bv, bi, w_inner, w_outer, out, inner_out, outer_out):
    d, half = wq.buffer.shape
    out[0:d, :half] = wq()[...].astype(F32)
    out[0:d, half:] = wk()[...].astype(F32)
    out.part(slice(0, d))
    out[d : 2 * d, :half] = wv()[...].astype(F32)
    out[d : d + half, half:] = wo()[:, :half].astype(F32)
    out[d + half : 2 * d, half:] = wo()[:, half:].astype(F32)
    out[2 * d : 2 * d + 1, :half] = bq()[...]
    out[2 * d : 2 * d + 1, half:] = bv()[...]
    out[2 * d + 1 : 2 * d + 2, :] = bi()[:, :d]
    out[2 * d + 2 : 2 * d + 3, :] = bi()[:, d:]
    out[2 * d + 3 :, :] = jnp.zeros((TINY - 3, d), F32)
    out.part(slice(d, 2 * d + TINY))
    for ref, result in ((w_inner, inner_out), (w_outer, outer_out)):
        rows = ref.buffer.shape[0] // 2
        for i in range(2):
            cut = slice(i * rows, (i + 1) * rows)
            result[cut, :] = ref()[cut, :].astype(F32)
            result.part(cut)


def row_index(other):
    return lambda core, *_: 1 - core[0] if other else core[0]


def row_of(array, other):
    return Take(array.shape[1:], array.dtype, [(array, row_index(other), None)])


def segments_of(place, fill_ref, seg, cols_ref):
    length = cols_ref.shape[0]
    fill = fill_ref[place]
    row = seg()[pl.ds(place, 1), :].astype(F32)
    places = lax.broadcasted_iota(jnp.int32, (1, length), 1)
    valid = places < fill
    keyed = jnp.where(valid, row, -1.0)
    cols_ref[...] = jnp.broadcast_to(keyed, (PAIR, length)).T
    return row, jnp.where(valid, 1.0, 0.0)


def mask_for(cols_ref, row, low, high, first):
    once = cols_ref[low:high, :] == row[:, first : first + BLOCK]
    return jnp.concatenate([once, once], axis=1)


def two_heads(array):
    lanes = lax.broadcasted_iota(jnp.int32, array.shape, 1)
    return jnp.where(lanes < HEAD_DIM, array, 0), jnp.where(lanes < HEAD_DIM, 0, array)


def stacked(pair, first):
    return jnp.concatenate([half[first : first + BLOCK] for half in pair], axis=0)


def forward_pair(p, x, w3, bias, row, valid, cols, qkv, mixed_out, lse):
    length = x.shape[0]
    half = bias.shape[1] // 2
    y = dot_nn(x, w3)
    at = p * PAIR
    q = y[:, :PAIR] + bias[0:1, at : at + PAIR]
    q = (q.astype(BF16) * 0.125).astype(BF16)
    k = y[:, PAIR : 2 * PAIR].astype(BF16)
    v = (y[:, 2 * PAIR :] + bias[0:1, half + at : half + at + PAIR]).astype(BF16)
    vt = v.T
    qkv[0] = q
    qkv[1] = k
    qkv[2] = v
    heads = two_heads(q)
    for first in range(0, length, BLOCK):
        low, high = window(first, length)
        block = slice(first, first + BLOCK)
        s = dot_nt(k[low:high], stacked(heads, first))
        s = jnp.where(mask_for(cols, row, low, high, first), s, MASKED)
        peak = jnp.max(s, axis=0, keepdims=True)
        e = jnp.exp(s - peak)
        total = jnp.sum(e, axis=0, keepdims=True)
        o = dot_nn(vt[:, low:high], e.astype(BF16))
        keep = valid[:, block]
        o0 = o[:HEAD_DIM, :BLOCK] * (keep / total[:, :BLOCK])
        o1 = o[HEAD_DIM:, BLOCK:] * (keep / total[:, BLOCK:])
        mixed_out[:HEAD_DIM, block] = o0.astype(BF16)
        mixed_out[HEAD_DIM:, block] = o1.astype(BF16)
        lse[0:1, 2 * first : 2 * first + 2 * BLOCK] = peak + jnp.log(total)


def start_all(*ones):
    for one in ones:
        one.start()


def forward_pairs(x, w3s, bias, row, valid, cols, qkv, mixed, lse):
    for p, w3 in enumerate(w3s):
        forward_pair(
            p, x, w3()[...].astype(BF16), bias(), row, valid, cols, qkv.buffer.at[p], mixed.buffer.at[p], lse.buffer.at[p]
        )
        qkv.part(p)
        mixed.part(p)
        lse.part(p)


def forward_own_kernel(core_ref, fill_ref, seg, x_in, w3_0, bias, w3_1, qkv, mixed, lse, cols):
    row, valid = segments_of(core_ref[0], fill_ref, seg, cols)
    x = x_in()[...]
    w3_0()
    start_all(w3_1)
    forward_pairs(x, (w3_0, w3_1), bias, row, valid, cols, qkv, mixed, lse)


def units_of(low, lowt, d_ffn, wi, bias, wo):
    pre = dot_nn(low, wi) + bias
    square = pre * pre
    t = jnp.tanh(pre * (GELU_C + (GELU_C * GELU_A) * square))
    cdf = 0.5 + 0.5 * t
    hidden = (pre * cdf).astype(BF16)
    slope = cdf + (0.5 * pre) * (1.0 - t * t) * (GELU_C + (3.0 * GELU_C * GELU_A) * square)
    d_pre = (dot_nt(d_ffn, wo) * slope).astype(BF16)
    bias_sum = jnp.sum(d_pre.astype(F32), axis=0, keepdims=True)
    return hidden, d_pre, dot_tn(hidden, d_ffn), dot_nn(lowt, d_pre), bias_sum


def all_units(low, lowt, d_ffn, wi, bias_of, wo, grads, bias_out, hidden_out, pre_out):
    units = wi().shape[1]
    part, step = units // 2, 256
    for at in range(0, units, step):
        i, inside = divmod(at, part)
        cut, held = slice(at, at + step), slice(inside, inside + step)
        hidden, d_pre, outer, inner, bias_sum = units_of(
            low, lowt, d_ffn, wi()[:, cut].astype(BF16), bias_of(i, held), wo()[cut, :].astype(BF16)
        )
        hidden_out[:, cut] = hidden
        pre_out[:, cut] = d_pre
        bias_out[i : i + 1, held] = bias_sum
        grads[i][held, :] = outer
        grads[i][part:, held] = inner
        if inside + step == part:
            grads[i].send()


def middle_kernel(core_ref, fill_ref, gate, feed_gate, seg, x_in, w3_0, bias, w3_1, wo, mixed_own, wo_own, out_bias,
                  cot, wi, w_outer, qkv, mixed, lse, mid, low_out, grad_0, grad_1, bias_out, hidden_out, pre_out, cols):
    row, valid = segments_of(core_ref[0], fill_ref, seg, cols)
    x = x_in()[...]
    w3_0()
    start_all(w3_1, wo, mixed_own, wo_own, out_bias, cot, wi, w_outer)
    forward_pairs(x, (w3_0, w3_1), bias, row, valid, cols, qkv, mixed, lse)
    for at in range(0, x.shape[0], ROWS):
        rows = slice(at, at + ROWS)
        branch = out_bias()[...]
        for p in range(2):
            cut = slice(p * PAIR, (p + 1) * PAIR)
            branch = branch + dot_tn(mixed_own()[p, :, rows], wo_own()[cut, :])
            branch = branch + dot_tn(mixed[p, :, rows], wo()[cut, :].astype(BF16))
        value = x[rows].astype(F32) + gate[0] * branch
        mid[rows, :] = value
        mid.part(rows)
        low_out[rows, :] = value.astype(BF16)
        low_out.part(rows)
    low = low_out[...]
    d_ffn = (feed_gate[0] * cot()[...].astype(F32)).astype(BF16)
    bias_out[...] = jnp.zeros(bias_out.buffer.shape, F32)
    all_units(
        low, low.T, d_ffn, wi, lambda i, cut: bias()[1 + i : 2 + i, cut], w_outer, (grad_0, grad_1), bias_out,
        hidden_out, pre_out,
    )


def feed_kernel(core_ref, gate, feed_gate, low_in, wi, bi, cot_in, w_outer, hidden_sent, pre_sent, wi_sent, wo_sent,
                out_bias, mid, x, grad_0, grad_1, out, dmid_out, dbranch_out, small, bias_out, hidden_out, pre_out):
    low = low_in()[...]
    length, d = low.shape
    wi()
    start_all(cot_in, w_outer)
    lowt = low.T
    cot = cot_in()[...].astype(F32)
    d_ffn = (feed_gate[0] * cot).astype(BF16)
    w_outer()
    start_all(hidden_sent, pre_sent, wi_sent, wo_sent, out_bias, mid, x)
    bias_out[...] = jnp.zeros_like(bias_out)
    part = d
    all_units(
        low, lowt, d_ffn, wi, lambda i, cut: bi()[:, i * part : (i + 1) * part][:, cut], w_outer, (grad_0, grad_1),
        bias_out, hidden_out, pre_out,
    )
    wi_other = wi_sent()[...].astype(BF16)
    wo_other = wo_sent()[...].astype(BF16)
    sums = [jnp.zeros((1, d), F32)] * 3
    for at in range(0, length, ROWS):
        rows = slice(at, at + ROWS)
        seen = cot_in()[rows, :].astype(F32)
        dmid = dot_nt(pre_sent()[rows, :], wi_other) + dot_nt(pre_out[rows, :], wi()[...]) + seen
        ffn = dot_nn(hidden_sent()[rows, :], wo_other) + dot_nn(hidden_out[rows, :], w_outer()[...]) + out_bias()[...]
        dmid_out[rows, :] = dmid
        dmid_out.part(rows)
        dbranch = (gate[0] * dmid).astype(BF16)
        dbranch_out[rows, :] = dbranch
        dbranch_out.part(rows)
        middle = mid()[rows, :]
        out[rows, :] = middle + feed_gate[0] * ffn
        out.part(rows)
        branch = middle - x()[rows, :].astype(F32)
        for i, value in enumerate((dbranch.astype(F32), dmid * branch, seen * ffn)):
            sums[i] = sums[i] + jnp.sum(value, axis=0, keepdims=True)
    small[...] = jnp.zeros(small.buffer.shape, F32)
    small[1:3, :] = bias_out[0:2, :]
    small[3:4, :] = sums[0]
    small[4:5, :] = jnp.sum(d_ffn.astype(F32), axis=0, keepdims=True)
    small[5:6, :] = sums[1] / gate[0]
    small[6:7, :] = sums[2]


def join_kernel(bit, a, a_came, b, b_came, keep, send):
    rows = keep.buffer.shape[0] // 2
    start_all(a, a_came, b, b_came)
    for i in range(2):
        cut = slice(i * rows, (i + 1) * rows)
        keep[cut, :] = a()[cut, :] + a_came()[cut, :]
        send[cut, :] = b()[cut, :] + b_came()[cut, :]
        part_swapped(bit[0] != 0, keep, send, (cut,), (cut,))


def backward_pair(dbranch, do, qkv, lse, mixed, x, row, cols, dk_acc, dv_acc, dqt, grad_out):
    length, d = dbranch.shape
    q, k, v = qkv[0], qkv[1], qkv[2]
    kt = k.T
    qs = two_heads(q)
    dos = two_heads(do)
    dk_acc[...] = jnp.zeros_like(dk_acc)
    dv_acc[...] = jnp.zeros_like(dv_acc)
    for first in range(0, length, BLOCK):
        low, high = window(first, length)
        block = slice(first, first + BLOCK)
        qq = stacked(qs, first)
        dd = stacked(dos, first)
        s = dot_nt(k[low:high], qq)
        s = jnp.where(mask_for(cols, row, low, high, first), s, MASKED)
        w = jnp.exp(s - lse[0:1, 2 * first : 2 * first + 2 * BLOCK])
        dw = dot_nt(v[low:high], dd)
        both = w * dw
        mean = jnp.sum(both, axis=0, keepdims=True)
        ds = (both - w * mean).astype(BF16)
        dv_acc[low:high, :] += dot_nn(w.astype(BF16), dd)
        dk_acc[low:high, :] += dot_nn(ds, qq)
        dq = dot_nn(kt[:, low:high], ds)
        dqt[:HEAD_DIM, block] = dq[:HEAD_DIM, :BLOCK]
        dqt[HEAD_DIM:, block] = dq[HEAD_DIM:, BLOCK:]
    dq = (0.125 * dqt[...]).T.astype(BF16)
    all3 = jnp.concatenate([dq, dk_acc[...].astype(BF16), dv_acc[...].astype(BF16)], axis=1)
    grad_out[:, : 3 * PAIR] = dot_tn(x, all3)
    out_grad = dot_nn(mixed, dbranch)
    for c in range(d // PAIR):
        cut = slice(c * PAIR, (c + 1) * PAIR)
        grad_out[cut, 3 * PAIR :] = out_grad[:, cut]
    return all3


def bias_sums(all3):
    sums = jnp.sum(all3.astype(F32), axis=0, keepdims=True)
    return jnp.concatenate([sums[:, :PAIR], sums[:, 2 * PAIR :]], axis=1)


def masked_heads(dbranch, wo, fill):
    places = lax.broadcasted_iota(jnp.int32, (dbranch.shape[0], 1), 0)
    return jnp.where(places < fill, dot_nt(dbranch, wo), 0.0).astype(BF16)


def backward_kernel(sent, last, core_ref, fill_ref, pair, *refs):
    if sent and not last:
        bit, *refs = refs
    seg, dbranch_in, wo, x_in, qkv, lse, mixed, *refs = refs
    late = []
    if last:
        w3, all3_in, w3_before, total_in, *refs = refs
        late += [w3, all3_in, w3_before, total_in]
    if sent:
        if last:
            bias_in, *refs = refs
            late.append(bias_in)
        else:
            parts, refs = refs[:4], refs[4:]
            late += parts
    else:
        came, *refs = refs
        late.append(came)
    small_in, *refs = refs
    late.append(small_in)
    if last:
        grad_out, small_out, total_out, *rest = refs
    else:
        grad_out, small_out, all3_out, *rest = refs
        if sent:
            keep, send, *rest = rest
    cols, dk_acc, dv_acc, dqt = rest
    row, _ = segments_of(core_ref[0], fill_ref, seg, cols)
    dbranch = dbranch_in()[...]
    length, d = dbranch.shape
    do = masked_heads(dbranch, wo()[...].astype(BF16), fill_ref[core_ref[0]])
    x = x_in()[...]
    qkv()
    start_all(*late)
    grads = grad_out.buffer.at[0:d]
    all3 = backward_pair(dbranch, do, qkv(), lse(), mixed()[...], x, row, cols, dk_acc, dv_acc, dqt, grads)
    small_out[...] = small_in()[...]
    if sent and last:
        small_out[1:3, :] = bias_in()[0:2, :]
    if not sent:
        grads[...] += came()[0:d, :]
    spot = pl.ds(pl.multiple_of(pair[0] * 2 * PAIR, PAIR), 2 * PAIR)
    if sent and not last:
        small_out[0:1, spot] = bias_sums(all3)
    else:
        small_out[0:1, spot] += bias_sums(all3)
    if last and not sent:
        small_out[...] += came()[d:, :]
    if last and sent:
        grad_out[d:, :] = small_out[...]
    grad_out.send()
    if last:
        for at in range(0, length, ROWS):
            rows = slice(at, at + ROWS)
            total = dot_nt(all3_in()[rows, :], w3_before()[...].astype(BF16)) + dot_nt(all3[rows], w3()[...].astype(BF16))
            total_out[rows, :] = total_in()[rows, :] + total
            total_out.part(rows)
    else:
        all3_out[...] = all3
        if sent:
            join_kernel(bit, *parts, keep, send)


def attention_scratch(length):
    return [pltpu.VMEM((length, PAIR), F32)] * 3 + [pltpu.VMEM((PAIR, length), F32)]


def place_in(refs, mask):
    at = 0
    for ref in refs:
        at = 2 * at + ref[0]
    return jnp.bitwise_xor(at, mask)


def sum_of(terms, cut):
    total = terms[0]()[cut, :]
    for one in terms[1:]:
        total = total + one()[cut, :]
    return total


class Stream:
    def __init__(self, chain, members, bits, send, out, back):
        self.chain, self.members, self.bits = chain, members, bits
        self.out, self.back = list(out), list(back)
        self.group = [0]
        self.came = [self.travel(send, 1)]
        self.tail, self.small, self.turned, self.lanes = 0, None, False, 1

    def keep(self, mine, small=None):
        self.mine, self.small = mine, small
        self.rows, self.width = mine.shape
        self.joined = []

    def join(self, other):
        self.joined = [other]

    def travel(self, array, mask):
        pairs = []
        for place in range(self.members):
            for core in range(2):
                partner = place
                for i, step in enumerate(reversed(self.group)):
                    if mask >> i & 1:
                        partner ^= 1 << (step ^ core if step < 2 else step)
                pairs.append((place * 2 + core, partner * 2 + core))
        return lax.ppermute(array, ("dp", "mp"), pairs)

    def call(self, kernel, name, group, outs, small=False):
        takes = [take(one) for stream in (self, *self.joined) for one in (stream.mine, *stream.came)]
        takes += [take(self.small)] if small else []
        results = self.chain.call(
            kernel, name, [self.bits[step] for step in group], takes, [shape(dims) for dims in outs],
            weight=self.weight, passes=self.passes,
        )
        self.passes = results[len(outs) :]
        return results[: len(outs)]

    def halve(self):
        group = self.out.pop(0)
        parts, n_terms = 1 << len(group), 1 + len(self.came)
        whole, tail = self.rows, self.tail
        rows = whole // parts
        begins = self.small is not None and not tail
        sources = 1 + len(self.joined)
        lanes = self.lanes = max(self.lanes, sources)

        def kernel(*refs):
            bits, refs = refs[: len(group)], refs[len(group) :]
            terms = [refs[i * n_terms : (i + 1) * n_terms] for i in range(sources)]
            refs = refs[sources * n_terms :]
            if begins:
                both = refs[0]()[...]
                refs = refs[1:]
            elif tail:
                both = sum_of(terms[0], slice(lanes * whole, lanes * whole + tail))
            for mask, out in enumerate(refs):
                at = place_in(bits, mask) * rows
                for lane in range(lanes):
                    source, base = (lane, 0) if sources > 1 else (0, lane * whole)
                    cut = pl.ds(pl.multiple_of(base + at, 8), rows)
                    out[lane * rows : (lane + 1) * rows, :] = sum_of(terms[source], cut)
                if begins or tail:
                    out[lanes * rows :, :] = both

        if begins:
            self.tail = TINY
        self.mine, *sends = self.call(
            kernel, "halve", group, [(lanes * rows + self.tail, self.width)] * parts, begins
        )
        self.joined = []
        self.group = group
        self.came = [self.travel(send, mask + 1) for mask, send in enumerate(sends)]
        self.rows = rows

    def turn(self):
        rows, tail = self.lanes * self.rows, self.tail
        n_came = len(self.came)

        def kernel(mine, *refs):
            came, refs = refs[:n_came], refs[n_came:]
            total = mine()[...]
            for one in came:
                total = total + one()[...]
            refs[0][...] = total[:rows]
            if tail:
                refs[1][...] = total[rows:]

        outs = [(rows, self.width)] + ([(TINY, self.width)] if tail else [])
        self.mine, *tiny = self.call(kernel, "turn", [], outs)
        self.small = tiny[0] if tiny else None
        self.turned = True
        self.spread()

    def double(self):
        rows, lanes = self.rows, self.lanes
        parts = len(self.came) + 1
        ends = len(self.back) == 1 and self.small is not None
        group = self.group

        def kernel(*refs):
            bits, refs = refs[: len(group)], refs[len(group) :]
            have, refs = refs[:parts], refs[parts:]
            out = refs[-1]
            if ends:
                out[lanes * parts * rows :, :] = refs[0]()[...]
            for mask, one in enumerate(have):
                at = place_in(bits, mask) * rows
                for lane in range(lanes):
                    cut = pl.ds(pl.multiple_of(lane * parts * rows + at, 8), rows)
                    out[cut, :] = one()[lane * rows : (lane + 1) * rows, :]

        self.rows = parts * rows
        (self.mine,) = self.call(
            kernel, "double", group, [(lanes * self.rows + (TINY if ends else 0), self.width)], ends
        )
        self.spread()

    def spread(self):
        self.group = self.back.pop(0)
        self.came = [self.travel(self.mine, mask) for mask in range(1, 1 << len(self.group))]

    def advance(self, weight=0.0, passes=()):
        self.weight, self.passes = weight, passes
        if self.out:
            self.halve()
        elif not self.turned:
            self.turn()
        elif self.back:
            self.double()
        return self.passes

    def done(self):
        return self.turned and not self.back


def in_order(bit, mine, came, low, high):
    @pl.when(bit[0] == 0)
    def _():
        low(mine())
        high(came())

    @pl.when(bit[0] != 0)
    def _():
        low(came())
        high(mine())


def final_feed(chain, stream, index, d, onto=()):
    units = stream.rows
    cut = slice(index * units, (index + 1) * units)

    def kernel(bit, mine, came, inner, outer):
        mine()
        came()

        def low(ref):
            outer[cut, :] = ref[...]

        def high(ref):
            inner[:, cut] = ref[...]

        in_order(bit, mine, came, low, high)
        outer.part(cut)
        inner.part(slice(None), cut)

    return chain.call(
        kernel, "final_feed_%d" % index, [stream.bits[0]], [fetch(stream.mine), fetch(stream.came[0])],
        [shape((d, 2 * units)), shape((2 * units, d))], leaves=True, onto=onto,
    )


def final_attention(chain, third, d):
    half = d // 2

    def kernel(bit, mine, came, gq, gk, gv, go, gqb, gvb, gob, gib, goutb, gates):
        small = mine()[d:, :] + came()[d:, :]
        for p in range(2):
            cut = slice(p * PAIR, (p + 1) * PAIR)
            gqb[:, cut] = small[0:1, 2 * p * PAIR : (2 * p + 1) * PAIR]
            gvb[:, cut] = small[0:1, (2 * p + 1) * PAIR : (2 * p + 2) * PAIR]
        gib[:, :d] = small[1:2, :]
        gib[:, d:] = small[2:3, :]
        gob[...] = small[3:4, :]
        goutb[...] = small[4:5, :]
        gates[...] = jnp.broadcast_to(jnp.sum(small, axis=1, keepdims=True), gates.buffer.shape)

        def place(p, ref):
            cut = slice(p * PAIR, (p + 1) * PAIR)
            gq[:, cut] = ref[:d, :PAIR]
            gk[:, cut] = ref[:d, PAIR : 2 * PAIR]
            gv[:, cut] = ref[:d, 2 * PAIR : 3 * PAIR]
            for c in range(d // PAIR):
                across = slice(c * PAIR, (c + 1) * PAIR)
                go[cut, across] = ref[across, 3 * PAIR :]

        in_order(bit, mine, came, partial(place, 0), partial(place, 1))

    return chain.call(
        kernel, "final_attention", [third.bits[0]], [take(third.mine), take(third.came[0])],
        [shape((d, half))] * 3
        + [shape((half, d)), shape((1, half)), shape((1, half)), shape((1, d)), shape((1, 2 * d)), shape((1, d)), shape((TINY, PAIR))],
        leaves=True,
    )


def rows_kernel(core_ref, own, came, out):
    out[core_ref[0]] = own()[...].astype(out.buffer.dtype)
    out.part(core_ref[0])
    out[1 - core_ref[0]] = came()[...].astype(out.buffer.dtype)
    out.part(1 - core_ref[0])


def shards(members, tokens, segment_ids, row_fill, query_weight, query_bias, key_weight,
           value_weight, value_bias, out_weight, out_bias, attention_gate, inner_weight,
           inner_bias, outer_weight, outer_bias, feed_gate, cotangent):
    _, length, d = tokens.shape
    half = d // 2
    place = lax.axis_index("dp")
    core_id = lax.axis_index("mp")
    core = core_id.astype(jnp.int32).reshape(1)
    bits = []
    for step in range(members.bit_length() - 1):
        bit = (place >> (step ^ core_id if step < 2 else step)) & 1
        bits.append(bit.astype(jnp.int32).reshape(1))
    not_mine = 1 - bits[0]
    chain = Chain()

    def across(array):
        return lax.ppermute(array, "mp", [(0, 1), (1, 0)])

    def as_row(array):
        return array.reshape(1, -1)

    def own_row(array):
        return row_of(array, False)

    a_gate = attention_gate.reshape(1)
    f_gate = feed_gate.reshape(1)
    qb, vb, ib, ob, fb = (as_row(a) for a in (query_bias, value_bias, inner_bias, out_bias, outer_bias))
    own = Weights(query_weight, key_weight, value_weight, qb, vb, out_weight)
    seg = fetch(segment_ids)
    cols = [pltpu.VMEM((length, PAIR), F32)]
    units = inner_weight.shape[1]

    pack, wi, wo = chain.call(
        pack_kernel, "pack", [],
        [fetch(a) for a in (query_weight, key_weight, value_weight, out_weight, qb, vb, ib, inner_weight, outer_weight)],
        [shape((2 * d + TINY, d)), shape((d, units)), shape((units, d))], leaves=True,
    )
    pack_came, wi_came, wo_came = across(pack), across(wi), across(wo)
    sent = SentWeights(pack_came)

    pair_outs = [shape((2, 3, length, PAIR), BF16), shape((2, PAIR, length), BF16), shape((2, TINY, 2 * length))]
    qkv_a, mixed_a, lse_a = chain.call(
        forward_own_kernel, "forward_own", [core, row_fill],
        [seg, own_row(tokens), own.triple(0), own.bias(), later(own.triple(1))], pair_outs, cols, leaves=True,
    )
    unit_outs = [shape((length, units), BF16)] * 2
    grad_outs = [shape((2 * d, d))] * 2
    qkv_b, mixed_b, lse_b, mid, low, g_sent_0, g_sent_1, bias_b, hidden_b, pre_b = chain.call(
        middle_kernel, "middle", [core, row_fill, a_gate, f_gate],
        [seg, own_row(tokens), sent.triple(0), sent.bias()]
        + [
            later(one)
            for one in (
                sent.triple(1), sent.out(0, 2), fetch(mixed_a), own.out(0, 2), fetch(ob), own_row(cotangent),
                fetch(wi_came), fetch(wo_came),
            )
        ],
        pair_outs + [shape((length, d)), shape((length, d), BF16)] + grad_outs + [shape((TINY, d))] + unit_outs,
        cols, leaves=True,
    )
    g_came_0, g_came_1 = across(g_sent_0), across(g_sent_1)
    g_own_0, g_own_1, out_own, dmid, dbranch, small = chain.call(
        feed_kernel, "feed", [core, a_gate, f_gate],
        [fetch(low), fetch(inner_weight), fetch(ib)]
        + [
            later(one)
            for one in (
                own_row(cotangent), fetch(outer_weight), fetch(hidden_b), fetch(pre_b), fetch(wi_came), fetch(wo_came),
                fetch(fb), fetch(mid), own_row(tokens),
            )
        ],
        grad_outs + [shape((length, d))] * 2 + [shape((length, d), BF16), shape((TINY, d))],
        [pltpu.VMEM((TINY, d), F32)] + [pltpu.VMEM((length, units), BF16)] * 2, leaves=True,
    )

    wide = [[step for step in pair if step < len(bits)] for pair in ((i, i + 1) for i in range(2, len(bits), 2))]
    one_by_one = [[step] for step in range(len(bits))]
    direct = ([[1], *wide], [*wide[::-1], [1], [0]])
    plain = (one_by_one[1:], one_by_one[::-1])

    def halves(mine, came):
        return [fetch(one, (slice(i * d, (i + 1) * d), slice(None)), (d, d)) for i in range(2) for one in (mine, came)]

    def stream(send, ways):
        return Stream(chain, members, bits, send, *ways)

    other_bit = ((place >> (1 - core_id)) & 1).astype(jnp.int32).reshape(1)
    pair_of = lambda core, fill, pair, *_: pair[0]
    pair_before = lambda core, fill, pair, *_: 1 - pair[0]

    def backward(sent, last, pair, weights, kept, extra, small, outs, bit=None):
        qkv, mixed, lse = kept
        takes = [
            seg, fetch(dbranch), weights.out(pair_of), own_row(tokens), fetch(qkv, pair_of, (3, length, PAIR)),
            fetch(lse, pair_of, (TINY, 2 * length)), fetch(mixed, pair_of, (PAIR, length)),
        ]
        more = list(extra)
        if last:
            all3, total, *rest = more
            more = [weights.triple(pair_of), fetch(all3), weights.triple(pair_before), fetch(total), *rest]
        takes += [later(one) for one in [*more, fetch(small)]]
        return chain.call(
            partial(backward_kernel, sent, last), "backward_%s_%d" % ("sent" if sent else "own", last),
            [core, row_fill, pair] + ([bit] if bit is not None else []), takes, outs, attention_scratch(length),
            leaves=True,
        )

    keep, send = chain.call(
        join_kernel, "join", [bits[0]], halves(g_own_0, g_came_0), [shape((d, d))] * 2, leaves=True
    )
    first = stream(send, direct)
    first.keep(keep)
    square, row8, rows3 = shape((d, d)), shape((TINY, d)), shape((length, 3 * PAIR), BF16)
    kept_a, kept_b = (qkv_a, mixed_a, lse_a), (qkv_b, mixed_b, lse_b)
    g_0, small_b, all3, keep, send = backward(
        True, False, 1 - other_bit, sent, kept_b, halves(g_own_1, g_came_1), small, [square, row8, rows3, square, square],
        bit=bits[0],
    )
    second = stream(send, plain)
    second.keep(keep)
    g_came_first = across(g_0)
    first.advance(0.0)
    g_1, _, total = backward(
        True, True, other_bit, sent, kept_b, (all3, dmid, fetch(bias_b)), small_b,
        [shape((d + TINY, d)), row8, shape((length, d))],
    )
    g_came_last = across(g_1)
    first.advance(0.0)
    second.advance(0.0)
    send, small, all3 = backward(
        False, False, not_mine, own, kept_a, (fetch(g_came_first),), small, [square, row8, rows3]
    )
    third = stream(send, direct)
    first.advance(0.0)
    second.advance(0.0)
    keep, small, total = backward(
        False, True, bits[0], own, kept_a, (all3, total, fetch(g_came_last)), small,
        [square, row8, shape((length, d))],
    )
    third.keep(keep, small)
    third.advance()
    first.advance()
    second.advance(20.0)
    while third.out:
        third.advance()
    while not first.done():
        first.advance(20.0)
    third.advance(20.0)
    second.advance()
    grads = final_feed(chain, first, 0, d)
    (out_own,) = third.advance(passes=(out_own,))
    out_came = across(out_own)
    second.advance()
    while not third.done():
        (total,) = third.advance(passes=(total,))
        second.advance()
    total_came = across(total)
    (output,) = chain.call(
        rows_kernel, "output", [core], [fetch(out_own), fetch(out_came)], [shape((2, length, d), BF16)], leaves=True
    )
    while not second.done():
        second.advance()
    (grad_tokens,) = chain.call(
        rows_kernel, "tokens", [core], [fetch(total), fetch(total_came)], [shape((2, length, d))], leaves=True
    )
    gq, gk, gv, go, gqb, gvb, gob, gib, goutb, gates = final_attention(chain, third, d)
    inner_grad, outer_grad = final_feed(chain, second, 1, d, grads)
    return (
        output, grad_tokens, gq, gqb.reshape(-1), gk, gv, gvb.reshape(-1), go, gob.reshape(-1), gates[5, 0],
        inner_grad, gib.reshape(-1), outer_grad, goutb.reshape(-1), gates[6, 0],
    )


def solution(mesh):
    rows = P("dp", None, None)
    col = P(None, "mp")
    cut = P("mp")
    in_specs = (
        rows, P("dp", None), P("dp"), col, cut, col, col, cut, P("mp", None), P(), P(),
        col, cut, P("mp", None), P(), P(), rows,
    )
    out_specs = (
        rows, rows, col, cut, col, col, cut, P("mp", None), P(), P(), col, cut,
        P("mp", None), P(), P(),
    )
    return jax.shard_map(
        partial(shards, mesh.shape["dp"]), mesh=mesh, in_specs=in_specs, out_specs=out_specs,
        check_vma=False,
    )
```

```python
from functools import partial
import math

import jax
import jax.numpy as jnp
from jax import lax
from jax.experimental import pallas as pl
from jax.experimental.pallas import tpu as pltpu
from jax.sharding import PartitionSpec as P

HEAD_DIM = 64
PAIR = 2 * HEAD_DIM
LONGEST = 256
BLOCK = 128
TINY = 8
PARTS = 12
ROWS = 256
MASKED = -1e30
F32 = jnp.float32
BF16 = jnp.bfloat16
GELU_C = math.sqrt(2.0 / math.pi)
GELU_A = 0.044715
BIG_LIMIT = 63 * 1024 * 1024
LIMITS = {"backward_sent_0": 30, "backward_sent_1": 30, "backward_own_0": 30, "backward_own_1": 30, "output": 63, "tokens": 63, "final_feed_0": 63, "final_feed_1": 63, "final_attention": 63}
WEIGHTS = {"backward_own": 80.0, "output": 80.0}
SMALL_LIMIT = 8 * 1024 * 1024
SMEM = pl.BlockSpec(memory_space=pltpu.SMEM)
VMEM = pl.BlockSpec(memory_space=pltpu.VMEM)
WHERE_IT_IS = pl.BlockSpec(memory_space=pl.ANY)
HBM = pl.BlockSpec(memory_space=pltpu.HBM)


def dot_nn(a, b):
    return lax.dot_general(a, b, (((1,), (0,)), ((), ())), preferred_element_type=F32)


def dot_nt(a, b):
    return lax.dot_general(a, b, (((1,), (1,)), ((), ())), preferred_element_type=F32)


def dot_tn(a, b):
    return lax.dot_general(a, b, (((0,), (0,)), ((), ())), preferred_element_type=F32)


def shape(dims, dtype=F32):
    return jax.ShapeDtypeStruct(tuple(dims), dtype)


class Take:
    def __init__(self, dims, dtype, copies, held=False):
        self.dims, self.dtype, self.copies, self.held = tuple(dims), dtype, copies, held
        self.late = False


def later(one):
    one.late = True
    return one


def take(array, index=None, dims=None):
    return Take(dims or array.shape, array.dtype, [(array, index, None)], True)


def fetch(array, index=None, dims=None):
    return Take(dims or array.shape, array.dtype, [(array, index, None)])


class Coming:
    def __init__(self, buffer, copies, late=False):
        self.buffer, self.copies, self.waiting = buffer, copies, late
        if not late:
            for copy in copies:
                copy.start()

    def start(self):
        if self.waiting:
            for copy in self.copies:
                copy.start()
        self.waiting = False

    def __call__(self):
        self.start()
        for copy in self.copies:
            copy.wait()
        self.copies = []
        return self.buffer


class Going:
    def __init__(self, target, buffer, sems):
        self.target, self.buffer, self.sems, self.copies = target, buffer, sems, []

    def __setitem__(self, index, value):
        self.buffer[index] = value

    def __getitem__(self, index):
        return self.buffer[index]

    def part(self, *index):
        copy = pltpu.make_async_copy(self.buffer.at[index], self.target.at[index], self.sems[len(self.copies)])
        copy.start()
        self.copies.append(copy)

    def send(self):
        if self.target is not None and not self.copies:
            copy = pltpu.make_async_copy(self.buffer, self.target, self.sems[0])
            copy.start()
            self.copies.append(copy)


def part_swapped(swap, one, two, one_index, two_index):
    straight, crossed = [], []
    for a, b, index in ((one, two, one_index), (two, one, two_index)):
        sem = a.sems[len(a.copies)]
        straight.append(pltpu.make_async_copy(a.buffer.at[index], a.target.at[index], sem))
        crossed.append(pltpu.make_async_copy(a.buffer.at[index], b.target.at[index], sem))

    @pl.when(swap)
    def _():
        for copy in crossed:
            copy.start()

    @pl.when(jnp.logical_not(swap))
    def _():
        for copy in straight:
            copy.start()

    one.copies.append(straight[0])
    two.copies.append(straight[1])


def pick(ref, index, scalars):
    if index is None:
        return ref
    return ref.at[index(*scalars) if callable(index) else index]


class Chain:
    def __init__(self):
        self.last = None

    def call(self, kernel, name, scalars, takes, outs, scratch=(), leaves=False, weight=None, passes=(), onto=()):
        arrays, spaces, spots = [], [], []

        def place(array, space):
            for i, (known, its) in enumerate(zip(arrays, spaces)):
                if known is array and its is space:
                    return i
            arrays.append(array)
            spaces.append(space)
            return len(arrays) - 1

        fetched = [one for one in takes if not one.held]
        views = []
        for one in takes:
            if one.held:
                views.append((place(one.copies[0][0], VMEM), one.copies[0][1]))
            else:
                spots.append([(place(a, HBM), s, t) for a, s, t in one.copies])
        after = [] if self.last is None else [self.last]
        n_scalar, n_array, n_out = len(scalars), len(arrays), len(outs)
        n_copies = sum(len(one) for one in spots)

        def body(*refs):
            numbers, refs = refs[:n_scalar], refs[n_scalar:]
            given, refs = refs[:n_array], refs[n_array + len(after) + len(passes) + len(onto) :]
            results, refs = refs[:n_out], refs[n_out + len(passes) :]
            sems, refs = refs[0], refs[1:]
            into, refs = refs[: len(fetched)], refs[len(fetched) :]
            outof, rest = (refs[:n_out], refs[n_out:]) if leaves else (results, refs)
            at = 0
            buffers = []
            for one, buffer, copies in zip(fetched, into, spots):
                listed = []
                for which, source, target in copies:
                    listed.append(
                        pltpu.make_async_copy(
                            pick(given[which], source, numbers), pick(buffer, target, numbers), sems.at[at]
                        )
                    )
                    at += 1
                buffers.append(Coming(buffer, listed, one.late))
            left, seen, coming = list(buffers), list(views), []
            for one in takes:
                if one.held:
                    which, index = seen.pop(0)
                    coming.append(Coming(pick(given[which], index, numbers), []))
                else:
                    coming.append(left.pop(0))
            going = [
                Going(result if leaves else None, buffer, [sems.at[at + PARTS * i + j] for j in range(PARTS)])
                for i, (result, buffer) in enumerate(zip(results, outof))
            ]
            kernel(*numbers, *coming, *going, *rest)
            for one in coming:
                one()
            for one in going:
                one.send()
            for one in going:
                for copy in one.copies:
                    copy.wait()

        body.__name__ = name
        out = pl.pallas_call(
            body,
            in_specs=[SMEM] * n_scalar + spaces + [WHERE_IT_IS] * len(after) + [HBM] * (len(passes) + len(onto)),
            out_specs=[HBM if leaves else VMEM] * n_out + [HBM] * len(passes),
            out_shape=list(outs) + [shape(one.shape, one.dtype) for one in passes],
            input_output_aliases={
                n_scalar + n_array + len(after) + i: (n_out + i if i < len(passes) else i - len(passes))
                for i in range(len(passes) + len(onto))
            },
            scratch_shapes=[pltpu.SemaphoreType.DMA((n_copies + PARTS * n_out,))]
            + [pltpu.VMEM(one.dims, one.dtype) for one in fetched]
            + [pltpu.VMEM(o.shape, o.dtype) for o in outs if leaves]
            + list(scratch),
            compiler_params=pltpu.CompilerParams(vmem_limit_bytes=LIMITS.get(name, BIG_LIMIT >> 20) << 20 if leaves else SMALL_LIMIT),
            cost_estimate=pl.CostEstimate(flops=int(1e9 * (WEIGHTS.get(name, 17.0 if leaves else 0.0) if weight is None else weight)) + 1000, bytes_accessed=1000, transcendentals=0),
            name=name,
        )(*scalars, *arrays, *after, *passes, *onto)
        self.last = out[0]
        return out


def window(first, length):
    return max(0, first - LONGEST), min(length, first + BLOCK + LONGEST)


class Weights:
    def __init__(self, wq, wk, wv, bq, bv, wo):
        self.projections, self.biases, self.wo = (wq, wk, wv), (bq, bv), wo

    def cut(self, p, n=1):
        if callable(p):
            return lambda *numbers: pl.ds(pl.multiple_of(p(*numbers) * PAIR, PAIR), n * PAIR)
        return lambda *numbers: slice(p * PAIR, (p + n) * PAIR)

    def triple(self, p):
        d = self.wo.shape[1]
        cut = self.cut(p)
        return Take(
            (d, 3 * PAIR), BF16,
            [
                (a, lambda *n: (slice(None), cut(*n)), (slice(None), slice(i * PAIR, (i + 1) * PAIR)))
                for i, a in enumerate(self.projections)
            ],
        )

    def out(self, p, n=1):
        d = self.wo.shape[1]
        cut = self.cut(p, n)
        return Take((n * PAIR, d), BF16, [(self.wo, lambda *k: (cut(*k), slice(None)), None)])

    def bias(self):
        bq, bv = self.biases
        half = bq.shape[1]
        return Take(
            (1, 2 * half), F32,
            [(bq, None, (slice(None), slice(0, half))), (bv, None, (slice(None), slice(half, 2 * half)))],
        )


class SentWeights:
    def __init__(self, pack):
        self.pack, self.d = pack, pack.shape[1]

    def cut(self, p, base, n=1):
        def index(*numbers):
            if callable(p):
                return pl.ds(pl.multiple_of(base + p(*numbers) * PAIR, PAIR), n * PAIR)
            return slice(base + p * PAIR, base + (p + n) * PAIR)

        return index

    def triple(self, p):
        d, half = self.d, self.d // 2
        copies = []
        for i, (rows, base) in enumerate(((slice(0, d), 0), (slice(0, d), half), (slice(d, 2 * d), 0))):
            cut = self.cut(p, base)
            copies.append(
                (self.pack, lambda *n, rows=rows, cut=cut: (rows, cut(*n)), (slice(None), slice(i * PAIR, (i + 1) * PAIR)))
            )
        return Take((d, 3 * PAIR), F32, copies)

    def out(self, p, n=1):
        d, half = self.d, self.d // 2
        copies = []
        for i in range(2):
            cut = self.cut(p, d + i * half, n)
            copies.append(
                (self.pack, lambda *k, cut=cut: (cut(*k), slice(half, d)), (slice(None), slice(i * half, (i + 1) * half)))
            )
        return Take((n * PAIR, d), F32, copies)

    def bias(self):
        d = self.d
        return fetch(self.pack, (slice(2 * d, 2 * d + TINY), slice(None)), (TINY, d))


def pack_kernel(wq, wk, wv, wo, bq, bv, bi, w_inner, w_outer, out, inner_out, outer_out):
    d, half = wq.buffer.shape
    out[0:d, :half] = wq()[...].astype(F32)
    out[0:d, half:] = wk()[...].astype(F32)
    out.part(slice(0, d))
    out[d : 2 * d, :half] = wv()[...].astype(F32)
    out[d : d + half, half:] = wo()[:, :half].astype(F32)
    out[d + half : 2 * d, half:] = wo()[:, half:].astype(F32)
    out[2 * d : 2 * d + 1, :half] = bq()[...]
    out[2 * d : 2 * d + 1, half:] = bv()[...]
    out[2 * d + 1 : 2 * d + 2, :] = bi()[:, :d]
    out[2 * d + 2 : 2 * d + 3, :] = bi()[:, d:]
    out[2 * d + 3 :, :] = jnp.zeros((TINY - 3, d), F32)
    out.part(slice(d, 2 * d + TINY))
    for ref, result in ((w_inner, inner_out), (w_outer, outer_out)):
        rows = ref.buffer.shape[0] // 2
        for i in range(2):
            cut = slice(i * rows, (i + 1) * rows)
            result[cut, :] = ref()[cut, :].astype(F32)
            result.part(cut)


def row_index(other):
    return lambda core, *_: 1 - core[0] if other else core[0]


def row_of(array, other):
    return Take(array.shape[1:], array.dtype, [(array, row_index(other), None)])


def segments_of(place, fill_ref, seg, cols_ref):
    length = cols_ref.shape[0]
    fill = fill_ref[place]
    row = seg()[pl.ds(place, 1), :].astype(F32)
    places = lax.broadcasted_iota(jnp.int32, (1, length), 1)
    valid = places < fill
    keyed = jnp.where(valid, row, -1.0)
    cols_ref[...] = jnp.broadcast_to(keyed, (PAIR, length)).T
    return row, jnp.where(valid, 1.0, 0.0)


def mask_for(cols_ref, row, low, high, first):
    once = cols_ref[low:high, :] == row[:, first : first + BLOCK]
    return jnp.concatenate([once, once], axis=1)


def two_heads(array):
    lanes = lax.broadcasted_iota(jnp.int32, array.shape, 1)
    return jnp.where(lanes < HEAD_DIM, array, 0), jnp.where(lanes < HEAD_DIM, 0, array)


def stacked(pair, first):
    return jnp.concatenate([half[first : first + BLOCK] for half in pair], axis=0)


def staged(items, one, two, three):
    items = list(items)
    ones, twos = {}, {}
    for i in range(len(items) + 2):
        if i < len(items):
            ones[i] = one(items[i])
        if 0 <= i - 1 < len(items):
            twos[i - 1] = two(items[i - 1], *ones.pop(i - 1))
        if 0 <= i - 2:
            three(items[i - 2], *twos.pop(i - 2))


def forward_pair(p, x, w3, bias, row, valid, cols, qkv, mixed_out, lse):
    length = x.shape[0]
    half = bias.shape[1] // 2
    y = dot_nn(x, w3)
    at = p * PAIR
    q = y[:, :PAIR] + bias[0:1, at : at + PAIR]
    q = (q.astype(BF16) * 0.125).astype(BF16)
    k = y[:, PAIR : 2 * PAIR].astype(BF16)
    v = (y[:, 2 * PAIR :] + bias[0:1, half + at : half + at + PAIR]).astype(BF16)
    vt = v.T
    qkv[0] = q
    qkv[1] = k
    qkv[2] = v
    heads = two_heads(q)

    def scores(first):
        low, high = window(first, length)
        return (dot_nt(k[low:high], stacked(heads, first)),)

    def weigh(first, s):
        low, high = window(first, length)
        s = jnp.where(mask_for(cols, row, low, high, first), s, MASKED)
        peak = jnp.max(s, axis=0, keepdims=True)
        e = jnp.exp(s - peak)
        total = jnp.sum(e, axis=0, keepdims=True)
        lse[0:1, 2 * first : 2 * first + 2 * BLOCK] = peak + jnp.log(total)
        return e.astype(BF16), total

    def mix(first, e, total):
        low, high = window(first, length)
        block = slice(first, first + BLOCK)
        o = dot_nn(vt[:, low:high], e)
        keep = valid[:, block]
        mixed_out[:HEAD_DIM, block] = (o[:HEAD_DIM, :BLOCK] * (keep / total[:, :BLOCK])).astype(BF16)
        mixed_out[HEAD_DIM:, block] = (o[HEAD_DIM:, BLOCK:] * (keep / total[:, BLOCK:])).astype(BF16)

    staged(range(0, length, BLOCK), scores, weigh, mix)


def start_all(*ones):
    for one in ones:
        one.start()


def forward_pairs(x, w3s, bias, row, valid, cols, qkv, mixed, lse):
    for p, w3 in enumerate(w3s):
        forward_pair(
            p, x, w3()[...].astype(BF16), bias(), row, valid, cols, qkv.buffer.at[p], mixed.buffer.at[p], lse.buffer.at[p]
        )
        qkv.part(p)
        mixed.part(p)
        lse.part(p)


def forward_own_kernel(core_ref, fill_ref, seg, x_in, w3_0, bias, w3_1, qkv, mixed, lse, cols):
    row, valid = segments_of(core_ref[0], fill_ref, seg, cols)
    x = x_in()[...]
    w3_0()
    start_all(w3_1)
    forward_pairs(x, (w3_0, w3_1), bias, row, valid, cols, qkv, mixed, lse)


def all_units(low, lowt, d_ffn, wi, bias_of, wo, grads, bias_out, hidden_out, pre_out):
    units = wi().shape[1]
    part, step = units // 2, 256

    def products(at):
        i, inside = divmod(at, part)
        cut, held = slice(at, at + step), slice(inside, inside + step)
        pre = dot_nn(low, wi()[:, cut].astype(BF16)) + bias_of(i, held)
        return pre, dot_nt(d_ffn, wo()[cut, :].astype(BF16))

    def bend(at, pre, d_hidden):
        square = pre * pre
        t = jnp.tanh(pre * (GELU_C + (GELU_C * GELU_A) * square))
        cdf = 0.5 + 0.5 * t
        hidden = (pre * cdf).astype(BF16)
        slope = cdf + (0.5 * pre) * (1.0 - t * t) * (GELU_C + (3.0 * GELU_C * GELU_A) * square)
        d_pre = (d_hidden * slope).astype(BF16)
        i, inside = divmod(at, part)
        bias_out[i : i + 1, inside : inside + step] = jnp.sum(d_pre.astype(F32), axis=0, keepdims=True)
        return hidden, d_pre

    def gather(at, hidden, d_pre):
        i, inside = divmod(at, part)
        cut, held = slice(at, at + step), slice(inside, inside + step)
        hidden_out[:, cut] = hidden
        pre_out[:, cut] = d_pre
        grads[i][held, :] = dot_tn(hidden, d_ffn)
        grads[i][part:, held] = dot_nn(lowt, d_pre)
        if inside + step == part:
            grads[i].send()

    staged(range(0, units, step), products, bend, gather)


def middle_kernel(core_ref, fill_ref, gate, feed_gate, seg, x_in, w3_0, bias, w3_1, wo, mixed_own, wo_own, out_bias,
                  cot, wi, w_outer, qkv, mixed, lse, mid, low_out, grad_0, grad_1, bias_out, hidden_out, pre_out, cols):
    row, valid = segments_of(core_ref[0], fill_ref, seg, cols)
    x = x_in()[...]
    w3_0()
    start_all(w3_1, wo, mixed_own, wo_own, out_bias, cot, wi, w_outer)
    forward_pairs(x, (w3_0, w3_1), bias, row, valid, cols, qkv, mixed, lse)
    for at in range(0, x.shape[0], ROWS):
        rows = slice(at, at + ROWS)
        branch = out_bias()[...]
        for p in range(2):
            cut = slice(p * PAIR, (p + 1) * PAIR)
            branch = branch + dot_tn(mixed_own()[p, :, rows], wo_own()[cut, :])
            branch = branch + dot_tn(mixed[p, :, rows], wo()[cut, :].astype(BF16))
        value = x[rows].astype(F32) + gate[0] * branch
        mid[rows, :] = value
        mid.part(rows)
        low_out[rows, :] = value.astype(BF16)
        low_out.part(rows)
    low = low_out[...]
    d_ffn = (feed_gate[0] * cot()[...].astype(F32)).astype(BF16)
    bias_out[...] = jnp.zeros(bias_out.buffer.shape, F32)
    all_units(
        low, low.T, d_ffn, wi, lambda i, cut: bias()[1 + i : 2 + i, cut], w_outer, (grad_0, grad_1), bias_out,
        hidden_out, pre_out,
    )


def feed_kernel(core_ref, gate, feed_gate, low_in, wi, bi, cot_in, w_outer, hidden_sent, pre_sent, wi_sent, wo_sent,
                out_bias, mid, x, grad_0, grad_1, out, dmid_out, dbranch_out, small, bias_out, hidden_out, pre_out):
    low = low_in()[...]
    length, d = low.shape
    wi()
    start_all(cot_in, w_outer)
    lowt = low.T
    cot = cot_in()[...].astype(F32)
    d_ffn = (feed_gate[0] * cot).astype(BF16)
    w_outer()
    start_all(hidden_sent, pre_sent, wi_sent, wo_sent, out_bias, mid, x)
    bias_out[...] = jnp.zeros_like(bias_out)
    part = d
    all_units(
        low, lowt, d_ffn, wi, lambda i, cut: bi()[:, i * part : (i + 1) * part][:, cut], w_outer, (grad_0, grad_1),
        bias_out, hidden_out, pre_out,
    )
    wi_other = wi_sent()[...].astype(BF16)
    wo_other = wo_sent()[...].astype(BF16)
    sums = [jnp.zeros((1, d), F32)] * 3
    for at in range(0, length, ROWS):
        rows = slice(at, at + ROWS)
        seen = cot_in()[rows, :].astype(F32)
        dmid = dot_nt(pre_sent()[rows, :], wi_other) + dot_nt(pre_out[rows, :], wi()[...]) + seen
        ffn = dot_nn(hidden_sent()[rows, :], wo_other) + dot_nn(hidden_out[rows, :], w_outer()[...]) + out_bias()[...]
        dmid_out[rows, :] = dmid
        dmid_out.part(rows)
        dbranch = (gate[0] * dmid).astype(BF16)
        dbranch_out[rows, :] = dbranch
        dbranch_out.part(rows)
        middle = mid()[rows, :]
        out[rows, :] = middle + feed_gate[0] * ffn
        out.part(rows)
        branch = middle - x()[rows, :].astype(F32)
        for i, value in enumerate((dbranch.astype(F32), dmid * branch, seen * ffn)):
            sums[i] = sums[i] + jnp.sum(value, axis=0, keepdims=True)
    small[...] = jnp.zeros(small.buffer.shape, F32)
    small[1:3, :] = bias_out[0:2, :]
    small[3:4, :] = sums[0]
    small[4:5, :] = jnp.sum(d_ffn.astype(F32), axis=0, keepdims=True)
    small[5:6, :] = sums[1] / gate[0]
    small[6:7, :] = sums[2]


def join_kernel(bit, a, a_came, b, b_came, keep, send):
    rows = keep.buffer.shape[0] // 2
    start_all(a, a_came, b, b_came)
    for i in range(2):
        cut = slice(i * rows, (i + 1) * rows)
        keep[cut, :] = a()[cut, :] + a_came()[cut, :]
        send[cut, :] = b()[cut, :] + b_came()[cut, :]
        part_swapped(bit[0] != 0, keep, send, (cut,), (cut,))


def backward_pair(dbranch, do, qkv, lse, mixed, x, row, cols, dk_acc, dv_acc, dqt, grad_out):
    length, d = dbranch.shape
    q, k, v = qkv[0], qkv[1], qkv[2]
    kt = k.T
    qs = two_heads(q)
    dos = two_heads(do)
    dk_acc[...] = jnp.zeros_like(dk_acc)
    dv_acc[...] = jnp.zeros_like(dv_acc)

    def products(first):
        low, high = window(first, length)
        qq, dd = stacked(qs, first), stacked(dos, first)
        return qq, dd, dot_nt(k[low:high], qq), dot_nt(v[low:high], dd)

    def weigh(first, qq, dd, s, dw):
        low, high = window(first, length)
        s = jnp.where(mask_for(cols, row, low, high, first), s, MASKED)
        w = jnp.exp(s - lse[0:1, 2 * first : 2 * first + 2 * BLOCK])
        both = w * dw
        mean = jnp.sum(both, axis=0, keepdims=True)
        return qq, dd, w.astype(BF16), (both - w * mean).astype(BF16)

    def gather(first, qq, dd, w, ds):
        low, high = window(first, length)
        block = slice(first, first + BLOCK)
        dv_acc[low:high, :] += dot_nn(w, dd)
        dk_acc[low:high, :] += dot_nn(ds, qq)
        dq = dot_nn(kt[:, low:high], ds)
        dqt[:HEAD_DIM, block] = dq[:HEAD_DIM, :BLOCK]
        dqt[HEAD_DIM:, block] = dq[HEAD_DIM:, BLOCK:]

    staged(range(0, length, BLOCK), products, weigh, gather)
    dq = (0.125 * dqt[...]).T.astype(BF16)
    all3 = jnp.concatenate([dq, dk_acc[...].astype(BF16), dv_acc[...].astype(BF16)], axis=1)
    grad_out[:, : 3 * PAIR] = dot_tn(x, all3)
    out_grad = dot_nn(mixed, dbranch)
    for c in range(d // PAIR):
        cut = slice(c * PAIR, (c + 1) * PAIR)
        grad_out[cut, 3 * PAIR :] = out_grad[:, cut]
    return all3


def bias_sums(all3):
    sums = jnp.sum(all3.astype(F32), axis=0, keepdims=True)
    return jnp.concatenate([sums[:, :PAIR], sums[:, 2 * PAIR :]], axis=1)


def masked_heads(dbranch, wo, fill):
    places = lax.broadcasted_iota(jnp.int32, (dbranch.shape[0], 1), 0)
    return jnp.where(places < fill, dot_nt(dbranch, wo), 0.0).astype(BF16)


def backward_kernel(sent, last, core_ref, fill_ref, pair, *refs):
    if sent and not last:
        bit, *refs = refs
    seg, dbranch_in, wo, x_in, qkv, lse, mixed, *refs = refs
    late = []
    if last:
        w3, all3_in, w3_before, total_in, *refs = refs
        late += [w3, all3_in, w3_before, total_in]
    if sent:
        if last:
            bias_in, *refs = refs
            late.append(bias_in)
        else:
            parts, refs = refs[:4], refs[4:]
            late += parts
    else:
        came, *refs = refs
        late.append(came)
    small_in, *refs = refs
    late.append(small_in)
    if last:
        grad_out, small_out, total_out, *rest = refs
    else:
        grad_out, small_out, all3_out, *rest = refs
        if sent:
            keep, send, *rest = rest
    cols, dk_acc, dv_acc, dqt = rest
    row, _ = segments_of(core_ref[0], fill_ref, seg, cols)
    dbranch = dbranch_in()[...]
    length, d = dbranch.shape
    do = masked_heads(dbranch, wo()[...].astype(BF16), fill_ref[core_ref[0]])
    x = x_in()[...]
    qkv()
    start_all(*late)
    grads = grad_out.buffer.at[0:d]
    all3 = backward_pair(dbranch, do, qkv(), lse(), mixed()[...], x, row, cols, dk_acc, dv_acc, dqt, grads)
    small_out[...] = small_in()[...]
    if sent and last:
        small_out[1:3, :] = bias_in()[0:2, :]
    if not sent:
        grads[...] += came()[0:d, :]
    spot = pl.ds(pl.multiple_of(pair[0] * 2 * PAIR, PAIR), 2 * PAIR)
    if sent and not last:
        small_out[0:1, spot] = bias_sums(all3)
    else:
        small_out[0:1, spot] += bias_sums(all3)
    if last and not sent:
        small_out[...] += came()[d:, :]
    if last and sent:
        grad_out[d:, :] = small_out[...]
    grad_out.send()
    if last:
        for at in range(0, length, ROWS):
            rows = slice(at, at + ROWS)
            total = dot_nt(all3_in()[rows, :], w3_before()[...].astype(BF16)) + dot_nt(all3[rows], w3()[...].astype(BF16))
            total_out[rows, :] = total_in()[rows, :] + total
            total_out.part(rows)
    else:
        all3_out[...] = all3
        if sent:
            join_kernel(bit, *parts, keep, send)


def attention_scratch(length):
    return [pltpu.VMEM((length, PAIR), F32)] * 3 + [pltpu.VMEM((PAIR, length), F32)]


def place_in(refs, mask):
    at = 0
    for ref in refs:
        at = 2 * at + ref[0]
    return jnp.bitwise_xor(at, mask)


def sum_of(terms, cut):
    total = terms[0]()[cut, :]
    for one in terms[1:]:
        total = total + one()[cut, :]
    return total


class Stream:
    def __init__(self, chain, members, bits, send, out, back):
        self.chain, self.members, self.bits = chain, members, bits
        self.out, self.back = list(out), list(back)
        self.group = [0]
        self.came = [self.travel(send, 1)]
        self.tail, self.small, self.turned, self.lanes = 0, None, False, 1

    def keep(self, mine, small=None):
        self.mine, self.small = mine, small
        self.rows, self.width = mine.shape
        self.joined = []

    def join(self, other):
        self.joined = [other]

    def travel(self, array, mask):
        pairs = []
        for place in range(self.members):
            for core in range(2):
                partner = place
                for i, step in enumerate(reversed(self.group)):
                    if mask >> i & 1:
                        partner ^= 1 << (step ^ core if step < 2 else step)
                pairs.append((place * 2 + core, partner * 2 + core))
        return lax.ppermute(array, ("dp", "mp"), pairs)

    def call(self, kernel, name, group, outs, small=False):
        takes = [take(one) for stream in (self, *self.joined) for one in (stream.mine, *stream.came)]
        takes += [take(self.small)] if small else []
        results = self.chain.call(
            kernel, name, [self.bits[step] for step in group], takes, [shape(dims) for dims in outs],
            weight=self.weight, passes=self.passes,
        )
        self.passes = results[len(outs) :]
        return results[: len(outs)]

    def halve(self):
        group = self.out.pop(0)
        parts, n_terms = 1 << len(group), 1 + len(self.came)
        whole, tail = self.rows, self.tail
        rows = whole // parts
        begins = self.small is not None and not tail
        sources = 1 + len(self.joined)
        lanes = self.lanes = max(self.lanes, sources)

        def kernel(*refs):
            bits, refs = refs[: len(group)], refs[len(group) :]
            terms = [refs[i * n_terms : (i + 1) * n_terms] for i in range(sources)]
            refs = refs[sources * n_terms :]
            if begins:
                both = refs[0]()[...]
                refs = refs[1:]
            elif tail:
                both = sum_of(terms[0], slice(lanes * whole, lanes * whole + tail))
            for mask, out in enumerate(refs):
                at = place_in(bits, mask) * rows
                for lane in range(lanes):
                    source, base = (lane, 0) if sources > 1 else (0, lane * whole)
                    cut = pl.ds(pl.multiple_of(base + at, 8), rows)
                    out[lane * rows : (lane + 1) * rows, :] = sum_of(terms[source], cut)
                if begins or tail:
                    out[lanes * rows :, :] = both

        if begins:
            self.tail = TINY
        self.mine, *sends = self.call(
            kernel, "halve", group, [(lanes * rows + self.tail, self.width)] * parts, begins
        )
        self.joined = []
        self.group = group
        self.came = [self.travel(send, mask + 1) for mask, send in enumerate(sends)]
        self.rows = rows

    def turn(self):
        rows, tail = self.lanes * self.rows, self.tail
        n_came = len(self.came)

        def kernel(mine, *refs):
            came, refs = refs[:n_came], refs[n_came:]
            total = mine()[...]
            for one in came:
                total = total + one()[...]
            refs[0][...] = total[:rows]
            if tail:
                refs[1][...] = total[rows:]

        outs = [(rows, self.width)] + ([(TINY, self.width)] if tail else [])
        self.mine, *tiny = self.call(kernel, "turn", [], outs)
        self.small = tiny[0] if tiny else None
        self.turned = True
        self.spread()

    def double(self):
        rows, lanes = self.rows, self.lanes
        parts = len(self.came) + 1
        ends = len(self.back) == 1 and self.small is not None
        group = self.group

        def kernel(*refs):
            bits, refs = refs[: len(group)], refs[len(group) :]
            have, refs = refs[:parts], refs[parts:]
            out = refs[-1]
            if ends:
                out[lanes * parts * rows :, :] = refs[0]()[...]
            for mask, one in enumerate(have):
                at = place_in(bits, mask) * rows
                for lane in range(lanes):
                    cut = pl.ds(pl.multiple_of(lane * parts * rows + at, 8), rows)
                    out[cut, :] = one()[lane * rows : (lane + 1) * rows, :]

        self.rows = parts * rows
        (self.mine,) = self.call(
            kernel, "double", group, [(lanes * self.rows + (TINY if ends else 0), self.width)], ends
        )
        self.spread()

    def spread(self):
        self.group = self.back.pop(0)
        self.came = [self.travel(self.mine, mask) for mask in range(1, 1 << len(self.group))]

    def advance(self, weight=0.0, passes=()):
        self.weight, self.passes = weight, passes
        if self.out:
            self.halve()
        elif not self.turned:
            self.turn()
        elif self.back:
            self.double()
        return self.passes

    def done(self):
        return self.turned and not self.back


def in_order(bit, mine, came, low, high):
    @pl.when(bit[0] == 0)
    def _():
        low(mine())
        high(came())

    @pl.when(bit[0] != 0)
    def _():
        low(came())
        high(mine())


def final_feed(chain, stream, index, d, onto=()):
    units = stream.rows
    cut = slice(index * units, (index + 1) * units)

    def kernel(bit, mine, came, inner, outer):
        mine()
        came()

        def low(ref):
            outer[cut, :] = ref[...]

        def high(ref):
            inner[:, cut] = ref[...]

        in_order(bit, mine, came, low, high)
        outer.part(cut)
        inner.part(slice(None), cut)

    return chain.call(
        kernel, "final_feed_%d" % index, [stream.bits[0]], [fetch(stream.mine), fetch(stream.came[0])],
        [shape((d, 2 * units)), shape((2 * units, d))], leaves=True, onto=onto,
    )


def final_attention(chain, third, d):
    half = d // 2

    def kernel(bit, mine, came, gq, gk, gv, go, gqb, gvb, gob, gib, goutb, gates):
        small = mine()[d:, :] + came()[d:, :]
        for p in range(2):
            cut = slice(p * PAIR, (p + 1) * PAIR)
            gqb[:, cut] = small[0:1, 2 * p * PAIR : (2 * p + 1) * PAIR]
            gvb[:, cut] = small[0:1, (2 * p + 1) * PAIR : (2 * p + 2) * PAIR]
        gib[:, :d] = small[1:2, :]
        gib[:, d:] = small[2:3, :]
        gob[...] = small[3:4, :]
        goutb[...] = small[4:5, :]
        gates[...] = jnp.broadcast_to(jnp.sum(small, axis=1, keepdims=True), gates.buffer.shape)

        def place(p, ref):
            cut = slice(p * PAIR, (p + 1) * PAIR)
            gq[:, cut] = ref[:d, :PAIR]
            gk[:, cut] = ref[:d, PAIR : 2 * PAIR]
            gv[:, cut] = ref[:d, 2 * PAIR : 3 * PAIR]
            for c in range(d // PAIR):
                across = slice(c * PAIR, (c + 1) * PAIR)
                go[cut, across] = ref[across, 3 * PAIR :]

        in_order(bit, mine, came, partial(place, 0), partial(place, 1))

    return chain.call(
        kernel, "final_attention", [third.bits[0]], [take(third.mine), take(third.came[0])],
        [shape((d, half))] * 3
        + [shape((half, d)), shape((1, half)), shape((1, half)), shape((1, d)), shape((1, 2 * d)), shape((1, d)), shape((TINY, PAIR))],
        leaves=True,
    )


def rows_kernel(core_ref, own, came, out):
    out[core_ref[0]] = own()[...].astype(out.buffer.dtype)
    out.part(core_ref[0])
    out[1 - core_ref[0]] = came()[...].astype(out.buffer.dtype)
    out.part(1 - core_ref[0])


def shards(members, tokens, segment_ids, row_fill, query_weight, query_bias, key_weight,
           value_weight, value_bias, out_weight, out_bias, attention_gate, inner_weight,
           inner_bias, outer_weight, outer_bias, feed_gate, cotangent):
    _, length, d = tokens.shape
    half = d // 2
    place = lax.axis_index("dp")
    core_id = lax.axis_index("mp")
    core = core_id.astype(jnp.int32).reshape(1)
    bits = []
    for step in range(members.bit_length() - 1):
        bit = (place >> (step ^ core_id if step < 2 else step)) & 1
        bits.append(bit.astype(jnp.int32).reshape(1))
    not_mine = 1 - bits[0]
    chain = Chain()

    def across(array):
        return lax.ppermute(array, "mp", [(0, 1), (1, 0)])

    def as_row(array):
        return array.reshape(1, -1)

    def own_row(array):
        return row_of(array, False)

    a_gate = attention_gate.reshape(1)
    f_gate = feed_gate.reshape(1)
    qb, vb, ib, ob, fb = (as_row(a) for a in (query_bias, value_bias, inner_bias, out_bias, outer_bias))
    own = Weights(query_weight, key_weight, value_weight, qb, vb, out_weight)
    seg = fetch(segment_ids)
    cols = [pltpu.VMEM((length, PAIR), F32)]
    units = inner_weight.shape[1]

    pack, wi, wo = chain.call(
        pack_kernel, "pack", [],
        [fetch(a) for a in (query_weight, key_weight, value_weight, out_weight, qb, vb, ib, inner_weight, outer_weight)],
        [shape((2 * d + TINY, d)), shape((d, units)), shape((units, d))], leaves=True,
    )
    pack_came, wi_came, wo_came = across(pack), across(wi), across(wo)
    sent = SentWeights(pack_came)

    pair_outs = [shape((2, 3, length, PAIR), BF16), shape((2, PAIR, length), BF16), shape((2, TINY, 2 * length))]
    qkv_a, mixed_a, lse_a = chain.call(
        forward_own_kernel, "forward_own", [core, row_fill],
        [seg, own_row(tokens), own.triple(0), own.bias(), later(own.triple(1))], pair_outs, cols, leaves=True,
    )
    unit_outs = [shape((length, units), BF16)] * 2
    grad_outs = [shape((2 * d, d))] * 2
    qkv_b, mixed_b, lse_b, mid, low, g_sent_0, g_sent_1, bias_b, hidden_b, pre_b = chain.call(
        middle_kernel, "middle", [core, row_fill, a_gate, f_gate],
        [seg, own_row(tokens), sent.triple(0), sent.bias()]
        + [
            later(one)
            for one in (
                sent.triple(1), sent.out(0, 2), fetch(mixed_a), own.out(0, 2), fetch(ob), own_row(cotangent),
                fetch(wi_came), fetch(wo_came),
            )
        ],
        pair_outs + [shape((length, d)), shape((length, d), BF16)] + grad_outs + [shape((TINY, d))] + unit_outs,
        cols, leaves=True,
    )
    g_came_0, g_came_1 = across(g_sent_0), across(g_sent_1)
    g_own_0, g_own_1, out_own, dmid, dbranch, small = chain.call(
        feed_kernel, "feed", [core, a_gate, f_gate],
        [fetch(low), fetch(inner_weight), fetch(ib)]
        + [
            later(one)
            for one in (
                own_row(cotangent), fetch(outer_weight), fetch(hidden_b), fetch(pre_b), fetch(wi_came), fetch(wo_came),
                fetch(fb), fetch(mid), own_row(tokens),
            )
        ],
        grad_outs + [shape((length, d))] * 2 + [shape((length, d), BF16), shape((TINY, d))],
        [pltpu.VMEM((TINY, d), F32)] + [pltpu.VMEM((length, units), BF16)] * 2, leaves=True,
    )

    wide = [[step for step in pair if step < len(bits)] for pair in ((i, i + 1) for i in range(2, len(bits), 2))]
    one_by_one = [[step] for step in range(len(bits))]
    direct = ([[1], *wide], [*wide[::-1], [1], [0]])
    plain = (one_by_one[1:], one_by_one[::-1])

    def halves(mine, came):
        return [fetch(one, (slice(i * d, (i + 1) * d), slice(None)), (d, d)) for i in range(2) for one in (mine, came)]

    def stream(send, ways):
        return Stream(chain, members, bits, send, *ways)

    other_bit = ((place >> (1 - core_id)) & 1).astype(jnp.int32).reshape(1)
    pair_of = lambda core, fill, pair, *_: pair[0]
    pair_before = lambda core, fill, pair, *_: 1 - pair[0]

    def backward(sent, last, pair, weights, kept, extra, small, outs, bit=None):
        qkv, mixed, lse = kept
        takes = [
            seg, fetch(dbranch), weights.out(pair_of), own_row(tokens), fetch(qkv, pair_of, (3, length, PAIR)),
            fetch(lse, pair_of, (TINY, 2 * length)), fetch(mixed, pair_of, (PAIR, length)),
        ]
        more = list(extra)
        if last:
            all3, total, *rest = more
            more = [weights.triple(pair_of), fetch(all3), weights.triple(pair_before), fetch(total), *rest]
        takes += [later(one) for one in [*more, fetch(small)]]
        return chain.call(
            partial(backward_kernel, sent, last), "backward_%s_%d" % ("sent" if sent else "own", last),
            [core, row_fill, pair] + ([bit] if bit is not None else []), takes, outs, attention_scratch(length),
            leaves=True,
        )

    keep, send = chain.call(
        join_kernel, "join", [bits[0]], halves(g_own_0, g_came_0), [shape((d, d))] * 2, leaves=True
    )
    first = stream(send, direct)
    first.keep(keep)
    square, row8, rows3 = shape((d, d)), shape((TINY, d)), shape((length, 3 * PAIR), BF16)
    kept_a, kept_b = (qkv_a, mixed_a, lse_a), (qkv_b, mixed_b, lse_b)
    g_0, small_b, all3, keep, send = backward(
        True, False, 1 - other_bit, sent, kept_b, halves(g_own_1, g_came_1), small, [square, row8, rows3, square, square],
        bit=bits[0],
    )
    second = stream(send, plain)
    second.keep(keep)
    g_came_first = across(g_0)
    first.advance(0.0)
    g_1, _, total = backward(
        True, True, other_bit, sent, kept_b, (all3, dmid, fetch(bias_b)), small_b,
        [shape((d + TINY, d)), row8, shape((length, d))],
    )
    g_came_last = across(g_1)
    first.advance(0.0)
    second.advance(0.0)
    send, small, all3 = backward(
        False, False, not_mine, own, kept_a, (fetch(g_came_first),), small, [square, row8, rows3]
    )
    third = stream(send, direct)
    first.advance(0.0)
    second.advance(0.0)
    keep, small, total = backward(
        False, True, bits[0], own, kept_a, (all3, total, fetch(g_came_last)), small,
        [square, row8, shape((length, d))],
    )
    third.keep(keep, small)
    third.advance()
    first.advance()
    second.advance(20.0)
    while third.out:
        third.advance()
    while not first.done():
        first.advance(20.0)
    third.advance(20.0)
    second.advance()
    grads = final_feed(chain, first, 0, d)
    (out_own,) = third.advance(passes=(out_own,))
    out_came = across(out_own)
    second.advance(20.0)
    while not third.done():
        (total,) = third.advance(passes=(total,))
        second.advance()
    total_came = across(total)
    (output,) = chain.call(
        rows_kernel, "output", [core], [fetch(out_own), fetch(out_came)], [shape((2, length, d), BF16)], leaves=True
    )
    while not second.done():
        second.advance()
    (grad_tokens,) = chain.call(
        rows_kernel, "tokens", [core], [fetch(total), fetch(total_came)], [shape((2, length, d))], leaves=True
    )
    gq, gk, gv, go, gqb, gvb, gob, gib, goutb, gates = final_attention(chain, third, d)
    inner_grad, outer_grad = final_feed(chain, second, 1, d, grads)
    return (
        output, grad_tokens, gq, gqb.reshape(-1), gk, gv, gvb.reshape(-1), go, gob.reshape(-1), gates[5, 0],
        inner_grad, gib.reshape(-1), outer_grad, goutb.reshape(-1), gates[6, 0],
    )


def solution(mesh):
    rows = P("dp", None, None)
    col = P(None, "mp")
    cut = P("mp")
    in_specs = (
        rows, P("dp", None), P("dp"), col, cut, col, col, cut, P("mp", None), P(), P(),
        col, cut, P("mp", None), P(), P(), rows,
    )
    out_specs = (
        rows, rows, col, cut, col, col, cut, P("mp", None), P(), P(), col, cut,
        P("mp", None), P(), P(),
    )
    return jax.shard_map(
        partial(shards, mesh.shape["dp"]), mesh=mesh, in_specs=in_specs, out_specs=out_specs,
        check_vma=False,
    )
```

```python
from functools import partial
import math

import jax
import jax.numpy as jnp
from jax import lax
from jax.experimental import pallas as pl
from jax.experimental.pallas import tpu as pltpu
from jax.sharding import PartitionSpec as P

HEAD_DIM = 64
PAIR = 2 * HEAD_DIM
LONGEST = 256
BLOCK = 128
TINY = 8
PARTS = 12
ROWS = 256
MASKED = -1e30
F32 = jnp.float32
BF16 = jnp.bfloat16
GELU_C = math.sqrt(2.0 / math.pi)
GELU_A = 0.044715
BIG_LIMIT = 63 * 1024 * 1024
LIMITS = {'backward_sent_0': 30, 'backward_sent_1': 30, 'backward_own_0': 30, 'backward_own_1': 30, 'output': 30, 'tokens': 63, 'final_feed_0': 63, 'final_feed_1': 63, 'final_attention': 63, 'join': 14}
WEIGHTS = {"backward_own": 80.0, "output": 80.0}
SMALL_LIMIT = 8 * 1024 * 1024
SMEM = pl.BlockSpec(memory_space=pltpu.SMEM)
VMEM = pl.BlockSpec(memory_space=pltpu.VMEM)
WHERE_IT_IS = pl.BlockSpec(memory_space=pl.ANY)
HBM = pl.BlockSpec(memory_space=pltpu.HBM)


def dot_nn(a, b):
    return lax.dot_general(a, b, (((1,), (0,)), ((), ())), preferred_element_type=F32)


def dot_nt(a, b):
    return lax.dot_general(a, b, (((1,), (1,)), ((), ())), preferred_element_type=F32)


def dot_tn(a, b):
    return lax.dot_general(a, b, (((0,), (0,)), ((), ())), preferred_element_type=F32)


def shape(dims, dtype=F32):
    return jax.ShapeDtypeStruct(tuple(dims), dtype)


class Take:
    def __init__(self, dims, dtype, copies, held=False):
        self.dims, self.dtype, self.copies, self.held = tuple(dims), dtype, copies, held
        self.late = False


def later(one):
    one.late = True
    return one


def take(array, index=None, dims=None):
    return Take(dims or array.shape, array.dtype, [(array, index, None)], True)


def fetch(array, index=None, dims=None):
    return Take(dims or array.shape, array.dtype, [(array, index, None)])


class Coming:
    def __init__(self, buffer, copies, late=False):
        self.buffer, self.copies, self.waiting = buffer, copies, late
        if not late:
            for copy in copies:
                copy.start()

    def start(self):
        if self.waiting:
            for copy in self.copies:
                copy.start()
        self.waiting = False

    def __call__(self):
        self.start()
        for copy in self.copies:
            copy.wait()
        self.copies = []
        return self.buffer


class Going:
    def __init__(self, target, buffer, sems):
        self.target, self.buffer, self.sems, self.copies = target, buffer, sems, []

    def __setitem__(self, index, value):
        self.buffer[index] = value

    def __getitem__(self, index):
        return self.buffer[index]

    def part(self, *index):
        copy = pltpu.make_async_copy(self.buffer.at[index], self.target.at[index], self.sems[len(self.copies)])
        copy.start()
        self.copies.append(copy)

    def send(self):
        if self.target is not None and not self.copies:
            copy = pltpu.make_async_copy(self.buffer, self.target, self.sems[0])
            copy.start()
            self.copies.append(copy)


def part_swapped(swap, one, two, one_index, two_index):
    straight, crossed = [], []
    for a, b, index in ((one, two, one_index), (two, one, two_index)):
        sem = a.sems[len(a.copies)]
        straight.append(pltpu.make_async_copy(a.buffer.at[index], a.target.at[index], sem))
        crossed.append(pltpu.make_async_copy(a.buffer.at[index], b.target.at[index], sem))

    @pl.when(swap)
    def _():
        for copy in crossed:
            copy.start()

    @pl.when(jnp.logical_not(swap))
    def _():
        for copy in straight:
            copy.start()

    one.copies.append(straight[0])
    two.copies.append(straight[1])


def pick(ref, index, scalars):
    if index is None:
        return ref
    return ref.at[index(*scalars) if callable(index) else index]


class Chain:
    def __init__(self):
        self.last = None

    def call(self, kernel, name, scalars, takes, outs, scratch=(), leaves=False, weight=None, passes=(), onto=()):
        arrays, spaces, spots = [], [], []

        def place(array, space):
            for i, (known, its) in enumerate(zip(arrays, spaces)):
                if known is array and its is space:
                    return i
            arrays.append(array)
            spaces.append(space)
            return len(arrays) - 1

        fetched = [one for one in takes if not one.held]
        views = []
        for one in takes:
            if one.held:
                views.append((place(one.copies[0][0], VMEM), one.copies[0][1]))
            else:
                spots.append([(place(a, HBM), s, t) for a, s, t in one.copies])
        after = [] if self.last is None else [self.last]
        n_scalar, n_array, n_out = len(scalars), len(arrays), len(outs)
        n_copies = sum(len(one) for one in spots)

        def body(*refs):
            numbers, refs = refs[:n_scalar], refs[n_scalar:]
            given, refs = refs[:n_array], refs[n_array + len(after) + len(passes) + len(onto) :]
            results, refs = refs[:n_out], refs[n_out + len(passes) :]
            sems, refs = refs[0], refs[1:]
            into, refs = refs[: len(fetched)], refs[len(fetched) :]
            outof, rest = (refs[:n_out], refs[n_out:]) if leaves else (results, refs)
            at = 0
            buffers = []
            for one, buffer, copies in zip(fetched, into, spots):
                listed = []
                for which, source, target in copies:
                    listed.append(
                        pltpu.make_async_copy(
                            pick(given[which], source, numbers), pick(buffer, target, numbers), sems.at[at]
                        )
                    )
                    at += 1
                buffers.append(Coming(buffer, listed, one.late))
            left, seen, coming = list(buffers), list(views), []
            for one in takes:
                if one.held:
                    which, index = seen.pop(0)
                    coming.append(Coming(pick(given[which], index, numbers), []))
                else:
                    coming.append(left.pop(0))
            going = [
                Going(result if leaves else None, buffer, [sems.at[at + PARTS * i + j] for j in range(PARTS)])
                for i, (result, buffer) in enumerate(zip(results, outof))
            ]
            kernel(*numbers, *coming, *going, *rest)
            for one in coming:
                one()
            for one in going:
                one.send()
            for one in going:
                for copy in one.copies:
                    copy.wait()

        body.__name__ = name
        out = pl.pallas_call(
            body,
            in_specs=[SMEM] * n_scalar + spaces + [WHERE_IT_IS] * len(after) + [HBM] * (len(passes) + len(onto)),
            out_specs=[HBM if leaves else VMEM] * n_out + [HBM] * len(passes),
            out_shape=list(outs) + [shape(one.shape, one.dtype) for one in passes],
            input_output_aliases={
                n_scalar + n_array + len(after) + i: (n_out + i if i < len(passes) else i - len(passes))
                for i in range(len(passes) + len(onto))
            },
            scratch_shapes=[pltpu.SemaphoreType.DMA((n_copies + PARTS * n_out,))]
            + [pltpu.VMEM(one.dims, one.dtype) for one in fetched]
            + [pltpu.VMEM(o.shape, o.dtype) for o in outs if leaves]
            + list(scratch),
            compiler_params=pltpu.CompilerParams(vmem_limit_bytes=LIMITS.get(name, BIG_LIMIT >> 20) << 20 if leaves else SMALL_LIMIT),
            cost_estimate=pl.CostEstimate(flops=int(1e9 * (WEIGHTS.get(name, 17.0 if leaves else 0.0) if weight is None else weight)) + 1000, bytes_accessed=1000, transcendentals=0),
            name=name,
        )(*scalars, *arrays, *after, *passes, *onto)
        self.last = out[0]
        return out


def window(first, length):
    return max(0, first - LONGEST), min(length, first + BLOCK + LONGEST)


class Weights:
    def __init__(self, wq, wk, wv, bq, bv, wo):
        self.projections, self.biases, self.wo = (wq, wk, wv), (bq, bv), wo

    def cut(self, p, n=1):
        if callable(p):
            return lambda *numbers: pl.ds(pl.multiple_of(p(*numbers) * PAIR, PAIR), n * PAIR)
        return lambda *numbers: slice(p * PAIR, (p + n) * PAIR)

    def triple(self, p):
        d = self.wo.shape[1]
        cut = self.cut(p)
        return Take(
            (d, 3 * PAIR), BF16,
            [
                (a, lambda *n: (slice(None), cut(*n)), (slice(None), slice(i * PAIR, (i + 1) * PAIR)))
                for i, a in enumerate(self.projections)
            ],
        )

    def out(self, p, n=1):
        d = self.wo.shape[1]
        cut = self.cut(p, n)
        return Take((n * PAIR, d), BF16, [(self.wo, lambda *k: (cut(*k), slice(None)), None)])

    def bias(self):
        bq, bv = self.biases
        half = bq.shape[1]
        return Take(
            (1, 2 * half), F32,
            [(bq, None, (slice(None), slice(0, half))), (bv, None, (slice(None), slice(half, 2 * half)))],
        )


class SentWeights:
    def __init__(self, pack):
        self.pack, self.d = pack, pack.shape[1]

    def cut(self, p, base, n=1):
        def index(*numbers):
            if callable(p):
                return pl.ds(pl.multiple_of(base + p(*numbers) * PAIR, PAIR), n * PAIR)
            return slice(base + p * PAIR, base + (p + n) * PAIR)

        return index

    def triple(self, p):
        d, half = self.d, self.d // 2
        copies = []
        for i, (rows, base) in enumerate(((slice(0, d), 0), (slice(0, d), half), (slice(d, 2 * d), 0))):
            cut = self.cut(p, base)
            copies.append(
                (self.pack, lambda *n, rows=rows, cut=cut: (rows, cut(*n)), (slice(None), slice(i * PAIR, (i + 1) * PAIR)))
            )
        return Take((d, 3 * PAIR), F32, copies)

    def out(self, p, n=1):
        d, half = self.d, self.d // 2
        copies = []
        for i in range(2):
            cut = self.cut(p, d + i * half, n)
            copies.append(
                (self.pack, lambda *k, cut=cut: (cut(*k), slice(half, d)), (slice(None), slice(i * half, (i + 1) * half)))
            )
        return Take((n * PAIR, d), F32, copies)

    def bias(self):
        d = self.d
        return fetch(self.pack, (slice(2 * d, 2 * d + TINY), slice(None)), (TINY, d))


def pack_kernel(wq, wk, wv, wo, bq, bv, bi, w_inner, w_outer, out, inner_out, outer_out):
    d, half = wq.buffer.shape
    out[0:d, :half] = wq()[...].astype(F32)
    out[0:d, half:] = wk()[...].astype(F32)
    out.part(slice(0, d))
    out[d : 2 * d, :half] = wv()[...].astype(F32)
    out[d : d + half, half:] = wo()[:, :half].astype(F32)
    out[d + half : 2 * d, half:] = wo()[:, half:].astype(F32)
    out[2 * d : 2 * d + 1, :half] = bq()[...]
    out[2 * d : 2 * d + 1, half:] = bv()[...]
    out[2 * d + 1 : 2 * d + 2, :] = bi()[:, :d]
    out[2 * d + 2 : 2 * d + 3, :] = bi()[:, d:]
    out[2 * d + 3 :, :] = jnp.zeros((TINY - 3, d), F32)
    out.part(slice(d, 2 * d + TINY))
    for ref, result in ((w_inner, inner_out), (w_outer, outer_out)):
        rows = ref.buffer.shape[0] // 2
        for i in range(2):
            cut = slice(i * rows, (i + 1) * rows)
            result[cut, :] = ref()[cut, :].astype(F32)
            result.part(cut)


def row_index(other):
    return lambda core, *_: 1 - core[0] if other else core[0]


def row_of(array, other):
    return Take(array.shape[1:], array.dtype, [(array, row_index(other), None)])


def segments_of(place, fill_ref, seg, cols_ref):
    length = cols_ref.shape[0]
    fill = fill_ref[place]
    row = seg()[pl.ds(place, 1), :].astype(F32)
    places = lax.broadcasted_iota(jnp.int32, (1, length), 1)
    valid = places < fill
    keyed = jnp.where(valid, row, -1.0)
    cols_ref[...] = jnp.broadcast_to(keyed, (PAIR, length)).T
    return row, jnp.where(valid, 1.0, 0.0)


def mask_for(cols_ref, row, low, high, first):
    once = cols_ref[low:high, :] == row[:, first : first + BLOCK]
    return jnp.concatenate([once, once], axis=1)


def two_heads(array):
    lanes = lax.broadcasted_iota(jnp.int32, array.shape, 1)
    return jnp.where(lanes < HEAD_DIM, array, 0), jnp.where(lanes < HEAD_DIM, 0, array)


def stacked(pair, first):
    return jnp.concatenate([half[first : first + BLOCK] for half in pair], axis=0)


def staged(items, one, two, three):
    items = list(items)
    ones, twos = {}, {}
    for i in range(len(items) + 2):
        if i < len(items):
            ones[i] = one(items[i])
        if 0 <= i - 1 < len(items):
            twos[i - 1] = two(items[i - 1], *ones.pop(i - 1))
        if 0 <= i - 2:
            three(items[i - 2], *twos.pop(i - 2))


def forward_pair(p, x, w3, bias, row, valid, cols, qkv, mixed_out, lse):
    length = x.shape[0]
    half = bias.shape[1] // 2
    y = dot_nn(x, w3)
    at = p * PAIR
    q = y[:, :PAIR] + bias[0:1, at : at + PAIR]
    q = (q.astype(BF16) * 0.125).astype(BF16)
    k = y[:, PAIR : 2 * PAIR].astype(BF16)
    v = (y[:, 2 * PAIR :] + bias[0:1, half + at : half + at + PAIR]).astype(BF16)
    vt = v.T
    qkv[0] = q
    qkv[1] = k
    qkv[2] = v
    heads = two_heads(q)

    def scores(first):
        low, high = window(first, length)
        return (dot_nt(k[low:high], stacked(heads, first)),)

    def weigh(first, s):
        low, high = window(first, length)
        s = jnp.where(mask_for(cols, row, low, high, first), s, MASKED)
        peak = jnp.max(s, axis=0, keepdims=True)
        e = jnp.exp(s - peak)
        total = jnp.sum(e, axis=0, keepdims=True)
        lse[0:1, 2 * first : 2 * first + 2 * BLOCK] = peak + jnp.log(total)
        return e.astype(BF16), total

    def mix(first, e, total):
        low, high = window(first, length)
        block = slice(first, first + BLOCK)
        o = dot_nn(vt[:, low:high], e)
        keep = valid[:, block]
        mixed_out[:HEAD_DIM, block] = (o[:HEAD_DIM, :BLOCK] * (keep / total[:, :BLOCK])).astype(BF16)
        mixed_out[HEAD_DIM:, block] = (o[HEAD_DIM:, BLOCK:] * (keep / total[:, BLOCK:])).astype(BF16)

    staged(range(0, length, BLOCK), scores, weigh, mix)


def start_all(*ones):
    for one in ones:
        one.start()


def forward_pairs(x, w3s, bias, row, valid, cols, qkv, mixed, lse):
    for p, w3 in enumerate(w3s):
        forward_pair(
            p, x, w3()[...].astype(BF16), bias(), row, valid, cols, qkv.buffer.at[p], mixed.buffer.at[p], lse.buffer.at[p]
        )
        qkv.part(p)
        mixed.part(p)
        lse.part(p)


def forward_own_kernel(core_ref, fill_ref, seg, x_in, w3_0, bias, w3_1, qkv, mixed, lse, cols):
    row, valid = segments_of(core_ref[0], fill_ref, seg, cols)
    x = x_in()[...]
    w3_0()
    start_all(w3_1)
    forward_pairs(x, (w3_0, w3_1), bias, row, valid, cols, qkv, mixed, lse)


def all_units(low, lowt, d_ffn, wi, bias_of, wo, grads, bias_out, hidden_out, pre_out):
    units = wi().shape[1]
    part, step = units // 2, 256

    def products(at):
        i, inside = divmod(at, part)
        cut, held = slice(at, at + step), slice(inside, inside + step)
        pre = dot_nn(low, wi()[:, cut].astype(BF16)) + bias_of(i, held)
        return pre, dot_nt(d_ffn, wo()[cut, :].astype(BF16))

    def bend(at, pre, d_hidden):
        square = pre * pre
        t = jnp.tanh(pre * (GELU_C + (GELU_C * GELU_A) * square))
        cdf = 0.5 + 0.5 * t
        hidden = (pre * cdf).astype(BF16)
        slope = cdf + (0.5 * pre) * (1.0 - t * t) * (GELU_C + (3.0 * GELU_C * GELU_A) * square)
        d_pre = (d_hidden * slope).astype(BF16)
        i, inside = divmod(at, part)
        bias_out[i : i + 1, inside : inside + step] = jnp.sum(d_pre.astype(F32), axis=0, keepdims=True)
        return hidden, d_pre

    def gather(at, hidden, d_pre):
        i, inside = divmod(at, part)
        cut, held = slice(at, at + step), slice(inside, inside + step)
        hidden_out[:, cut] = hidden
        pre_out[:, cut] = d_pre
        grads[i][held, :] = dot_tn(hidden, d_ffn)
        grads[i][part:, held] = dot_nn(lowt, d_pre)
        if inside + step == part:
            grads[i].send()

    staged(range(0, units, step), products, bend, gather)


def middle_kernel(core_ref, fill_ref, gate, feed_gate, seg, x_in, w3_0, bias, w3_1, wo, mixed_own, wo_own, out_bias,
                  cot, wi, w_outer, qkv, mixed, lse, mid, low_out, grad_0, grad_1, bias_out, hidden_out, pre_out, cols):
    row, valid = segments_of(core_ref[0], fill_ref, seg, cols)
    x = x_in()[...]
    w3_0()
    start_all(w3_1, wo, mixed_own, wo_own, out_bias, cot, wi, w_outer)
    forward_pairs(x, (w3_0, w3_1), bias, row, valid, cols, qkv, mixed, lse)
    for at in range(0, x.shape[0], ROWS):
        rows = slice(at, at + ROWS)
        branch = out_bias()[...]
        for p in range(2):
            cut = slice(p * PAIR, (p + 1) * PAIR)
            branch = branch + dot_tn(mixed_own()[p, :, rows], wo_own()[cut, :])
            branch = branch + dot_tn(mixed[p, :, rows], wo()[cut, :].astype(BF16))
        value = x[rows].astype(F32) + gate[0] * branch
        mid[rows, :] = value
        mid.part(rows)
        low_out[rows, :] = value.astype(BF16)
        low_out.part(rows)
    low = low_out[...]
    d_ffn = (feed_gate[0] * cot()[...].astype(F32)).astype(BF16)
    bias_out[...] = jnp.zeros(bias_out.buffer.shape, F32)
    all_units(
        low, low.T, d_ffn, wi, lambda i, cut: bias()[1 + i : 2 + i, cut], w_outer, (grad_0, grad_1), bias_out,
        hidden_out, pre_out,
    )


def feed_kernel(core_ref, gate, feed_gate, low_in, wi, bi, cot_in, w_outer, hidden_sent, pre_sent, wi_sent, wo_sent,
                out_bias, mid, x, grad_0, grad_1, out, dmid_out, dbranch_out, small, bias_out, hidden_out, pre_out):
    low = low_in()[...]
    length, d = low.shape
    wi()
    start_all(cot_in, w_outer)
    lowt = low.T
    cot = cot_in()[...].astype(F32)
    d_ffn = (feed_gate[0] * cot).astype(BF16)
    w_outer()
    start_all(hidden_sent, pre_sent, wi_sent, wo_sent, out_bias, mid, x)
    bias_out[...] = jnp.zeros_like(bias_out)
    part = d
    all_units(
        low, lowt, d_ffn, wi, lambda i, cut: bi()[:, i * part : (i + 1) * part][:, cut], w_outer, (grad_0, grad_1),
        bias_out, hidden_out, pre_out,
    )
    wi_other = wi_sent()[...].astype(BF16)
    wo_other = wo_sent()[...].astype(BF16)
    sums = [jnp.zeros((1, d), F32)] * 3
    for at in range(0, length, ROWS):
        rows = slice(at, at + ROWS)
        seen = cot_in()[rows, :].astype(F32)
        dmid = dot_nt(pre_sent()[rows, :], wi_other) + dot_nt(pre_out[rows, :], wi()[...]) + seen
        ffn = dot_nn(hidden_sent()[rows, :], wo_other) + dot_nn(hidden_out[rows, :], w_outer()[...]) + out_bias()[...]
        dmid_out[rows, :] = dmid
        dmid_out.part(rows)
        dbranch = (gate[0] * dmid).astype(BF16)
        dbranch_out[rows, :] = dbranch
        dbranch_out.part(rows)
        middle = mid()[rows, :]
        out[rows, :] = middle + feed_gate[0] * ffn
        out.part(rows)
        branch = middle - x()[rows, :].astype(F32)
        for i, value in enumerate((dbranch.astype(F32), dmid * branch, seen * ffn)):
            sums[i] = sums[i] + jnp.sum(value, axis=0, keepdims=True)
    small[...] = jnp.zeros(small.buffer.shape, F32)
    small[1:3, :] = bias_out[0:2, :]
    small[3:4, :] = sums[0]
    small[4:5, :] = jnp.sum(d_ffn.astype(F32), axis=0, keepdims=True)
    small[5:6, :] = sums[1] / gate[0]
    small[6:7, :] = sums[2]


def join_kernel(bit, a, a_came, b, b_came, keep, send):
    rows = keep.buffer.shape[0] // 2
    start_all(a, a_came, b, b_came)
    for i in range(2):
        cut = slice(i * rows, (i + 1) * rows)
        keep[cut, :] = a()[cut, :] + a_came()[cut, :]
        send[cut, :] = b()[cut, :] + b_came()[cut, :]
        part_swapped(bit[0] != 0, keep, send, (cut,), (cut,))


def backward_pair(dbranch, do, qkv, lse, mixed, x, row, cols, dk_acc, dv_acc, dqt, grad_out):
    length, d = dbranch.shape
    q, k, v = qkv[0], qkv[1], qkv[2]
    kt = k.T
    qs = two_heads(q)
    dos = two_heads(do)
    dk_acc[...] = jnp.zeros_like(dk_acc)
    dv_acc[...] = jnp.zeros_like(dv_acc)

    def products(first):
        low, high = window(first, length)
        qq, dd = stacked(qs, first), stacked(dos, first)
        return qq, dd, dot_nt(k[low:high], qq), dot_nt(v[low:high], dd)

    def weigh(first, qq, dd, s, dw):
        low, high = window(first, length)
        s = jnp.where(mask_for(cols, row, low, high, first), s, MASKED)
        w = jnp.exp(s - lse[0:1, 2 * first : 2 * first + 2 * BLOCK])
        both = w * dw
        mean = jnp.sum(both, axis=0, keepdims=True)
        return qq, dd, w.astype(BF16), (both - w * mean).astype(BF16)

    def gather(first, qq, dd, w, ds):
        low, high = window(first, length)
        block = slice(first, first + BLOCK)
        dv_acc[low:high, :] += dot_nn(w, dd)
        dk_acc[low:high, :] += dot_nn(ds, qq)
        dq = dot_nn(kt[:, low:high], ds)
        dqt[:HEAD_DIM, block] = dq[:HEAD_DIM, :BLOCK]
        dqt[HEAD_DIM:, block] = dq[HEAD_DIM:, BLOCK:]

    staged(range(0, length, BLOCK), products, weigh, gather)
    dq = (0.125 * dqt[...]).T.astype(BF16)
    all3 = jnp.concatenate([dq, dk_acc[...].astype(BF16), dv_acc[...].astype(BF16)], axis=1)
    grad_out[:, : 3 * PAIR] = dot_tn(x, all3)
    out_grad = dot_nn(mixed, dbranch)
    for c in range(d // PAIR):
        cut = slice(c * PAIR, (c + 1) * PAIR)
        grad_out[cut, 3 * PAIR :] = out_grad[:, cut]
    return all3


def bias_sums(all3):
    sums = jnp.sum(all3.astype(F32), axis=0, keepdims=True)
    return jnp.concatenate([sums[:, :PAIR], sums[:, 2 * PAIR :]], axis=1)


def masked_heads(dbranch, wo, fill):
    places = lax.broadcasted_iota(jnp.int32, (dbranch.shape[0], 1), 0)
    return jnp.where(places < fill, dot_nt(dbranch, wo), 0.0).astype(BF16)


def backward_kernel(sent, last, core_ref, fill_ref, pair, *refs):
    if sent and not last:
        bit, *refs = refs
    seg, dbranch_in, wo, x_in, qkv, lse, mixed, *refs = refs
    late = []
    if last:
        w3, all3_in, w3_before, total_in, *refs = refs
        late += [w3, all3_in, w3_before, total_in]
    if sent:
        if last:
            bias_in, *refs = refs
            late.append(bias_in)
        else:
            parts, refs = refs[:4], refs[4:]
            late += parts
    else:
        came, *refs = refs
        late.append(came)
    small_in, *refs = refs
    late.append(small_in)
    if last:
        grad_out, small_out, total_out, *rest = refs
    else:
        grad_out, small_out, all3_out, *rest = refs
        if sent:
            keep, send, *rest = rest
    cols, dk_acc, dv_acc, dqt = rest
    row, _ = segments_of(core_ref[0], fill_ref, seg, cols)
    dbranch = dbranch_in()[...]
    length, d = dbranch.shape
    do = masked_heads(dbranch, wo()[...].astype(BF16), fill_ref[core_ref[0]])
    x = x_in()[...]
    qkv()
    start_all(*late)
    grads = grad_out.buffer.at[0:d]
    all3 = backward_pair(dbranch, do, qkv(), lse(), mixed()[...], x, row, cols, dk_acc, dv_acc, dqt, grads)
    small_out[...] = small_in()[...]
    if sent and last:
        small_out[1:3, :] = bias_in()[0:2, :]
    if not sent:
        grads[...] += came()[0:d, :]
    spot = pl.ds(pl.multiple_of(pair[0] * 2 * PAIR, PAIR), 2 * PAIR)
    if sent and not last:
        small_out[0:1, spot] = bias_sums(all3)
    else:
        small_out[0:1, spot] += bias_sums(all3)
    if last and not sent:
        small_out[...] += came()[d:, :]
    if last and sent:
        grad_out[d:, :] = small_out[...]
    grad_out.send()
    if last:
        for at in range(0, length, ROWS):
            rows = slice(at, at + ROWS)
            total = dot_nt(all3_in()[rows, :], w3_before()[...].astype(BF16)) + dot_nt(all3[rows], w3()[...].astype(BF16))
            total_out[rows, :] = total_in()[rows, :] + total
            total_out.part(rows)
    else:
        all3_out[...] = all3
        if sent:
            join_kernel(bit, *parts, keep, send)


def attention_scratch(length):
    return [pltpu.VMEM((length, PAIR), F32)] * 3 + [pltpu.VMEM((PAIR, length), F32)]


def place_in(refs, mask):
    at = 0
    for ref in refs:
        at = 2 * at + ref[0]
    return jnp.bitwise_xor(at, mask)


def sum_of(terms, cut):
    total = terms[0]()[cut, :]
    for one in terms[1:]:
        total = total + one()[cut, :]
    return total


class Stream:
    def __init__(self, chain, members, bits, send, out, back):
        self.chain, self.members, self.bits = chain, members, bits
        self.out, self.back = list(out), list(back)
        self.group = [0]
        self.came = [self.travel(send, 1)]
        self.tail, self.small, self.turned, self.lanes = 0, None, False, 1

    def keep(self, mine, small=None):
        self.mine, self.small = mine, small
        self.rows, self.width = mine.shape
        self.joined = []

    def join(self, other):
        self.joined = [other]

    def travel(self, array, mask):
        pairs = []
        for place in range(self.members):
            for core in range(2):
                partner = place
                for i, step in enumerate(reversed(self.group)):
                    if mask >> i & 1:
                        partner ^= 1 << (step ^ core if step < 2 else step)
                pairs.append((place * 2 + core, partner * 2 + core))
        return lax.ppermute(array, ("dp", "mp"), pairs)

    def call(self, kernel, name, group, outs, small=False):
        takes = [take(one) for stream in (self, *self.joined) for one in (stream.mine, *stream.came)]
        takes += [take(self.small)] if small else []
        results = self.chain.call(
            kernel, name, [self.bits[step] for step in group], takes, [shape(dims) for dims in outs],
            weight=self.weight, passes=self.passes,
        )
        self.passes = results[len(outs) :]
        return results[: len(outs)]

    def halve(self):
        group = self.out.pop(0)
        parts, n_terms = 1 << len(group), 1 + len(self.came)
        whole, tail = self.rows, self.tail
        rows = whole // parts
        begins = self.small is not None and not tail
        sources = 1 + len(self.joined)
        lanes = self.lanes = max(self.lanes, sources)

        def kernel(*refs):
            bits, refs = refs[: len(group)], refs[len(group) :]
            terms = [refs[i * n_terms : (i + 1) * n_terms] for i in range(sources)]
            refs = refs[sources * n_terms :]
            if begins:
                both = refs[0]()[...]
                refs = refs[1:]
            elif tail:
                both = sum_of(terms[0], slice(lanes * whole, lanes * whole + tail))
            for mask, out in enumerate(refs):
                at = place_in(bits, mask) * rows
                for lane in range(lanes):
                    source, base = (lane, 0) if sources > 1 else (0, lane * whole)
                    cut = pl.ds(pl.multiple_of(base + at, 8), rows)
                    out[lane * rows : (lane + 1) * rows, :] = sum_of(terms[source], cut)
                if begins or tail:
                    out[lanes * rows :, :] = both

        if begins:
            self.tail = TINY
        self.mine, *sends = self.call(
            kernel, "halve", group, [(lanes * rows + self.tail, self.width)] * parts, begins
        )
        self.joined = []
        self.group = group
        self.came = [self.travel(send, mask + 1) for mask, send in enumerate(sends)]
        self.rows = rows

    def turn(self):
        rows, tail = self.lanes * self.rows, self.tail
        n_came = len(self.came)

        def kernel(mine, *refs):
            came, refs = refs[:n_came], refs[n_came:]
            total = mine()[...]
            for one in came:
                total = total + one()[...]
            refs[0][...] = total[:rows]
            if tail:
                refs[1][...] = total[rows:]

        outs = [(rows, self.width)] + ([(TINY, self.width)] if tail else [])
        self.mine, *tiny = self.call(kernel, "turn", [], outs)
        self.small = tiny[0] if tiny else None
        self.turned = True
        self.spread()

    def double(self):
        rows, lanes = self.rows, self.lanes
        parts = len(self.came) + 1
        ends = len(self.back) == 1 and self.small is not None
        group = self.group

        def kernel(*refs):
            bits, refs = refs[: len(group)], refs[len(group) :]
            have, refs = refs[:parts], refs[parts:]
            out = refs[-1]
            if ends:
                out[lanes * parts * rows :, :] = refs[0]()[...]
            for mask, one in enumerate(have):
                at = place_in(bits, mask) * rows
                for lane in range(lanes):
                    cut = pl.ds(pl.multiple_of(lane * parts * rows + at, 8), rows)
                    out[cut, :] = one()[lane * rows : (lane + 1) * rows, :]

        self.rows = parts * rows
        (self.mine,) = self.call(
            kernel, "double", group, [(lanes * self.rows + (TINY if ends else 0), self.width)], ends
        )
        self.spread()

    def spread(self):
        self.group = self.back.pop(0)
        self.came = [self.travel(self.mine, mask) for mask in range(1, 1 << len(self.group))]

    def advance(self, weight=0.0, passes=()):
        self.weight, self.passes = weight, passes
        if self.out:
            self.halve()
        elif not self.turned:
            self.turn()
        elif self.back:
            self.double()
        return self.passes

    def done(self):
        return self.turned and not self.back


def in_order(bit, mine, came, low, high):
    @pl.when(bit[0] == 0)
    def _():
        low(mine())
        high(came())

    @pl.when(bit[0] != 0)
    def _():
        low(came())
        high(mine())


def final_feed(chain, stream, index, d, onto=()):
    units = stream.rows
    cut = slice(index * units, (index + 1) * units)

    def kernel(bit, mine, came, inner, outer):
        mine()
        came()

        def low(ref):
            outer[cut, :] = ref[...]

        def high(ref):
            inner[:, cut] = ref[...]

        in_order(bit, mine, came, low, high)
        outer.part(cut)
        inner.part(slice(None), cut)

    return chain.call(
        kernel, "final_feed_%d" % index, [stream.bits[0]], [fetch(stream.mine), fetch(stream.came[0])],
        [shape((d, 2 * units)), shape((2 * units, d))], leaves=True, onto=onto,
    )


def final_attention(chain, third, d):
    half = d // 2

    def kernel(bit, mine, came, gq, gk, gv, go, gqb, gvb, gob, gib, goutb, gates):
        small = mine()[d:, :] + came()[d:, :]
        for p in range(2):
            cut = slice(p * PAIR, (p + 1) * PAIR)
            gqb[:, cut] = small[0:1, 2 * p * PAIR : (2 * p + 1) * PAIR]
            gvb[:, cut] = small[0:1, (2 * p + 1) * PAIR : (2 * p + 2) * PAIR]
        gib[:, :d] = small[1:2, :]
        gib[:, d:] = small[2:3, :]
        gob[...] = small[3:4, :]
        goutb[...] = small[4:5, :]
        gates[...] = jnp.broadcast_to(jnp.sum(small, axis=1, keepdims=True), gates.buffer.shape)

        def place(p, ref):
            cut = slice(p * PAIR, (p + 1) * PAIR)
            gq[:, cut] = ref[:d, :PAIR]
            gk[:, cut] = ref[:d, PAIR : 2 * PAIR]
            gv[:, cut] = ref[:d, 2 * PAIR : 3 * PAIR]
            for c in range(d // PAIR):
                across = slice(c * PAIR, (c + 1) * PAIR)
                go[cut, across] = ref[across, 3 * PAIR :]

        in_order(bit, mine, came, partial(place, 0), partial(place, 1))

    return chain.call(
        kernel, "final_attention", [third.bits[0]], [take(third.mine), take(third.came[0])],
        [shape((d, half))] * 3
        + [shape((half, d)), shape((1, half)), shape((1, half)), shape((1, d)), shape((1, 2 * d)), shape((1, d)), shape((TINY, PAIR))],
        leaves=True,
    )


def rows_kernel(core_ref, own, came, out):
    out[core_ref[0]] = own()[...].astype(out.buffer.dtype)
    out.part(core_ref[0])
    out[1 - core_ref[0]] = came()[...].astype(out.buffer.dtype)
    out.part(1 - core_ref[0])


def shards(members, tokens, segment_ids, row_fill, query_weight, query_bias, key_weight,
           value_weight, value_bias, out_weight, out_bias, attention_gate, inner_weight,
           inner_bias, outer_weight, outer_bias, feed_gate, cotangent):
    _, length, d = tokens.shape
    half = d // 2
    place = lax.axis_index("dp")
    core_id = lax.axis_index("mp")
    core = core_id.astype(jnp.int32).reshape(1)
    bits = []
    for step in range(members.bit_length() - 1):
        bit = (place >> (step ^ core_id if step < 2 else step)) & 1
        bits.append(bit.astype(jnp.int32).reshape(1))
    not_mine = 1 - bits[0]
    chain = Chain()

    def across(array):
        return lax.ppermute(array, "mp", [(0, 1), (1, 0)])

    def as_row(array):
        return array.reshape(1, -1)

    def own_row(array):
        return row_of(array, False)

    a_gate = attention_gate.reshape(1)
    f_gate = feed_gate.reshape(1)
    qb, vb, ib, ob, fb = (as_row(a) for a in (query_bias, value_bias, inner_bias, out_bias, outer_bias))
    own = Weights(query_weight, key_weight, value_weight, qb, vb, out_weight)
    seg = fetch(segment_ids)
    cols = [pltpu.VMEM((length, PAIR), F32)]
    units = inner_weight.shape[1]

    pack, wi, wo = chain.call(
        pack_kernel, "pack", [],
        [fetch(a) for a in (query_weight, key_weight, value_weight, out_weight, qb, vb, ib, inner_weight, outer_weight)],
        [shape((2 * d + TINY, d)), shape((d, units)), shape((units, d))], leaves=True,
    )
    pack_came, wi_came, wo_came = across(pack), across(wi), across(wo)
    sent = SentWeights(pack_came)

    pair_outs = [shape((2, 3, length, PAIR), BF16), shape((2, PAIR, length), BF16), shape((2, TINY, 2 * length))]
    qkv_a, mixed_a, lse_a = chain.call(
        forward_own_kernel, "forward_own", [core, row_fill],
        [seg, own_row(tokens), own.triple(0), own.bias(), later(own.triple(1))], pair_outs, cols, leaves=True,
    )
    unit_outs = [shape((length, units), BF16)] * 2
    grad_outs = [shape((2 * d, d))] * 2
    qkv_b, mixed_b, lse_b, mid, low, g_sent_0, g_sent_1, bias_b, hidden_b, pre_b = chain.call(
        middle_kernel, "middle", [core, row_fill, a_gate, f_gate],
        [seg, own_row(tokens), sent.triple(0), sent.bias()]
        + [
            later(one)
            for one in (
                sent.triple(1), sent.out(0, 2), fetch(mixed_a), own.out(0, 2), fetch(ob), own_row(cotangent),
                fetch(wi_came), fetch(wo_came),
            )
        ],
        pair_outs + [shape((length, d)), shape((length, d), BF16)] + grad_outs + [shape((TINY, d))] + unit_outs,
        cols, leaves=True,
    )
    g_came_0, g_came_1 = across(g_sent_0), across(g_sent_1)
    g_own_0, g_own_1, out_own, dmid, dbranch, small = chain.call(
        feed_kernel, "feed", [core, a_gate, f_gate],
        [fetch(low), fetch(inner_weight), fetch(ib)]
        + [
            later(one)
            for one in (
                own_row(cotangent), fetch(outer_weight), fetch(hidden_b), fetch(pre_b), fetch(wi_came), fetch(wo_came),
                fetch(fb), fetch(mid), own_row(tokens),
            )
        ],
        grad_outs + [shape((length, d))] * 2 + [shape((length, d), BF16), shape((TINY, d))],
        [pltpu.VMEM((TINY, d), F32)] + [pltpu.VMEM((length, units), BF16)] * 2, leaves=True,
    )

    wide = [[step for step in pair if step < len(bits)] for pair in ((i, i + 1) for i in range(2, len(bits), 2))]
    one_by_one = [[step] for step in range(len(bits))]
    direct = ([[1], *wide], [*wide[::-1], [1], [0]])
    plain = (one_by_one[1:], one_by_one[::-1])

    def halves(mine, came):
        return [fetch(one, (slice(i * d, (i + 1) * d), slice(None)), (d, d)) for i in range(2) for one in (mine, came)]

    def stream(send, ways):
        return Stream(chain, members, bits, send, *ways)

    other_bit = ((place >> (1 - core_id)) & 1).astype(jnp.int32).reshape(1)
    pair_of = lambda core, fill, pair, *_: pair[0]
    pair_before = lambda core, fill, pair, *_: 1 - pair[0]

    def backward(sent, last, pair, weights, kept, extra, small, outs, bit=None):
        qkv, mixed, lse = kept
        takes = [
            seg, fetch(dbranch), weights.out(pair_of), own_row(tokens), fetch(qkv, pair_of, (3, length, PAIR)),
            fetch(lse, pair_of, (TINY, 2 * length)), fetch(mixed, pair_of, (PAIR, length)),
        ]
        more = list(extra)
        if last:
            all3, total, *rest = more
            more = [weights.triple(pair_of), fetch(all3), weights.triple(pair_before), fetch(total), *rest]
        takes += [later(one) for one in [*more, fetch(small)]]
        return chain.call(
            partial(backward_kernel, sent, last), "backward_%s_%d" % ("sent" if sent else "own", last),
            [core, row_fill, pair] + ([bit] if bit is not None else []), takes, outs, attention_scratch(length),
            leaves=True,
        )

    keep, send = chain.call(
        join_kernel, "join", [bits[0]], halves(g_own_0, g_came_0), [shape((d, d))] * 2, leaves=True
    )
    first = stream(send, direct)
    first.keep(keep)
    square, row8, rows3 = shape((d, d)), shape((TINY, d)), shape((length, 3 * PAIR), BF16)
    kept_a, kept_b = (qkv_a, mixed_a, lse_a), (qkv_b, mixed_b, lse_b)
    g_0, small_b, all3, keep, send = backward(
        True, False, 1 - other_bit, sent, kept_b, halves(g_own_1, g_came_1), small, [square, row8, rows3, square, square],
        bit=bits[0],
    )
    second = stream(send, plain)
    second.keep(keep)
    g_came_first = across(g_0)
    first.advance(0.0)
    g_1, _, total = backward(
        True, True, other_bit, sent, kept_b, (all3, dmid, fetch(bias_b)), small_b,
        [shape((d + TINY, d)), row8, shape((length, d))],
    )
    g_came_last = across(g_1)
    first.advance(0.0)
    second.advance(0.0)
    send, small, all3 = backward(
        False, False, not_mine, own, kept_a, (fetch(g_came_first),), small, [square, row8, rows3]
    )
    third = stream(send, direct)
    first.advance(0.0)
    second.advance(0.0)
    keep, small, total = backward(
        False, True, bits[0], own, kept_a, (all3, total, fetch(g_came_last)), small,
        [square, row8, shape((length, d))],
    )
    third.keep(keep, small)
    third.advance()
    first.advance()
    second.advance(20.0)
    while third.out:
        third.advance()
    while not first.done():
        first.advance(20.0)
    third.advance(20.0)
    second.advance()
    grads = final_feed(chain, first, 0, d)
    (out_own,) = third.advance(passes=(out_own,))
    out_came = across(out_own)
    second.advance(20.0)
    while not third.done():
        (total,) = third.advance(passes=(total,))
        second.advance()
    total_came = across(total)
    (output,) = chain.call(
        rows_kernel, "output", [core], [fetch(out_own), fetch(out_came)], [shape((2, length, d), BF16)], leaves=True
    )
    while not second.done():
        second.advance()
    (grad_tokens,) = chain.call(
        rows_kernel, "tokens", [core], [fetch(total), fetch(total_came)], [shape((2, length, d))], leaves=True
    )
    gq, gk, gv, go, gqb, gvb, gob, gib, goutb, gates = final_attention(chain, third, d)
    inner_grad, outer_grad = final_feed(chain, second, 1, d, grads)
    return (
        output, grad_tokens, gq, gqb.reshape(-1), gk, gv, gvb.reshape(-1), go, gob.reshape(-1), gates[5, 0],
        inner_grad, gib.reshape(-1), outer_grad, goutb.reshape(-1), gates[6, 0],
    )


def solution(mesh):
    rows = P("dp", None, None)
    col = P(None, "mp")
    cut = P("mp")
    in_specs = (
        rows, P("dp", None), P("dp"), col, cut, col, col, cut, P("mp", None), P(), P(),
        col, cut, P("mp", None), P(), P(), rows,
    )
    out_specs = (
        rows, rows, col, cut, col, col, cut, P("mp", None), P(), P(), col, cut,
        P("mp", None), P(), P(),
    )
    return jax.shard_map(
        partial(shards, mesh.shape["dp"]), mesh=mesh, in_specs=in_specs, out_specs=out_specs,
        check_vma=False,
    )
```

```python
from functools import partial
import math

import jax
import jax.numpy as jnp
from jax import lax
from jax.experimental import pallas as pl
from jax.experimental.pallas import tpu as pltpu
from jax.sharding import PartitionSpec as P

HEAD_DIM = 64
PAIR = 2 * HEAD_DIM
LONGEST = 256
BLOCK = 128
TINY = 8
PARTS = 12
ROWS = 512
MASKED = -1e30
F32 = jnp.float32
BF16 = jnp.bfloat16
GELU_C = math.sqrt(2.0 / math.pi)
GELU_A = 0.044715
BIG_LIMIT = 63 * 1024 * 1024
LIMITS = {'backward_sent_0': 30, 'backward_sent_1': 30, 'backward_own_0': 30, 'backward_own_1': 30, 'output': 30, 'tokens': 63, 'final_feed_0': 63, 'final_feed_1': 63, 'final_attention': 63, 'join': 14}
WEIGHTS = {"backward_own": 80.0, "output": 80.0}
SMALL_LIMIT = 8 * 1024 * 1024
SMEM = pl.BlockSpec(memory_space=pltpu.SMEM)
VMEM = pl.BlockSpec(memory_space=pltpu.VMEM)
WHERE_IT_IS = pl.BlockSpec(memory_space=pl.ANY)
HBM = pl.BlockSpec(memory_space=pltpu.HBM)


def dot_nn(a, b):
    return lax.dot_general(a, b, (((1,), (0,)), ((), ())), preferred_element_type=F32)


def dot_nt(a, b):
    return lax.dot_general(a, b, (((1,), (1,)), ((), ())), preferred_element_type=F32)


def dot_tn(a, b):
    return lax.dot_general(a, b, (((0,), (0,)), ((), ())), preferred_element_type=F32)


def shape(dims, dtype=F32):
    return jax.ShapeDtypeStruct(tuple(dims), dtype)


class Take:
    def __init__(self, dims, dtype, copies, held=False):
        self.dims, self.dtype, self.copies, self.held = tuple(dims), dtype, copies, held
        self.late = False


def later(one):
    one.late = True
    return one


def take(array, index=None, dims=None):
    return Take(dims or array.shape, array.dtype, [(array, index, None)], True)


def fetch(array, index=None, dims=None):
    return Take(dims or array.shape, array.dtype, [(array, index, None)])


class Coming:
    def __init__(self, buffer, copies, late=False):
        self.buffer, self.copies, self.waiting = buffer, copies, late
        if not late:
            for copy in copies:
                copy.start()

    def start(self):
        if self.waiting:
            for copy in self.copies:
                copy.start()
        self.waiting = False

    def __call__(self):
        self.start()
        for copy in self.copies:
            copy.wait()
        self.copies = []
        return self.buffer


class Going:
    def __init__(self, target, buffer, sems):
        self.target, self.buffer, self.sems, self.copies = target, buffer, sems, []

    def __setitem__(self, index, value):
        self.buffer[index] = value

    def __getitem__(self, index):
        return self.buffer[index]

    def part(self, *index):
        copy = pltpu.make_async_copy(self.buffer.at[index], self.target.at[index], self.sems[len(self.copies)])
        copy.start()
        self.copies.append(copy)

    def send(self):
        if self.target is not None and not self.copies:
            copy = pltpu.make_async_copy(self.buffer, self.target, self.sems[0])
            copy.start()
            self.copies.append(copy)


def part_swapped(swap, one, two, one_index, two_index):
    straight, crossed = [], []
    for a, b, index in ((one, two, one_index), (two, one, two_index)):
        sem = a.sems[len(a.copies)]
        straight.append(pltpu.make_async_copy(a.buffer.at[index], a.target.at[index], sem))
        crossed.append(pltpu.make_async_copy(a.buffer.at[index], b.target.at[index], sem))

    @pl.when(swap)
    def _():
        for copy in crossed:
            copy.start()

    @pl.when(jnp.logical_not(swap))
    def _():
        for copy in straight:
            copy.start()

    one.copies.append(straight[0])
    two.copies.append(straight[1])


def pick(ref, index, scalars):
    if index is None:
        return ref
    return ref.at[index(*scalars) if callable(index) else index]


class Chain:
    def __init__(self):
        self.last = None

    def call(self, kernel, name, scalars, takes, outs, scratch=(), leaves=False, weight=None, passes=(), onto=()):
        arrays, spaces, spots = [], [], []

        def place(array, space):
            for i, (known, its) in enumerate(zip(arrays, spaces)):
                if known is array and its is space:
                    return i
            arrays.append(array)
            spaces.append(space)
            return len(arrays) - 1

        fetched = [one for one in takes if not one.held]
        views = []
        for one in takes:
            if one.held:
                views.append((place(one.copies[0][0], VMEM), one.copies[0][1]))
            else:
                spots.append([(place(a, HBM), s, t) for a, s, t in one.copies])
        after = [] if self.last is None else [self.last]
        n_scalar, n_array, n_out = len(scalars), len(arrays), len(outs)
        n_copies = sum(len(one) for one in spots)

        def body(*refs):
            numbers, refs = refs[:n_scalar], refs[n_scalar:]
            given, refs = refs[:n_array], refs[n_array + len(after) + len(passes) + len(onto) :]
            results, refs = refs[:n_out], refs[n_out + len(passes) :]
            sems, refs = refs[0], refs[1:]
            into, refs = refs[: len(fetched)], refs[len(fetched) :]
            outof, rest = (refs[:n_out], refs[n_out:]) if leaves else (results, refs)
            at = 0
            buffers = []
            for one, buffer, copies in zip(fetched, into, spots):
                listed = []
                for which, source, target in copies:
                    listed.append(
                        pltpu.make_async_copy(
                            pick(given[which], source, numbers), pick(buffer, target, numbers), sems.at[at]
                        )
                    )
                    at += 1
                buffers.append(Coming(buffer, listed, one.late))
            left, seen, coming = list(buffers), list(views), []
            for one in takes:
                if one.held:
                    which, index = seen.pop(0)
                    coming.append(Coming(pick(given[which], index, numbers), []))
                else:
                    coming.append(left.pop(0))
            going = [
                Going(result if leaves else None, buffer, [sems.at[at + PARTS * i + j] for j in range(PARTS)])
                for i, (result, buffer) in enumerate(zip(results, outof))
            ]
            kernel(*numbers, *coming, *going, *rest)
            for one in coming:
                one()
            for one in going:
                one.send()
            for one in going:
                for copy in one.copies:
                    copy.wait()

        body.__name__ = name
        out = pl.pallas_call(
            body,
            in_specs=[SMEM] * n_scalar + spaces + [WHERE_IT_IS] * len(after) + [HBM] * (len(passes) + len(onto)),
            out_specs=[HBM if leaves else VMEM] * n_out + [HBM] * len(passes),
            out_shape=list(outs) + [shape(one.shape, one.dtype) for one in passes],
            input_output_aliases={
                n_scalar + n_array + len(after) + i: (n_out + i if i < len(passes) else i - len(passes))
                for i in range(len(passes) + len(onto))
            },
            scratch_shapes=[pltpu.SemaphoreType.DMA((n_copies + PARTS * n_out,))]
            + [pltpu.VMEM(one.dims, one.dtype) for one in fetched]
            + [pltpu.VMEM(o.shape, o.dtype) for o in outs if leaves]
            + list(scratch),
            compiler_params=pltpu.CompilerParams(vmem_limit_bytes=LIMITS.get(name, BIG_LIMIT >> 20) << 20 if leaves else SMALL_LIMIT),
            cost_estimate=pl.CostEstimate(flops=int(1e9 * (WEIGHTS.get(name, 17.0 if leaves else 0.0) if weight is None else weight)) + 1000, bytes_accessed=1000, transcendentals=0),
            name=name,
        )(*scalars, *arrays, *after, *passes, *onto)
        self.last = out[0]
        return out


def window(first, length):
    return max(0, first - LONGEST), min(length, first + BLOCK + LONGEST)


class Weights:
    def __init__(self, wq, wk, wv, bq, bv, wo):
        self.projections, self.biases, self.wo = (wq, wk, wv), (bq, bv), wo

    def cut(self, p, n=1):
        if callable(p):
            return lambda *numbers: pl.ds(pl.multiple_of(p(*numbers) * PAIR, PAIR), n * PAIR)
        return lambda *numbers: slice(p * PAIR, (p + n) * PAIR)

    def triple(self, p):
        d = self.wo.shape[1]
        cut = self.cut(p)
        return Take(
            (d, 3 * PAIR), BF16,
            [
                (a, lambda *n: (slice(None), cut(*n)), (slice(None), slice(i * PAIR, (i + 1) * PAIR)))
                for i, a in enumerate(self.projections)
            ],
        )

    def out(self, p, n=1):
        d = self.wo.shape[1]
        cut = self.cut(p, n)
        return Take((n * PAIR, d), BF16, [(self.wo, lambda *k: (cut(*k), slice(None)), None)])

    def bias(self):
        bq, bv = self.biases
        half = bq.shape[1]
        return Take(
            (1, 2 * half), F32,
            [(bq, None, (slice(None), slice(0, half))), (bv, None, (slice(None), slice(half, 2 * half)))],
        )


class SentWeights:
    def __init__(self, pack):
        self.pack, self.d = pack, pack.shape[1]

    def cut(self, p, base, n=1):
        def index(*numbers):
            if callable(p):
                return pl.ds(pl.multiple_of(base + p(*numbers) * PAIR, PAIR), n * PAIR)
            return slice(base + p * PAIR, base + (p + n) * PAIR)

        return index

    def triple(self, p):
        d, half = self.d, self.d // 2
        copies = []
        for i, (rows, base) in enumerate(((slice(0, d), 0), (slice(0, d), half), (slice(d, 2 * d), 0))):
            cut = self.cut(p, base)
            copies.append(
                (self.pack, lambda *n, rows=rows, cut=cut: (rows, cut(*n)), (slice(None), slice(i * PAIR, (i + 1) * PAIR)))
            )
        return Take((d, 3 * PAIR), F32, copies)

    def out(self, p, n=1):
        d, half = self.d, self.d // 2
        copies = []
        for i in range(2):
            cut = self.cut(p, d + i * half, n)
            copies.append(
                (self.pack, lambda *k, cut=cut: (cut(*k), slice(half, d)), (slice(None), slice(i * half, (i + 1) * half)))
            )
        return Take((n * PAIR, d), F32, copies)

    def bias(self):
        d = self.d
        return fetch(self.pack, (slice(2 * d, 2 * d + TINY), slice(None)), (TINY, d))


def pack_kernel(wq, wk, wv, wo, bq, bv, bi, w_inner, w_outer, out, inner_out, outer_out):
    d, half = wq.buffer.shape
    out[0:d, :half] = wq()[...].astype(F32)
    out[0:d, half:] = wk()[...].astype(F32)
    out.part(slice(0, d))
    out[d : 2 * d, :half] = wv()[...].astype(F32)
    out[d : d + half, half:] = wo()[:, :half].astype(F32)
    out[d + half : 2 * d, half:] = wo()[:, half:].astype(F32)
    out[2 * d : 2 * d + 1, :half] = bq()[...]
    out[2 * d : 2 * d + 1, half:] = bv()[...]
    out[2 * d + 1 : 2 * d + 2, :] = bi()[:, :d]
    out[2 * d + 2 : 2 * d + 3, :] = bi()[:, d:]
    out[2 * d + 3 :, :] = jnp.zeros((TINY - 3, d), F32)
    out.part(slice(d, 2 * d + TINY))
    for ref, result in ((w_inner, inner_out), (w_outer, outer_out)):
        rows = ref.buffer.shape[0] // 2
        for i in range(2):
            cut = slice(i * rows, (i + 1) * rows)
            result[cut, :] = ref()[cut, :].astype(F32)
            result.part(cut)


def row_index(other):
    return lambda core, *_: 1 - core[0] if other else core[0]


def row_of(array, other):
    return Take(array.shape[1:], array.dtype, [(array, row_index(other), None)])


def segments_of(place, fill_ref, seg, cols_ref):
    length = cols_ref.shape[0]
    fill = fill_ref[place]
    row = seg()[pl.ds(place, 1), :].astype(F32)
    places = lax.broadcasted_iota(jnp.int32, (1, length), 1)
    valid = places < fill
    keyed = jnp.where(valid, row, -1.0)
    cols_ref[...] = jnp.broadcast_to(keyed, (PAIR, length)).T
    return row, jnp.where(valid, 1.0, 0.0)


def mask_for(cols_ref, row, low, high, first):
    once = cols_ref[low:high, :] == row[:, first : first + BLOCK]
    return jnp.concatenate([once, once], axis=1)


def two_heads(array):
    lanes = lax.broadcasted_iota(jnp.int32, array.shape, 1)
    return jnp.where(lanes < HEAD_DIM, array, 0), jnp.where(lanes < HEAD_DIM, 0, array)


def stacked(pair, first):
    return jnp.concatenate([half[first : first + BLOCK] for half in pair], axis=0)


def staged(items, one, two, three):
    items = list(items)
    ones, twos = {}, {}
    for i in range(len(items) + 2):
        if i < len(items):
            ones[i] = one(items[i])
        if 0 <= i - 1 < len(items):
            twos[i - 1] = two(items[i - 1], *ones.pop(i - 1))
        if 0 <= i - 2:
            three(items[i - 2], *twos.pop(i - 2))


def forward_pair(p, x, w3, bias, row, valid, cols, qkv, mixed_out, lse):
    length = x.shape[0]
    half = bias.shape[1] // 2
    y = dot_nn(x, w3)
    at = p * PAIR
    q = y[:, :PAIR] + bias[0:1, at : at + PAIR]
    q = (q.astype(BF16) * 0.125).astype(BF16)
    k = y[:, PAIR : 2 * PAIR].astype(BF16)
    v = (y[:, 2 * PAIR :] + bias[0:1, half + at : half + at + PAIR]).astype(BF16)
    vt = v.T
    qkv[0] = q
    qkv[1] = k
    qkv[2] = v
    heads = two_heads(q)

    def scores(first):
        low, high = window(first, length)
        return (dot_nt(k[low:high], stacked(heads, first)),)

    def weigh(first, s):
        low, high = window(first, length)
        s = jnp.where(mask_for(cols, row, low, high, first), s, MASKED)
        peak = jnp.max(s, axis=0, keepdims=True)
        e = jnp.exp(s - peak)
        total = jnp.sum(e, axis=0, keepdims=True)
        lse[0:1, 2 * first : 2 * first + 2 * BLOCK] = peak + jnp.log(total)
        return e.astype(BF16), total

    def mix(first, e, total):
        low, high = window(first, length)
        block = slice(first, first + BLOCK)
        o = dot_nn(vt[:, low:high], e)
        keep = valid[:, block]
        mixed_out[:HEAD_DIM, block] = (o[:HEAD_DIM, :BLOCK] * (keep / total[:, :BLOCK])).astype(BF16)
        mixed_out[HEAD_DIM:, block] = (o[HEAD_DIM:, BLOCK:] * (keep / total[:, BLOCK:])).astype(BF16)

    staged(range(0, length, BLOCK), scores, weigh, mix)


def start_all(*ones):
    for one in ones:
        one.start()


def forward_pairs(x, w3s, bias, row, valid, cols, qkv, mixed, lse):
    for p, w3 in enumerate(w3s):
        forward_pair(
            p, x, w3()[...].astype(BF16), bias(), row, valid, cols, qkv.buffer.at[p], mixed.buffer.at[p], lse.buffer.at[p]
        )
        qkv.part(p)
        mixed.part(p)
        lse.part(p)


def forward_own_kernel(core_ref, fill_ref, seg, x_in, w3_0, bias, w3_1, qkv, mixed, lse, cols):
    row, valid = segments_of(core_ref[0], fill_ref, seg, cols)
    x = x_in()[...]
    w3_0()
    start_all(w3_1)
    forward_pairs(x, (w3_0, w3_1), bias, row, valid, cols, qkv, mixed, lse)


def all_units(low, lowt, d_ffn, wi, bias_of, wo, grads, bias_out, hidden_out, pre_out):
    units = wi().shape[1]
    part, step = units // 2, 256

    def products(at):
        i, inside = divmod(at, part)
        cut, held = slice(at, at + step), slice(inside, inside + step)
        pre = dot_nn(low, wi()[:, cut].astype(BF16)) + bias_of(i, held)
        return pre, dot_nt(d_ffn, wo()[cut, :].astype(BF16))

    def bend(at, pre, d_hidden):
        square = pre * pre
        t = jnp.tanh(pre * (GELU_C + (GELU_C * GELU_A) * square))
        cdf = 0.5 + 0.5 * t
        hidden = (pre * cdf).astype(BF16)
        slope = cdf + (0.5 * pre) * (1.0 - t * t) * (GELU_C + (3.0 * GELU_C * GELU_A) * square)
        d_pre = (d_hidden * slope).astype(BF16)
        i, inside = divmod(at, part)
        bias_out[i : i + 1, inside : inside + step] = jnp.sum(d_pre.astype(F32), axis=0, keepdims=True)
        return hidden, d_pre

    def gather(at, hidden, d_pre):
        i, inside = divmod(at, part)
        cut, held = slice(at, at + step), slice(inside, inside + step)
        hidden_out[:, cut] = hidden
        pre_out[:, cut] = d_pre
        grads[i][held, :] = dot_tn(hidden, d_ffn)
        grads[i][part:, held] = dot_nn(lowt, d_pre)
        if inside + step == part:
            grads[i].send()

    staged(range(0, units, step), products, bend, gather)


def middle_kernel(core_ref, fill_ref, gate, feed_gate, seg, x_in, w3_0, bias, w3_1, wo, mixed_own, wo_own, out_bias,
                  cot, wi, w_outer, qkv, mixed, lse, mid, low_out, grad_0, grad_1, bias_out, hidden_out, pre_out, cols):
    row, valid = segments_of(core_ref[0], fill_ref, seg, cols)
    x = x_in()[...]
    w3_0()
    start_all(w3_1, wo, mixed_own, wo_own, out_bias, cot, wi, w_outer)
    forward_pairs(x, (w3_0, w3_1), bias, row, valid, cols, qkv, mixed, lse)
    for at in range(0, x.shape[0], ROWS):
        rows = slice(at, at + ROWS)
        branch = out_bias()[...]
        for p in range(2):
            cut = slice(p * PAIR, (p + 1) * PAIR)
            branch = branch + dot_tn(mixed_own()[p, :, rows], wo_own()[cut, :])
            branch = branch + dot_tn(mixed[p, :, rows], wo()[cut, :].astype(BF16))
        value = x[rows].astype(F32) + gate[0] * branch
        mid[rows, :] = value
        mid.part(rows)
        low_out[rows, :] = value.astype(BF16)
        low_out.part(rows)
    low = low_out[...]
    d_ffn = (feed_gate[0] * cot()[...].astype(F32)).astype(BF16)
    bias_out[...] = jnp.zeros(bias_out.buffer.shape, F32)
    all_units(
        low, low.T, d_ffn, wi, lambda i, cut: bias()[1 + i : 2 + i, cut], w_outer, (grad_0, grad_1), bias_out,
        hidden_out, pre_out,
    )


def feed_kernel(core_ref, gate, feed_gate, low_in, wi, bi, cot_in, w_outer, hidden_sent, pre_sent, wi_sent, wo_sent,
                out_bias, mid, x, grad_0, grad_1, out, dmid_out, dbranch_out, small, bias_out, hidden_out, pre_out):
    low = low_in()[...]
    length, d = low.shape
    wi()
    start_all(cot_in, w_outer)
    lowt = low.T
    cot = cot_in()[...].astype(F32)
    d_ffn = (feed_gate[0] * cot).astype(BF16)
    w_outer()
    start_all(hidden_sent, pre_sent, wi_sent, wo_sent, out_bias, mid, x)
    bias_out[...] = jnp.zeros_like(bias_out)
    part = d
    all_units(
        low, lowt, d_ffn, wi, lambda i, cut: bi()[:, i * part : (i + 1) * part][:, cut], w_outer, (grad_0, grad_1),
        bias_out, hidden_out, pre_out,
    )
    wi_other = wi_sent()[...].astype(BF16)
    wo_other = wo_sent()[...].astype(BF16)
    sums = [jnp.zeros((1, d), F32)] * 3
    for at in range(0, length, ROWS):
        rows = slice(at, at + ROWS)
        seen = cot_in()[rows, :].astype(F32)
        dmid = dot_nt(pre_sent()[rows, :], wi_other) + dot_nt(pre_out[rows, :], wi()[...]) + seen
        ffn = dot_nn(hidden_sent()[rows, :], wo_other) + dot_nn(hidden_out[rows, :], w_outer()[...]) + out_bias()[...]
        dmid_out[rows, :] = dmid
        dmid_out.part(rows)
        dbranch = (gate[0] * dmid).astype(BF16)
        dbranch_out[rows, :] = dbranch
        dbranch_out.part(rows)
        middle = mid()[rows, :]
        out[rows, :] = middle + feed_gate[0] * ffn
        out.part(rows)
        branch = middle - x()[rows, :].astype(F32)
        for i, value in enumerate((dbranch.astype(F32), dmid * branch, seen * ffn)):
            sums[i] = sums[i] + jnp.sum(value, axis=0, keepdims=True)
    small[...] = jnp.zeros(small.buffer.shape, F32)
    small[1:3, :] = bias_out[0:2, :]
    small[3:4, :] = sums[0]
    small[4:5, :] = jnp.sum(d_ffn.astype(F32), axis=0, keepdims=True)
    small[5:6, :] = sums[1] / gate[0]
    small[6:7, :] = sums[2]


def join_kernel(bit, a, a_came, b, b_came, keep, send):
    rows = keep.buffer.shape[0] // 2
    start_all(a, a_came, b, b_came)
    for i in range(2):
        cut = slice(i * rows, (i + 1) * rows)
        keep[cut, :] = a()[cut, :] + a_came()[cut, :]
        send[cut, :] = b()[cut, :] + b_came()[cut, :]
        part_swapped(bit[0] != 0, keep, send, (cut,), (cut,))


def backward_pair(dbranch, do, qkv, lse, mixed, x, row, cols, dk_acc, dv_acc, dqt, grad_out):
    length, d = dbranch.shape
    q, k, v = qkv[0], qkv[1], qkv[2]
    kt = k.T
    qs = two_heads(q)
    dos = two_heads(do)
    dk_acc[...] = jnp.zeros_like(dk_acc)
    dv_acc[...] = jnp.zeros_like(dv_acc)

    def products(first):
        low, high = window(first, length)
        qq, dd = stacked(qs, first), stacked(dos, first)
        return qq, dd, dot_nt(k[low:high], qq), dot_nt(v[low:high], dd)

    def weigh(first, qq, dd, s, dw):
        low, high = window(first, length)
        s = jnp.where(mask_for(cols, row, low, high, first), s, MASKED)
        w = jnp.exp(s - lse[0:1, 2 * first : 2 * first + 2 * BLOCK])
        both = w * dw
        mean = jnp.sum(both, axis=0, keepdims=True)
        return qq, dd, w.astype(BF16), (both - w * mean).astype(BF16)

    def gather(first, qq, dd, w, ds):
        low, high = window(first, length)
        block = slice(first, first + BLOCK)
        dv_acc[low:high, :] += dot_nn(w, dd)
        dk_acc[low:high, :] += dot_nn(ds, qq)
        dq = dot_nn(kt[:, low:high], ds)
        dqt[:HEAD_DIM, block] = dq[:HEAD_DIM, :BLOCK]
        dqt[HEAD_DIM:, block] = dq[HEAD_DIM:, BLOCK:]

    staged(range(0, length, BLOCK), products, weigh, gather)
    dq = (0.125 * dqt[...]).T.astype(BF16)
    all3 = jnp.concatenate([dq, dk_acc[...].astype(BF16), dv_acc[...].astype(BF16)], axis=1)
    grad_out[:, : 3 * PAIR] = dot_tn(x, all3)
    out_grad = dot_nn(mixed, dbranch)
    for c in range(d // PAIR):
        cut = slice(c * PAIR, (c + 1) * PAIR)
        grad_out[cut, 3 * PAIR :] = out_grad[:, cut]
    return all3


def bias_sums(all3):
    sums = jnp.sum(all3.astype(F32), axis=0, keepdims=True)
    return jnp.concatenate([sums[:, :PAIR], sums[:, 2 * PAIR :]], axis=1)


def masked_heads(dbranch, wo, fill):
    places = lax.broadcasted_iota(jnp.int32, (dbranch.shape[0], 1), 0)
    return jnp.where(places < fill, dot_nt(dbranch, wo), 0.0).astype(BF16)


def backward_kernel(sent, last, core_ref, fill_ref, pair, *refs):
    if sent and not last:
        bit, *refs = refs
    seg, dbranch_in, wo, x_in, qkv, lse, mixed, *refs = refs
    late = []
    if last:
        w3, all3_in, w3_before, total_in, *refs = refs
        late += [w3, all3_in, w3_before, total_in]
    if sent:
        if last:
            bias_in, *refs = refs
            late.append(bias_in)
        else:
            parts, refs = refs[:4], refs[4:]
            late += parts
    else:
        came, *refs = refs
        late.append(came)
    small_in, *refs = refs
    late.append(small_in)
    if last:
        grad_out, small_out, total_out, *rest = refs
    else:
        grad_out, small_out, all3_out, *rest = refs
        if sent:
            keep, send, *rest = rest
    cols, dk_acc, dv_acc, dqt = rest
    row, _ = segments_of(core_ref[0], fill_ref, seg, cols)
    dbranch = dbranch_in()[...]
    length, d = dbranch.shape
    do = masked_heads(dbranch, wo()[...].astype(BF16), fill_ref[core_ref[0]])
    x = x_in()[...]
    qkv()
    start_all(*late)
    grads = grad_out.buffer.at[0:d]
    all3 = backward_pair(dbranch, do, qkv(), lse(), mixed()[...], x, row, cols, dk_acc, dv_acc, dqt, grads)
    small_out[...] = small_in()[...]
    if sent and last:
        small_out[1:3, :] = bias_in()[0:2, :]
    if not sent:
        grads[...] += came()[0:d, :]
    spot = pl.ds(pl.multiple_of(pair[0] * 2 * PAIR, PAIR), 2 * PAIR)
    if sent and not last:
        small_out[0:1, spot] = bias_sums(all3)
    else:
        small_out[0:1, spot] += bias_sums(all3)
    if last and not sent:
        small_out[...] += came()[d:, :]
    if last and sent:
        grad_out[d:, :] = small_out[...]
    grad_out.send()
    if last:
        for at in range(0, length, ROWS):
            rows = slice(at, at + ROWS)
            total = dot_nt(all3_in()[rows, :], w3_before()[...].astype(BF16)) + dot_nt(all3[rows], w3()[...].astype(BF16))
            total_out[rows, :] = total_in()[rows, :] + total
            total_out.part(rows)
    else:
        all3_out[...] = all3
        if sent:
            join_kernel(bit, *parts, keep, send)


def attention_scratch(length):
    return [pltpu.VMEM((length, PAIR), F32)] * 3 + [pltpu.VMEM((PAIR, length), F32)]


def place_in(refs, mask):
    at = 0
    for ref in refs:
        at = 2 * at + ref[0]
    return jnp.bitwise_xor(at, mask)


def sum_of(terms, cut):
    total = terms[0]()[cut, :]
    for one in terms[1:]:
        total = total + one()[cut, :]
    return total


class Stream:
    def __init__(self, chain, members, bits, send, out, back):
        self.chain, self.members, self.bits = chain, members, bits
        self.out, self.back = list(out), list(back)
        self.group = [0]
        self.came = [self.travel(send, 1)]
        self.tail, self.small, self.turned, self.lanes = 0, None, False, 1

    def keep(self, mine, small=None):
        self.mine, self.small = mine, small
        self.rows, self.width = mine.shape
        self.joined = []

    def join(self, other):
        self.joined = [other]

    def travel(self, array, mask):
        pairs = []
        for place in range(self.members):
            for core in range(2):
                partner = place
                for i, step in enumerate(reversed(self.group)):
                    if mask >> i & 1:
                        partner ^= 1 << (step ^ core if step < 2 else step)
                pairs.append((place * 2 + core, partner * 2 + core))
        return lax.ppermute(array, ("dp", "mp"), pairs)

    def call(self, kernel, name, group, outs, small=False):
        takes = [take(one) for stream in (self, *self.joined) for one in (stream.mine, *stream.came)]
        takes += [take(self.small)] if small else []
        results = self.chain.call(
            kernel, name, [self.bits[step] for step in group], takes, [shape(dims) for dims in outs],
            weight=self.weight, passes=self.passes,
        )
        self.passes = results[len(outs) :]
        return results[: len(outs)]

    def halve(self):
        group = self.out.pop(0)
        parts, n_terms = 1 << len(group), 1 + len(self.came)
        whole, tail = self.rows, self.tail
        rows = whole // parts
        begins = self.small is not None and not tail
        sources = 1 + len(self.joined)
        lanes = self.lanes = max(self.lanes, sources)

        def kernel(*refs):
            bits, refs = refs[: len(group)], refs[len(group) :]
            terms = [refs[i * n_terms : (i + 1) * n_terms] for i in range(sources)]
            refs = refs[sources * n_terms :]
            if begins:
                both = refs[0]()[...]
                refs = refs[1:]
            elif tail:
                both = sum_of(terms[0], slice(lanes * whole, lanes * whole + tail))
            for mask, out in enumerate(refs):
                at = place_in(bits, mask) * rows
                for lane in range(lanes):
                    source, base = (lane, 0) if sources > 1 else (0, lane * whole)
                    cut = pl.ds(pl.multiple_of(base + at, 8), rows)
                    out[lane * rows : (lane + 1) * rows, :] = sum_of(terms[source], cut)
                if begins or tail:
                    out[lanes * rows :, :] = both

        if begins:
            self.tail = TINY
        self.mine, *sends = self.call(
            kernel, "halve", group, [(lanes * rows + self.tail, self.width)] * parts, begins
        )
        self.joined = []
        self.group = group
        self.came = [self.travel(send, mask + 1) for mask, send in enumerate(sends)]
        self.rows = rows

    def turn(self):
        rows, tail = self.lanes * self.rows, self.tail
        n_came = len(self.came)

        def kernel(mine, *refs):
            came, refs = refs[:n_came], refs[n_came:]
            total = mine()[...]
            for one in came:
                total = total + one()[...]
            refs[0][...] = total[:rows]
            if tail:
                refs[1][...] = total[rows:]

        outs = [(rows, self.width)] + ([(TINY, self.width)] if tail else [])
        self.mine, *tiny = self.call(kernel, "turn", [], outs)
        self.small = tiny[0] if tiny else None
        self.turned = True
        self.spread()

    def double(self):
        rows, lanes = self.rows, self.lanes
        parts = len(self.came) + 1
        ends = len(self.back) == 1 and self.small is not None
        group = self.group

        def kernel(*refs):
            bits, refs = refs[: len(group)], refs[len(group) :]
            have, refs = refs[:parts], refs[parts:]
            out = refs[-1]
            if ends:
                out[lanes * parts * rows :, :] = refs[0]()[...]
            for mask, one in enumerate(have):
                at = place_in(bits, mask) * rows
                for lane in range(lanes):
                    cut = pl.ds(pl.multiple_of(lane * parts * rows + at, 8), rows)
                    out[cut, :] = one()[lane * rows : (lane + 1) * rows, :]

        self.rows = parts * rows
        (self.mine,) = self.call(
            kernel, "double", group, [(lanes * self.rows + (TINY if ends else 0), self.width)], ends
        )
        self.spread()

    def spread(self):
        self.group = self.back.pop(0)
        self.came = [self.travel(self.mine, mask) for mask in range(1, 1 << len(self.group))]

    def advance(self, weight=0.0, passes=()):
        self.weight, self.passes = weight, passes
        if self.out:
            self.halve()
        elif not self.turned:
            self.turn()
        elif self.back:
            self.double()
        return self.passes

    def done(self):
        return self.turned and not self.back


def in_order(bit, mine, came, low, high):
    @pl.when(bit[0] == 0)
    def _():
        low(mine())
        high(came())

    @pl.when(bit[0] != 0)
    def _():
        low(came())
        high(mine())


def final_feed(chain, stream, index, d, onto=()):
    units = stream.rows
    cut = slice(index * units, (index + 1) * units)

    def kernel(bit, mine, came, inner, outer):
        mine()
        came()

        def low(ref):
            outer[cut, :] = ref[...]

        def high(ref):
            inner[:, cut] = ref[...]

        in_order(bit, mine, came, low, high)
        outer.part(cut)
        inner.part(slice(None), cut)

    return chain.call(
        kernel, "final_feed_%d" % index, [stream.bits[0]], [fetch(stream.mine), fetch(stream.came[0])],
        [shape((d, 2 * units)), shape((2 * units, d))], leaves=True, onto=onto,
    )


def final_attention(chain, third, d):
    half = d // 2

    def kernel(bit, mine, came, gq, gk, gv, go, gqb, gvb, gob, gib, goutb, gates):
        small = mine()[d:, :] + came()[d:, :]
        for p in range(2):
            cut = slice(p * PAIR, (p + 1) * PAIR)
            gqb[:, cut] = small[0:1, 2 * p * PAIR : (2 * p + 1) * PAIR]
            gvb[:, cut] = small[0:1, (2 * p + 1) * PAIR : (2 * p + 2) * PAIR]
        gib[:, :d] = small[1:2, :]
        gib[:, d:] = small[2:3, :]
        gob[...] = small[3:4, :]
        goutb[...] = small[4:5, :]
        gates[...] = jnp.broadcast_to(jnp.sum(small, axis=1, keepdims=True), gates.buffer.shape)

        def place(p, ref):
            cut = slice(p * PAIR, (p + 1) * PAIR)
            gq[:, cut] = ref[:d, :PAIR]
            gk[:, cut] = ref[:d, PAIR : 2 * PAIR]
            gv[:, cut] = ref[:d, 2 * PAIR : 3 * PAIR]
            for c in range(d // PAIR):
                across = slice(c * PAIR, (c + 1) * PAIR)
                go[cut, across] = ref[across, 3 * PAIR :]

        in_order(bit, mine, came, partial(place, 0), partial(place, 1))

    return chain.call(
        kernel, "final_attention", [third.bits[0]], [take(third.mine), take(third.came[0])],
        [shape((d, half))] * 3
        + [shape((half, d)), shape((1, half)), shape((1, half)), shape((1, d)), shape((1, 2 * d)), shape((1, d)), shape((TINY, PAIR))],
        leaves=True,
    )


def rows_kernel(core_ref, own, came, out):
    out[core_ref[0]] = own()[...].astype(out.buffer.dtype)
    out.part(core_ref[0])
    out[1 - core_ref[0]] = came()[...].astype(out.buffer.dtype)
    out.part(1 - core_ref[0])


def shards(members, tokens, segment_ids, row_fill, query_weight, query_bias, key_weight,
           value_weight, value_bias, out_weight, out_bias, attention_gate, inner_weight,
           inner_bias, outer_weight, outer_bias, feed_gate, cotangent):
    _, length, d = tokens.shape
    half = d // 2
    place = lax.axis_index("dp")
    core_id = lax.axis_index("mp")
    core = core_id.astype(jnp.int32).reshape(1)
    bits = []
    for step in range(members.bit_length() - 1):
        bit = (place >> (step ^ core_id if step < 2 else step)) & 1
        bits.append(bit.astype(jnp.int32).reshape(1))
    not_mine = 1 - bits[0]
    chain = Chain()

    def across(array):
        return lax.ppermute(array, "mp", [(0, 1), (1, 0)])

    def as_row(array):
        return array.reshape(1, -1)

    def own_row(array):
        return row_of(array, False)

    a_gate = attention_gate.reshape(1)
    f_gate = feed_gate.reshape(1)
    qb, vb, ib, ob, fb = (as_row(a) for a in (query_bias, value_bias, inner_bias, out_bias, outer_bias))
    own = Weights(query_weight, key_weight, value_weight, qb, vb, out_weight)
    seg = fetch(segment_ids)
    cols = [pltpu.VMEM((length, PAIR), F32)]
    units = inner_weight.shape[1]

    pack, wi, wo = chain.call(
        pack_kernel, "pack", [],
        [fetch(a) for a in (query_weight, key_weight, value_weight, out_weight, qb, vb, ib, inner_weight, outer_weight)],
        [shape((2 * d + TINY, d)), shape((d, units)), shape((units, d))], leaves=True,
    )
    pack_came, wi_came, wo_came = across(pack), across(wi), across(wo)
    sent = SentWeights(pack_came)

    pair_outs = [shape((2, 3, length, PAIR), BF16), shape((2, PAIR, length), BF16), shape((2, TINY, 2 * length))]
    qkv_a, mixed_a, lse_a = chain.call(
        forward_own_kernel, "forward_own", [core, row_fill],
        [seg, own_row(tokens), own.triple(0), own.bias(), later(own.triple(1))], pair_outs, cols, leaves=True,
    )
    unit_outs = [shape((length, units), BF16)] * 2
    grad_outs = [shape((2 * d, d))] * 2
    qkv_b, mixed_b, lse_b, mid, low, g_sent_0, g_sent_1, bias_b, hidden_b, pre_b = chain.call(
        middle_kernel, "middle", [core, row_fill, a_gate, f_gate],
        [seg, own_row(tokens), sent.triple(0), sent.bias()]
        + [
            later(one)
            for one in (
                sent.triple(1), sent.out(0, 2), fetch(mixed_a), own.out(0, 2), fetch(ob), own_row(cotangent),
                fetch(wi_came), fetch(wo_came),
            )
        ],
        pair_outs + [shape((length, d)), shape((length, d), BF16)] + grad_outs + [shape((TINY, d))] + unit_outs,
        cols, leaves=True,
    )
    g_came_0, g_came_1 = across(g_sent_0), across(g_sent_1)
    g_own_0, g_own_1, out_own, dmid, dbranch, small = chain.call(
        feed_kernel, "feed", [core, a_gate, f_gate],
        [fetch(low), fetch(inner_weight), fetch(ib)]
        + [
            later(one)
            for one in (
                own_row(cotangent), fetch(outer_weight), fetch(hidden_b), fetch(pre_b), fetch(wi_came), fetch(wo_came),
                fetch(fb), fetch(mid), own_row(tokens),
            )
        ],
        grad_outs + [shape((length, d))] * 2 + [shape((length, d), BF16), shape((TINY, d))],
        [pltpu.VMEM((TINY, d), F32)] + [pltpu.VMEM((length, units), BF16)] * 2, leaves=True,
    )

    wide = [[step for step in pair if step < len(bits)] for pair in ((i, i + 1) for i in range(2, len(bits), 2))]
    one_by_one = [[step] for step in range(len(bits))]
    direct = ([[1], *wide], [*wide[::-1], [1], [0]])
    plain = (one_by_one[1:], one_by_one[::-1])

    def halves(mine, came):
        return [fetch(one, (slice(i * d, (i + 1) * d), slice(None)), (d, d)) for i in range(2) for one in (mine, came)]

    def stream(send, ways):
        return Stream(chain, members, bits, send, *ways)

    other_bit = ((place >> (1 - core_id)) & 1).astype(jnp.int32).reshape(1)
    pair_of = lambda core, fill, pair, *_: pair[0]
    pair_before = lambda core, fill, pair, *_: 1 - pair[0]

    def backward(sent, last, pair, weights, kept, extra, small, outs, bit=None):
        qkv, mixed, lse = kept
        takes = [
            seg, fetch(dbranch), weights.out(pair_of), own_row(tokens), fetch(qkv, pair_of, (3, length, PAIR)),
            fetch(lse, pair_of, (TINY, 2 * length)), fetch(mixed, pair_of, (PAIR, length)),
        ]
        more = list(extra)
        if last:
            all3, total, *rest = more
            more = [weights.triple(pair_of), fetch(all3), weights.triple(pair_before), fetch(total), *rest]
        takes += [later(one) for one in [*more, fetch(small)]]
        return chain.call(
            partial(backward_kernel, sent, last), "backward_%s_%d" % ("sent" if sent else "own", last),
            [core, row_fill, pair] + ([bit] if bit is not None else []), takes, outs, attention_scratch(length),
            leaves=True,
        )

    keep, send = chain.call(
        join_kernel, "join", [bits[0]], halves(g_own_0, g_came_0), [shape((d, d))] * 2, leaves=True
    )
    first = stream(send, direct)
    first.keep(keep)
    square, row8, rows3 = shape((d, d)), shape((TINY, d)), shape((length, 3 * PAIR), BF16)
    kept_a, kept_b = (qkv_a, mixed_a, lse_a), (qkv_b, mixed_b, lse_b)
    g_0, small_b, all3, keep, send = backward(
        True, False, 1 - other_bit, sent, kept_b, halves(g_own_1, g_came_1), small, [square, row8, rows3, square, square],
        bit=bits[0],
    )
    second = stream(send, plain)
    second.keep(keep)
    g_came_first = across(g_0)
    first.advance(0.0)
    g_1, _, total = backward(
        True, True, other_bit, sent, kept_b, (all3, dmid, fetch(bias_b)), small_b,
        [shape((d + TINY, d)), row8, shape((length, d))],
    )
    g_came_last = across(g_1)
    first.advance(0.0)
    second.advance(0.0)
    send, small, all3 = backward(
        False, False, not_mine, own, kept_a, (fetch(g_came_first),), small, [square, row8, rows3]
    )
    third = stream(send, direct)
    first.advance(0.0)
    second.advance(0.0)
    keep, small, total = backward(
        False, True, bits[0], own, kept_a, (all3, total, fetch(g_came_last)), small,
        [square, row8, shape((length, d))],
    )
    third.keep(keep, small)
    third.advance()
    first.advance()
    second.advance(20.0)
    while third.out:
        third.advance()
    while not first.done():
        first.advance(20.0)
    third.advance(20.0)
    second.advance()
    grads = final_feed(chain, first, 0, d)
    (out_own,) = third.advance(passes=(out_own,))
    out_came = across(out_own)
    second.advance(20.0)
    while not third.done():
        (total,) = third.advance(passes=(total,))
        second.advance()
    total_came = across(total)
    (output,) = chain.call(
        rows_kernel, "output", [core], [fetch(out_own), fetch(out_came)], [shape((2, length, d), BF16)], leaves=True
    )
    while not second.done():
        second.advance()
    (grad_tokens,) = chain.call(
        rows_kernel, "tokens", [core], [fetch(total), fetch(total_came)], [shape((2, length, d))], leaves=True
    )
    gq, gk, gv, go, gqb, gvb, gob, gib, goutb, gates = final_attention(chain, third, d)
    inner_grad, outer_grad = final_feed(chain, second, 1, d, grads)
    return (
        output, grad_tokens, gq, gqb.reshape(-1), gk, gv, gvb.reshape(-1), go, gob.reshape(-1), gates[5, 0],
        inner_grad, gib.reshape(-1), outer_grad, goutb.reshape(-1), gates[6, 0],
    )


def solution(mesh):
    rows = P("dp", None, None)
    col = P(None, "mp")
    cut = P("mp")
    in_specs = (
        rows, P("dp", None), P("dp"), col, cut, col, col, cut, P("mp", None), P(), P(),
        col, cut, P("mp", None), P(), P(), rows,
    )
    out_specs = (
        rows, rows, col, cut, col, col, cut, P("mp", None), P(), P(), col, cut,
        P("mp", None), P(), P(),
    )
    return jax.shard_map(
        partial(shards, mesh.shape["dp"]), mesh=mesh, in_specs=in_specs, out_specs=out_specs,
        check_vma=False,
    )
```
